32 devices in a mesh: cls: 16 (over z, y, x), dp: 2 (over core).
Axes of the slice: x: 2, y: 2, z: 4, core: 2. Of those that a mesh axis runs over, the one named last changes fastest.
Arguments:
- features: bfloat16 [4096, 512], P(('cls', 'dp')), may hold values from -6 to 6
- labels: int32 [4096], P(('cls', 'dp')), may hold values from 0 to 4095, as said below
- weights: float32 [16384, 512], P('cls'), may hold values from -0.25 to 0.25
- sampled: int32 [4096], P('cls'), may hold values from 0 to 1023, as said below
Outputs:
- sample_loss: float32 [4096], P(('cls', 'dp'))
- weight_grad: float32 [4096, 512], P(('cls', 'dp'))
The draws below stay inside these ranges and needn't reach their ends.
Inputs may be any that keep to these rules, and one draw needn't show every extreme that they name: The owner of a label is label // 256. In the rows of one device (aligned blocks of 128 rows) exactly one owner receives 10 of the labels and every other owner fewer. `sampled`: each aligned block of 256 entries holds distinct rows of the owner's bank.
All inputs are finite; a program needn't handle non-finite values.
Results may differ from the reference program's by a relative error of at most 0.0038.
Values may be sent and summed in bfloat16 or wider, within the bound.
No kernel may reach another device: no remote copies, remote signals or barrier semaphores. Data moves between devices by JAX's collectives and lax.ppermute only.
A program may use at most 64 MiB of HBM per device.

```python
import math
import jax
import jax.numpy as jnp
from jax import lax

D = 512
B_DEV = 128
BANK = 1024
SAMP = 256
CAP = 10
BATCH = 4096
BANK_ALL = 16384
SAMPLED_ALL = 4096
N_CLS = 16
N_DP = 2


def draw_sampled(key, part):
    keys = jax.random.split(key, N_CLS)

    def one_shard(shard_key):
        return jax.random.permutation(shard_key, BANK)[:SAMP]
    picked = jax.vmap(one_shard)(keys)
    return picked.reshape(-1).astype(jnp.int32)


def draw_labels(key, part):
    count_blocks = BATCH // B_DEV
    keys = jax.random.split(key, count_blocks)

    def one_block(block_key):
        key_hot, key_rest, key_order, key_slot = jax.random.split(block_key, 4)
        hot_owner = jax.random.randint(key_hot, (), 0, N_CLS).astype(jnp.int32)
        candidates = jnp.repeat(jnp.arange(N_CLS - 1, dtype=jnp.int32), CAP - 1)
        others = jax.random.permutation(key_rest, candidates)[:B_DEV - CAP]
        others = others + (others >= hot_owner).astype(jnp.int32)
        owner_ids = jnp.concatenate([jnp.full((CAP,), hot_owner, jnp.int32), others])
        owner_ids = jax.random.permutation(key_order, owner_ids)
        slot_ids = jax.random.randint(key_slot, (B_DEV,), 0, SAMP).astype(jnp.int32)
        return owner_ids * SAMP + slot_ids
    return jax.vmap(one_block)(keys).reshape(-1).astype(jnp.int32)


def block_scale(key, shape, cuts, least, high):
    loudness, own = 1.0, jax.random.fold_in(key, 6)
    for position, parts in cuts:
        steps = jnp.exp(jax.random.uniform(jax.random.fold_in(own, position), (parts,), jnp.float32, least / len(cuts), high / len(cuts)))
        loudness = loudness * jnp.repeat(steps, shape[position] // parts).reshape([-1 if axis == position else 1 for axis in range(len(shape))])
    return loudness


def gaussian(rng, dims, deviation, bound, cuts=(), kind=jnp.bfloat16):
    result = jax.random.normal(rng, dims, jnp.float32) * deviation
    if len(cuts) > 0:
        result = block_scale(rng, dims, cuts, -0.22, 0.18) * result
    return jnp.clip(result, min=-bound, max=bound).astype(kind)


def setup_inputs(seed: int = 0) -> dict:
    key_of = jax.random.split(jax.random.key(seed), 5)
    features = gaussian(key_of[0], (BATCH, D), 1.0, 6.0, ((0, 32),))
    labels = draw_labels(jax.random.fold_in(key_of[4], 71), 0)
    weights = gaussian(key_of[2], (BANK_ALL, D), D ** -0.5, 0.25, ((0, 16),), jnp.float32)
    sampled = draw_sampled(jax.random.fold_in(key_of[4], 71), 0)
    return dict(features=features, labels=labels, weights=weights, sampled=sampled)


logit_scale = 64.0
margin = 0.35
epsilon = 1e-06

def normalize_rows(matrix):
    squares = lax.optimization_barrier(jnp.sum(matrix * matrix, axis=1, keepdims=True))
    return lax.rsqrt(squares + epsilon)

def reference(features, labels, weights, sampled):
    feat_wide = features.astype(jnp.float32)
    unit_feats = (feat_wide * normalize_rows(feat_wide)).astype(jnp.bfloat16)
    bank_rows = sampled + jnp.arange(SAMPLED_ALL, dtype=jnp.int32) // SAMP * BANK
    chosen = weights[bank_rows]
    inverse_norm = normalize_rows(chosen)
    unit_f32 = chosen * inverse_norm
    unit_rows = unit_f32.astype(jnp.bfloat16)
    class_ids = jnp.arange(SAMPLED_ALL, dtype=jnp.int32)
    block_rows = math.gcd(BATCH, 512)
    feat_blocks = unit_feats.reshape(BATCH // block_rows, block_rows, D)
    label_blocks = labels.reshape(BATCH // block_rows, block_rows)

    def logits_of(feat_block, label_block):
        cosine = jnp.dot(feat_block, unit_rows.T, preferred_element_type=jnp.float32)
        target_hit = label_block[:, None] == class_ids[None, :]
        logits = logit_scale * (cosine - margin * target_hit.astype(jnp.float32))
        return (logits, target_hit)

    def first_pass(operands):
        logits, target_hit = logits_of(operands[0], operands[1])
        totals = lax.optimization_barrier(jnp.sum(jnp.exp(logits - logit_scale), axis=1))
        targets = lax.optimization_barrier(jnp.sum(jnp.where(target_hit, logits, 0.0), axis=1))
        return (totals, targets)
    totals, targets = lax.map(first_pass, (feat_blocks, label_blocks))
    sample_loss = logit_scale + jnp.log(totals) - targets

    def second_pass(running, triple):
        logits, target_hit = logits_of(triple[0], triple[1])
        softmax = jnp.exp(logits - logit_scale) / triple[2][:, None]
        grads_low = (logit_scale * (softmax - target_hit.astype(jnp.float32)) / N_DP).astype(jnp.bfloat16)
        return (running + jnp.dot(grads_low.T, triple[0], preferred_element_type=jnp.float32), None)
    start_grad = jnp.zeros((SAMPLED_ALL, D), jnp.float32)
    unit_grad, _ = lax.scan(second_pass, start_grad, (feat_blocks, label_blocks, totals))
    radial = lax.optimization_barrier(jnp.sum(unit_f32 * unit_grad, axis=1, keepdims=True))
    weight_grad = inverse_norm * (unit_grad - unit_f32 * radial)
    return (sample_loss.reshape(BATCH), weight_grad)
```

```python
import functools

import jax
import jax.numpy as jnp
from jax import lax
from jax.experimental import pallas as pl
from jax.experimental.pallas import tpu as pltpu
from jax.sharding import PartitionSpec as P

logit_scale = 64.0
margin = 0.35
epsilon = 1e-06

vmem_spec = pl.BlockSpec(memory_space=pltpu.VMEM)
smem_spec = pl.BlockSpec(memory_space=pltpu.SMEM)
params = pltpu.CompilerParams(vmem_limit_bytes=48 * 1024 * 1024)


def normalize_kernel(feat_ref, out_ref):
    wide = feat_ref[...].astype(jnp.float32)
    squares = jnp.sum(wide * wide, axis=1, keepdims=True)
    out_ref[...] = (wide * lax.rsqrt(squares + epsilon)).astype(jnp.bfloat16)


def choose_kernel(sampled_ref, weight_ref, low_ref, unit_ref, norm_ref, chosen):
    classes = low_ref.shape[0]

    def copy_rows(step, carry):
        for lane in range(8):
            row = step * 8 + lane
            chosen[pl.ds(row, 1), :] = weight_ref[pl.ds(sampled_ref[row], 1), :]
        return carry

    lax.fori_loop(0, classes // 8, copy_rows, 0)
    rows = chosen[...]
    inverse = lax.rsqrt(jnp.sum(rows * rows, axis=1, keepdims=True) + epsilon)
    unit = rows * inverse
    low_ref[...] = unit.astype(jnp.bfloat16)
    unit_ref[...] = unit
    norm_ref[...] = inverse


def class_ids(place_ref, classes, lanes):
    line = lax.broadcasted_iota(jnp.int32, (2 * classes, lanes), 0)
    return line + jnp.where(line < classes, place_ref[0], place_ref[1] - classes)


def logits_kernel(count, place_ref, label_ref, own_ref, near_ref, *refs):
    feats, exp_ref, stat_ref, rows = refs[:count], refs[count], refs[count + 1], refs[count + 2]
    classes = own_ref.shape[0]
    lanes = feats[0].shape[0]
    rows[:classes, :] = own_ref[...]
    rows[classes:, :] = near_ref[...]
    ids = class_ids(place_ref, classes, lanes)
    for pair in range(0, count, 2):
        both = jnp.concatenate([feats[pair][...], feats[pair + 1][...]], axis=0)
        cosine = lax.dot_general(
            rows[...], both, (((1,), (1,)), ((), ())), preferred_element_type=jnp.float32
        )
        for block in (pair, pair + 1):
            start = (block - pair) * lanes
            hit = label_ref[block : block + 1, :] == ids
            logits = logit_scale * (
                cosine[:, start : start + lanes] - margin * hit.astype(jnp.float32)
            )
            exps = jnp.exp(logits - logit_scale)
            exp_ref[:, block * lanes : (block + 1) * lanes] = exps
            stat_ref[block : block + 1, :] = jnp.sum(exps, axis=0, keepdims=True)
            stat_ref[count + block : count + block + 1, :] = jnp.sum(
                jnp.where(hit, logits, 0.0), axis=0, keepdims=True
            )


def grads_kernel(count, replicas, place_ref, label_ref, exp_ref, *refs):
    stats, feats = refs[:count], refs[count : 2 * count]
    outs = refs[2 * count : 2 * count + 2 * replicas]
    loss_ref, grads, every, total = refs[2 * count + 2 * replicas :]
    lanes = feats[0].shape[0]
    classes = exp_ref.shape[0] // 2
    part = classes // replicas
    scale = logit_scale / replicas
    ids = class_ids(place_ref, classes, lanes)
    for block in range(count):
        summed = stats[0][block : block + 1, :]
        for other in range(1, count):
            summed = summed + stats[other][block ^ other : (block ^ other) + 1, :]
        if block == 0:
            target = stats[0][count : count + 1, :]
            for other in range(1, count):
                target = target + stats[other][count + other : count + other + 1, :]
            loss_ref[...] = logit_scale + jnp.log(summed) - target
        columns = slice(block * lanes, (block + 1) * lanes)
        hit = label_ref[block : block + 1, :] == ids
        grads[:, columns] = (
            exp_ref[:, columns] * (1.0 / summed) - jnp.where(hit, 1.0, 0.0)
        ).astype(jnp.bfloat16)
        every[columns, :] = feats[block][...]
    total[...] = jnp.dot(grads[...], every[...], preferred_element_type=jnp.float32)
    for index, out in enumerate(outs):
        side, shift = divmod(index, replicas)
        first = pl.multiple_of(side * classes + (place_ref[2] ^ shift) * part, part)
        out[...] = (total[pl.ds(first, part), :] * scale).astype(out.dtype)


def finish_kernel(count, place_ref, unit_ref, norm_ref, own_ref, *refs):
    others, out_ref = refs[:count], refs[count]
    part = own_ref.shape[0]
    first = pl.multiple_of(place_ref[2] * part, part)
    summed = own_ref[...]
    for other in others:
        summed = summed + other[...].astype(jnp.float32)
    unit = unit_ref[pl.ds(first, part), :]
    inverse = norm_ref[pl.ds(first, part), :]
    radial = jnp.sum(unit * summed, axis=1, keepdims=True)
    out_ref[...] = inverse * (summed - unit * radial)


def per_device(features, labels, weights, sampled):
    groups = lax.axis_size("cls")
    replicas = lax.axis_size("dp")
    local_rows, width = features.shape
    classes = sampled.shape[0]
    part = classes // replicas
    position = lax.axis_index("cls").astype(jnp.int32)
    place = jnp.stack(
        [position * classes, (position ^ 1) * classes, lax.axis_index("dp").astype(jnp.int32)]
    )

    def swap(value, mask):
        return lax.ppermute(value, "cls", [(i, i ^ mask) for i in range(groups)])

    def swap_all(value, mask):
        return lax.ppermute(
            value, ("cls", "dp"), [(i, i ^ mask) for i in range(groups * replicas)]
        )

    unit_feats = pl.pallas_call(
        normalize_kernel,
        out_shape=jax.ShapeDtypeStruct(features.shape, jnp.bfloat16),
        in_specs=[vmem_spec],
        out_specs=vmem_spec,
        name="normalize",
    )(features)
    far = range(4, groups, 4)
    blocks = [unit_feats] + [swap(unit_feats, mask) for mask in far]
    blocks = blocks + [swap(block, 2) for block in blocks]
    marks = labels.reshape(1, local_rows)
    marks = jnp.concatenate([marks] + [swap(marks, mask) for mask in far], axis=0)
    marks = jnp.concatenate([marks, swap(marks, 2)], axis=0)
    count = len(blocks)
    low_rows, unit_rows, norms = pl.pallas_call(
        choose_kernel,
        out_shape=[
            jax.ShapeDtypeStruct((classes, width), jnp.bfloat16),
            jax.ShapeDtypeStruct((classes, width), jnp.float32),
            jax.ShapeDtypeStruct((classes, 1), jnp.float32),
        ],
        in_specs=[smem_spec, vmem_spec],
        out_specs=[vmem_spec] * 3,
        scratch_shapes=[pltpu.VMEM((classes, width), jnp.float32)],
        compiler_params=params,
        name="choose",
    )(sampled, weights)
    near_rows = swap(low_rows, 1)

    exps, stats = pl.pallas_call(
        functools.partial(logits_kernel, count),
        out_shape=[
            jax.ShapeDtypeStruct((2 * classes, count * local_rows), jnp.float32),
            jax.ShapeDtypeStruct((2 * count, local_rows), jnp.float32),
        ],
        in_specs=[smem_spec] + [vmem_spec] * (3 + count),
        out_specs=[vmem_spec] * 2,
        scratch_shapes=[pltpu.VMEM((2 * classes, width), jnp.bfloat16)],
        compiler_params=params,
        name="logits",
    )(place, marks, low_rows, near_rows, *blocks)
    quarter = count // 2
    masks = [4 * (i % quarter) + 2 * (i // quarter) for i in range(count)]
    all_stats = [stats] + [swap(stats, mask) for mask in masks[1:]]
    outs = pl.pallas_call(
        functools.partial(grads_kernel, count, replicas),
        out_shape=[jax.ShapeDtypeStruct((part, width), jnp.float32)]
        + [jax.ShapeDtypeStruct((part, width), jnp.bfloat16)] * (2 * replicas - 1)
        + [jax.ShapeDtypeStruct((1, local_rows), jnp.float32)],
        in_specs=[smem_spec] + [vmem_spec] * (2 + 2 * count),
        out_specs=[vmem_spec] * (2 * replicas + 1),
        scratch_shapes=[
            pltpu.VMEM((2 * classes, count * local_rows), jnp.bfloat16),
            pltpu.VMEM((count * local_rows, width), jnp.bfloat16),
            pltpu.VMEM((2 * classes, width), jnp.float32),
        ],
        compiler_params=params,
        name="grads",
    )(place, marks, exps, *all_stats, *blocks)
    mine, loss = outs[0], outs[-1]
    others = [swap_all(outs[mask], mask) for mask in range(1, 2 * replicas)]
    weight_grad = pl.pallas_call(
        functools.partial(finish_kernel, len(others)),
        out_shape=jax.ShapeDtypeStruct((part, width), jnp.float32),
        in_specs=[smem_spec] + [vmem_spec] * (3 + len(others)),
        out_specs=vmem_spec,
        name="finish",
    )(place, unit_rows, norms, mine, *others)
    return (loss.reshape(local_rows), weight_grad)


def solution(mesh):
    in_specs = (P(("cls", "dp"), None), P(("cls", "dp")), P("cls", None), P("cls"))
    out_specs = (P(("cls", "dp")), P(("cls", "dp"), None))
    return jax.shard_map(
        per_device, mesh=mesh, in_specs=in_specs, out_specs=out_specs, check_vma=False
    )
```

```python
import functools

import jax
import jax.numpy as jnp
from jax import lax
from jax.experimental import pallas as pl
from jax.experimental.pallas import tpu as pltpu
from jax.sharding import PartitionSpec as P

logit_scale = 64.0
margin = 0.35
epsilon = 1e-06
digit = 256
extra = 16

vmem_spec = pl.BlockSpec(memory_space=pltpu.VMEM)
smem_spec = pl.BlockSpec(memory_space=pltpu.SMEM)
params = pltpu.CompilerParams(vmem_limit_bytes=48 * 1024 * 1024)


def normalize_kernel(feat_ref, label_ref, out_ref):
    rows = feat_ref.shape[0]
    wide = feat_ref[...].astype(jnp.float32)
    squares = jnp.sum(wide * wide, axis=1, keepdims=True)
    out_ref[:rows, :] = (wide * lax.rsqrt(squares + epsilon)).astype(jnp.bfloat16)
    labels = label_ref[...]
    digits = jnp.concatenate([labels // digit, labels % digit], axis=1).astype(jnp.float32)
    blank = jnp.zeros((extra, feat_ref.shape[1]), jnp.float32)
    digits = jnp.concatenate([digits, blank[:1, digits.shape[1] :]], axis=1)
    line = lax.broadcasted_iota(jnp.int32, blank.shape, 0)
    out_ref[rows:, :] = jnp.where(line == 0, digits, blank).astype(jnp.bfloat16)


def labels_of(feat_ref):
    rows = feat_ref.shape[0] - extra
    digits = feat_ref[rows:, :].astype(jnp.float32)[:1, :].astype(jnp.int32)
    return digits[:, :rows] * digit + digits[:, rows : 2 * rows]


def choose_kernel(sampled_ref, weight_ref, low_ref, unit_ref, norm_ref, chosen):
    classes = low_ref.shape[0]

    def copy_rows(step, carry):
        for lane in range(8):
            row = step * 8 + lane
            chosen[pl.ds(row, 1), :] = weight_ref[pl.ds(sampled_ref[row], 1), :]
        return carry

    lax.fori_loop(0, classes // 8, copy_rows, 0)
    rows = chosen[...]
    inverse = lax.rsqrt(jnp.sum(rows * rows, axis=1, keepdims=True) + epsilon)
    unit = rows * inverse
    low_ref[...] = unit.astype(jnp.bfloat16)
    unit_ref[...] = unit
    norm_ref[...] = inverse


def class_ids(place_ref, classes, lanes):
    line = lax.broadcasted_iota(jnp.int32, (2 * classes, lanes), 0)
    return line + jnp.where(line < classes, place_ref[0], place_ref[1] - classes)


def logits_kernel(count, place_ref, own_ref, near_ref, *refs):
    feats, exp_ref, stat_ref, rows = refs[:count], refs[count], refs[count + 1], refs[count + 2]
    classes = own_ref.shape[0]
    lanes = feats[0].shape[0] - extra
    rows[:classes, :] = own_ref[...]
    rows[classes:, :] = near_ref[...]
    ids = class_ids(place_ref, classes, lanes)
    for pair in range(0, count, 2):
        both = jnp.concatenate([feats[pair][:lanes, :], feats[pair + 1][:lanes, :]], axis=0)
        cosine = lax.dot_general(
            rows[...], both, (((1,), (1,)), ((), ())), preferred_element_type=jnp.float32
        )
        for block in (pair, pair + 1):
            start = (block - pair) * lanes
            hit = labels_of(feats[block]) == ids
            logits = logit_scale * (
                cosine[:, start : start + lanes] - margin * hit.astype(jnp.float32)
            )
            exps = jnp.exp(logits - logit_scale)
            exp_ref[:, block * lanes : (block + 1) * lanes] = exps
            group = place_ref[3] ^ block
            stat_ref[pl.ds(group, 1), :] = jnp.sum(exps, axis=0, keepdims=True)
            stat_ref[pl.ds(count + group, 1), :] = jnp.sum(
                jnp.where(hit, logits, 0.0), axis=0, keepdims=True
            )


def grads_kernel(count, replicas, side, place_ref, exp_ref, stat_ref, *refs):
    feats, outs = refs[:count], refs[count : count + replicas]
    grads, every, total, sums = refs[-4:]
    lanes = feats[0].shape[0] - extra
    classes = exp_ref.shape[0] // 2
    part = classes // replicas
    scale = logit_scale / replicas
    ids = class_ids(place_ref, classes, lanes)[side * classes : (side + 1) * classes]
    sums[...] = jnp.sum(stat_ref[...], axis=0)
    if side == 0:
        own = place_ref[3]
        refs[count + replicas][...] = (
            logit_scale + jnp.log(sums[pl.ds(own, 1), :]) - sums[pl.ds(count + own, 1), :]
        )
    for block in range(count):
        summed = sums[pl.ds(place_ref[3] ^ block, 1), :]
        columns = slice(block * lanes, (block + 1) * lanes)
        hit = labels_of(feats[block]) == ids
        exps = exp_ref[side * classes : (side + 1) * classes, columns]
        grads[:, columns] = (exps * (1.0 / summed) - jnp.where(hit, 1.0, 0.0)).astype(
            jnp.bfloat16
        )
        every[columns, :] = feats[block][:lanes, :]
    total[...] = jnp.dot(grads[...], every[...], preferred_element_type=jnp.float32)
    for shift in range(replicas):
        first = pl.multiple_of((place_ref[2] ^ shift) * part, part)
        outs[shift][...] = (total[pl.ds(first, part), :] * scale).astype(outs[shift].dtype)


def finish_kernel(count, place_ref, unit_ref, norm_ref, own_ref, *refs):
    others, out_ref = refs[:count], refs[count]
    part = own_ref.shape[0]
    first = pl.multiple_of(place_ref[2] * part, part)
    summed = own_ref[...]
    for other in others:
        summed = summed + other[...].astype(jnp.float32)
    unit = unit_ref[pl.ds(first, part), :]
    inverse = norm_ref[pl.ds(first, part), :]
    radial = jnp.sum(unit * summed, axis=1, keepdims=True)
    out_ref[...] = inverse * (summed - unit * radial)


def per_device(features, labels, weights, sampled):
    groups = lax.axis_size("cls")
    replicas = lax.axis_size("dp")
    local_rows, width = features.shape
    classes = sampled.shape[0]
    part = classes // replicas
    position = lax.axis_index("cls").astype(jnp.int32)
    place = jnp.stack(
        [
            position * classes,
            (position ^ 1) * classes,
            lax.axis_index("dp").astype(jnp.int32),
            position // 2,
        ]
    )

    def swap(value, mask):
        return lax.ppermute(value, "cls", [(i, i ^ mask) for i in range(groups)])

    def swap_all(value, mask):
        return lax.ppermute(
            value, ("cls", "dp"), [(i, i ^ mask) for i in range(groups * replicas)]
        )

    unit_feats = pl.pallas_call(
        normalize_kernel,
        out_shape=jax.ShapeDtypeStruct((local_rows + extra, width), jnp.bfloat16),
        in_specs=[vmem_spec] * 2,
        out_specs=vmem_spec,
        name="normalize",
    )(features, labels.reshape(1, local_rows))
    blocks = [unit_feats] + [swap(unit_feats, mask) for mask in range(4, groups, 4)]
    blocks = [b for block in blocks for b in (block, swap(block, 2))]
    count = len(blocks)
    low_rows, unit_rows, norms = pl.pallas_call(
        choose_kernel,
        out_shape=[
            jax.ShapeDtypeStruct((classes, width), jnp.bfloat16),
            jax.ShapeDtypeStruct((classes, width), jnp.float32),
            jax.ShapeDtypeStruct((classes, 1), jnp.float32),
        ],
        in_specs=[smem_spec, vmem_spec],
        out_specs=[vmem_spec] * 3,
        scratch_shapes=[pltpu.VMEM((classes, width), jnp.float32)],
        compiler_params=params,
        name="choose",
    )(sampled, weights)
    near_rows = swap(low_rows, 1)

    exps, stats = pl.pallas_call(
        functools.partial(logits_kernel, count),
        out_shape=[
            jax.ShapeDtypeStruct((2 * classes, count * local_rows), jnp.float32),
            jax.ShapeDtypeStruct((2 * count, local_rows), jnp.float32),
        ],
        in_specs=[smem_spec] + [vmem_spec] * (2 + count),
        out_specs=[vmem_spec] * 2,
        scratch_shapes=[pltpu.VMEM((2 * classes, width), jnp.bfloat16)],
        compiler_params=params,
        name="logits",
    )(place, low_rows, near_rows, *blocks)
    stats = lax.all_to_all(
        jnp.broadcast_to(stats[None], (count,) + stats.shape),
        "cls",
        split_axis=0,
        concat_axis=0,
        axis_index_groups=[list(range(side, groups, 2)) for side in (0, 1)],
        tiled=True,
    )

    def grads(side):
        kinds = [jnp.float32 if side == 0 and shift == 0 else jnp.bfloat16 for shift in range(replicas)]
        shapes = [jax.ShapeDtypeStruct((part, width), kind) for kind in kinds]
        if side == 0:
            shapes.append(jax.ShapeDtypeStruct((1, local_rows), jnp.float32))
        return pl.pallas_call(
            functools.partial(grads_kernel, count, replicas, side),
            out_shape=shapes,
            in_specs=[smem_spec] + [vmem_spec] * (2 + count),
            out_specs=[vmem_spec] * len(shapes),
            scratch_shapes=[
                pltpu.VMEM((classes, count * local_rows), jnp.bfloat16),
                pltpu.VMEM((count * local_rows, width), jnp.bfloat16),
                pltpu.VMEM((classes, width), jnp.float32),
                pltpu.VMEM((2 * count, local_rows), jnp.float32),
            ],
            compiler_params=params,
            name="grads",
        )(place, exps, stats, *blocks)

    away = [swap_all(block, replicas + shift) for shift, block in enumerate(grads(1))]
    *near, loss = grads(0)
    mine = near[0]
    others = away + [swap_all(near[shift], shift) for shift in range(1, replicas)]
    weight_grad = pl.pallas_call(
        functools.partial(finish_kernel, len(others)),
        out_shape=jax.ShapeDtypeStruct((part, width), jnp.float32),
        in_specs=[smem_spec] + [vmem_spec] * (3 + len(others)),
        out_specs=vmem_spec,
        name="finish",
    )(place, unit_rows, norms, mine, *others)
    return (loss.reshape(local_rows), weight_grad)


def solution(mesh):
    in_specs = (P(("cls", "dp"), None), P(("cls", "dp")), P("cls", None), P("cls"))
    out_specs = (P(("cls", "dp")), P(("cls", "dp"), None))
    return jax.shard_map(
        per_device, mesh=mesh, in_specs=in_specs, out_specs=out_specs, check_vma=False
    )
```

```python
import functools

import jax
import jax.numpy as jnp
from jax import lax
from jax.experimental import pallas as pl
from jax.experimental.pallas import tpu as pltpu
from jax.sharding import PartitionSpec as P

logit_scale = 64.0
margin = 0.35
epsilon = 1e-06
digit = 256
extra = 16
square = 4

vmem_spec = pl.BlockSpec(memory_space=pltpu.VMEM)
smem_spec = pl.BlockSpec(memory_space=pltpu.SMEM)
any_spec = pl.BlockSpec(memory_space=pl.ANY)


def params(mebibytes):
    return pltpu.CompilerParams(vmem_limit_bytes=mebibytes * 1024 * 1024)


def normalize_kernel(feat_ref, label_ref, out_ref):
    rows = feat_ref.shape[0]
    wide = feat_ref[...].astype(jnp.float32)
    squares = jnp.sum(wide * wide, axis=1, keepdims=True)
    out_ref[:rows, :] = (wide * lax.rsqrt(squares + epsilon)).astype(jnp.bfloat16)
    labels = label_ref[...]
    digits = jnp.concatenate([labels // digit, labels % digit], axis=1).astype(jnp.float32)
    blank = jnp.zeros((extra, feat_ref.shape[1]), jnp.float32)
    digits = jnp.concatenate([digits, blank[:1, digits.shape[1] :]], axis=1)
    line = lax.broadcasted_iota(jnp.int32, blank.shape, 0)
    out_ref[rows:, :] = jnp.where(line == 0, digits, blank).astype(jnp.bfloat16)


def labels_of(feat_ref):
    rows = feat_ref.shape[0] - extra
    digits = feat_ref[rows:, :].astype(jnp.float32)[:1, :].astype(jnp.int32)
    return digits[:, :rows] * digit + digits[:, rows : 2 * rows]


def choose_kernel(place_ref, sampled_ref, weight_ref, low_ref, chosen_ref, sem):
    part = low_ref.shape[0]
    first = place_ref[square] * part

    def start_row(row, carry):
        pltpu.make_async_copy(
            weight_ref.at[pl.ds(sampled_ref[first + row], 1), :],
            chosen_ref.at[pl.ds(row, 1), :],
            sem,
        ).start()
        return carry

    lax.fori_loop(0, part, start_row, 0, unroll=8)
    pltpu.make_async_copy(weight_ref.at[pl.ds(0, part), :], chosen_ref, sem).wait()
    rows = chosen_ref[...]
    inverse = lax.rsqrt(jnp.sum(rows * rows, axis=1, keepdims=True) + epsilon)
    low_ref[...] = (rows * inverse).astype(jnp.bfloat16)


def logits_kernel(count, place_ref, *refs):
    classes, feats = refs[:square], refs[square : square + count]
    exp_ref, stat_ref, every_ref, label_ref, rows = refs[square + count :]
    part = classes[0].shape[0]
    lanes = feats[0].shape[0] - extra
    for side in range(square):
        rows[side * part : (side + 1) * part, :] = classes[side][...]
    for block in range(count):
        every_ref[block * lanes : (block + 1) * lanes, :] = feats[block][:lanes, :]
        label_ref[block : block + 1, :] = labels_of(feats[block])
    line = lax.broadcasted_iota(jnp.int32, (part, lanes), 0)
    for pair in range(0, count, 2):
        cosine = lax.dot_general(
            rows[...],
            every_ref[pair * lanes : (pair + 2) * lanes, :],
            (((1,), (1,)), ((), ())),
            preferred_element_type=jnp.float32,
        )
        for block in (pair, pair + 1):
            start = (block - pair) * lanes
            labels = label_ref[block : block + 1, :]
            total = jnp.zeros((1, lanes), jnp.float32)
            target = jnp.zeros((1, lanes), jnp.float32)
            for side in range(square):
                span = slice(side * part, (side + 1) * part)
                hit = labels - place_ref[side] == line
                logits = logit_scale * (
                    cosine[span, start : start + lanes] - margin * hit.astype(jnp.float32)
                )
                exps = jnp.exp(logits - logit_scale)
                exp_ref[span, block * lanes : (block + 1) * lanes] = exps
                total = total + jnp.sum(exps, axis=0, keepdims=True)
                target = target + jnp.sum(jnp.where(hit, logits, 0.0), axis=0, keepdims=True)
            group = place_ref[square + 1] ^ block
            stat_ref[pl.ds(group, 1), :] = total
            stat_ref[pl.ds(count + group, 1), :] = target


def grads_kernel(count, replicas, sides, place_ref, exp_ref, stat_ref, every_ref, label_ref, *refs):
    outs, grads, total = refs[: len(sides)], refs[-2], refs[-1]
    part = exp_ref.shape[0] // square
    lanes = label_ref.shape[1]
    scale = logit_scale / replicas
    group = place_ref[square + 1]
    if 0 in sides:
        refs[len(sides)][...] = (
            logit_scale
            + jnp.log(stat_ref[pl.ds(group, 1), :])
            - stat_ref[pl.ds(count + group, 1), :]
        )
    line = lax.broadcasted_iota(jnp.int32, (part, lanes), 0)
    for block in range(count):
        inverse = 1.0 / stat_ref[pl.ds(group ^ block, 1), :]
        columns = slice(block * lanes, (block + 1) * lanes)
        labels = label_ref[block : block + 1, :]
        for index, side in enumerate(sides):
            hit = labels - place_ref[side] == line
            exps = exp_ref[side * part : (side + 1) * part, columns]
            grads[index * part : (index + 1) * part, columns] = (
                exps * inverse - jnp.where(hit, 1.0, 0.0)
            ).astype(jnp.bfloat16)
    total[...] = jnp.dot(grads[...], every_ref[...], preferred_element_type=jnp.float32)
    for index, out in enumerate(outs):
        out[...] = (total[index * part : (index + 1) * part, :] * scale).astype(out.dtype)


def finish_kernel(chosen_ref, own_ref, *refs):
    others, out_ref = refs[:-1], refs[-1]
    summed = own_ref[...]
    for other in others:
        summed = summed + other[...].astype(jnp.float32)
    rows = chosen_ref[...]
    inverse = lax.rsqrt(jnp.sum(rows * rows, axis=1, keepdims=True) + epsilon)
    unit = rows * inverse
    radial = jnp.sum(unit * summed, axis=1, keepdims=True)
    out_ref[...] = inverse * (summed - unit * radial)


def per_device(features, labels, weights, sampled):
    groups = lax.axis_size("cls")
    replicas = lax.axis_size("dp")
    local_rows, width = features.shape
    classes = sampled.shape[0]
    part = classes // replicas
    position = lax.axis_index("cls").astype(jnp.int32)
    replica = lax.axis_index("dp").astype(jnp.int32)
    place = jnp.stack(
        [(position ^ side) * classes + replica * part for side in range(square)]
        + [replica, position // square * replicas + replica]
    )

    def swap(value, chip_mask, core_mask):
        mask = chip_mask * replicas + core_mask
        return lax.ppermute(
            value, ("cls", "dp"), [(i, i ^ mask) for i in range(groups * replicas)]
        )

    bits = [(0, 1 << bit) for bit in range(replicas.bit_length() - 1)]
    far_bits = [(1 << bit, 0) for bit in range(2, groups.bit_length() - 1)]

    unit_feats = pl.pallas_call(
        normalize_kernel,
        out_shape=jax.ShapeDtypeStruct((local_rows + extra, width), jnp.bfloat16),
        in_specs=[vmem_spec] * 2,
        out_specs=vmem_spec,
        compiler_params=params(8),
        name="normalize",
    )(features, labels.reshape(1, local_rows))
    far = [unit_feats] + [swap(unit_feats, mask, 0) for mask in range(square, groups, square)]
    blocks = []
    for block in far:
        spread = [block]
        for _, bit in bits:
            spread = spread + [swap(value, 0, bit) for value in spread]
        blocks = blocks + spread
    count = len(blocks)
    low_rows, chosen = pl.pallas_call(
        choose_kernel,
        out_shape=[
            jax.ShapeDtypeStruct((part, width), jnp.bfloat16),
            jax.ShapeDtypeStruct((part, width), jnp.float32),
        ],
        in_specs=[smem_spec, smem_spec, any_spec],
        out_specs=[vmem_spec] * 2,
        scratch_shapes=[pltpu.SemaphoreType.DMA],
        compiler_params=params(8),
        name="choose",
    )(place, sampled, weights)
    rows = [low_rows] + [swap(low_rows, side, 0) for side in range(1, square)]

    exps, stats, every, marks = pl.pallas_call(
        functools.partial(logits_kernel, count),
        out_shape=[
            jax.ShapeDtypeStruct((square * part, count * local_rows), jnp.float32),
            jax.ShapeDtypeStruct((2 * count, local_rows), jnp.float32),
            jax.ShapeDtypeStruct((count * local_rows, width), jnp.bfloat16),
            jax.ShapeDtypeStruct((count, local_rows), jnp.int32),
        ],
        in_specs=[smem_spec] + [vmem_spec] * (square + count),
        out_specs=[vmem_spec] * 4,
        scratch_shapes=[pltpu.VMEM((square * part, width), jnp.bfloat16)],
        compiler_params=params(48),
        name="logits",
    )(place, *rows, *blocks)
    for chip_mask, core_mask in bits + far_bits:
        stats = stats + swap(stats, chip_mask, core_mask)

    def grads(sides):
        kinds = [jnp.bfloat16 if side else jnp.float32 for side in sides]
        shapes = [jax.ShapeDtypeStruct((part, width), kind) for kind in kinds]
        if 0 in sides:
            shapes.append(jax.ShapeDtypeStruct((1, local_rows), jnp.float32))
        return pl.pallas_call(
            functools.partial(grads_kernel, count, replicas, sides),
            out_shape=shapes,
            in_specs=[smem_spec] + [vmem_spec] * 4,
            out_specs=[vmem_spec] * len(shapes),
            scratch_shapes=[
                pltpu.VMEM((len(sides) * part, count * local_rows), jnp.bfloat16),
                pltpu.VMEM((len(sides) * part, width), jnp.float32),
            ],
            compiler_params=params(48),
            name="grads",
        )(place, exps, stats, every, marks)

    away = [swap(block, side, 0) for side, block in enumerate(grads((1, 2, 3)), 1)]
    mine, loss = grads((0,))
    weight_grad = pl.pallas_call(
        finish_kernel,
        out_shape=jax.ShapeDtypeStruct((part, width), jnp.float32),
        in_specs=[vmem_spec] * (2 + len(away)),
        out_specs=vmem_spec,
        compiler_params=params(8),
        name="finish",
    )(chosen, mine, *away)
    return (loss.reshape(local_rows), weight_grad)


def solution(mesh):
    in_specs = (P(("cls", "dp"), None), P(("cls", "dp")), P("cls", None), P("cls"))
    out_specs = (P(("cls", "dp")), P(("cls", "dp"), None))
    return jax.shard_map(
        per_device, mesh=mesh, in_specs=in_specs, out_specs=out_specs, check_vma=False
    )
```

```python
import functools

import jax
import jax.numpy as jnp
from jax import lax
from jax.experimental import pallas as pl
from jax.experimental.pallas import tpu as pltpu
from jax.sharding import PartitionSpec as P

logit_scale = 64.0
margin = 0.35
epsilon = 1e-06
digit = 256
extra = 16
square = 4

vmem_spec = pl.BlockSpec(memory_space=pltpu.VMEM)
smem_spec = pl.BlockSpec(memory_space=pltpu.SMEM)
hbm_spec = pl.BlockSpec(memory_space=pltpu.HBM)


vmem_bytes = 64 * 1024 * 1024


def params(room):
    return pltpu.CompilerParams(vmem_limit_bytes=vmem_bytes - room * 1024)


def normalize_kernel(feat_hbm, label_hbm, out_ref, feat_ref, label_ref, sems):
    copies = [
        pltpu.make_async_copy(feat_hbm, feat_ref, sems.at[0]),
        pltpu.make_async_copy(label_hbm, label_ref, sems.at[1]),
    ]
    for copy in copies:
        copy.start()
    for copy in copies:
        copy.wait()
    rows = feat_ref.shape[0]
    wide = feat_ref[...].astype(jnp.float32)
    squares = jnp.sum(wide * wide, axis=1, keepdims=True)
    out_ref[:rows, :] = (wide * lax.rsqrt(squares + epsilon)).astype(jnp.bfloat16)
    labels = label_ref[...]
    digits = jnp.concatenate([labels // digit, labels % digit], axis=1).astype(jnp.float32)
    blank = jnp.zeros((extra, feat_ref.shape[1]), jnp.float32)
    digits = jnp.concatenate([digits, blank[:1, digits.shape[1] :]], axis=1)
    line = lax.broadcasted_iota(jnp.int32, blank.shape, 0)
    out_ref[rows:, :] = jnp.where(line == 0, digits, blank).astype(jnp.bfloat16)


def labels_of(feat_ref):
    rows = feat_ref.shape[0] - extra
    digits = feat_ref[rows:, :].astype(jnp.float32)[:1, :].astype(jnp.int32)
    return digits[:, :rows] * digit + digits[:, rows : 2 * rows]


def choose_kernel(place_ref, sampled_hbm, weight_hbm, low_ref, chosen_ref, sampled_ref, sems):
    part = low_ref.shape[0]
    first = place_ref[square] * part
    copy = pltpu.make_async_copy(sampled_hbm, sampled_ref, sems.at[0])
    copy.start()
    copy.wait()

    def start_row(row, carry):
        pltpu.make_async_copy(
            weight_hbm.at[pl.ds(sampled_ref[first + row], 1), :],
            chosen_ref.at[pl.ds(row, 1), :],
            sems.at[1],
        ).start()
        return carry

    lax.fori_loop(0, part, start_row, 0, unroll=8)
    pltpu.make_async_copy(weight_hbm.at[pl.ds(0, part), :], chosen_ref, sems.at[1]).wait()
    rows = chosen_ref[...]
    inverse = lax.rsqrt(jnp.sum(rows * rows, axis=1, keepdims=True) + epsilon)
    low_ref[...] = (rows * inverse).astype(jnp.bfloat16)


def logits_kernel(count, span, place_ref, *refs):
    classes, feats = refs[:square], refs[square : square + len(span)]
    exp_ref, stat_ref, every_ref, label_ref, rows = refs[-5:]
    part = classes[0].shape[0]
    lanes = feats[0].shape[0] - extra
    if span[0] > 0:
        stat_ref[...] = refs[square + len(span)][...]
    for side in range(square):
        rows[side * part : (side + 1) * part, :] = classes[side][...]
    for index in range(len(span)):
        every_ref[index * lanes : (index + 1) * lanes, :] = feats[index][:lanes, :]
        label_ref[index : index + 1, :] = labels_of(feats[index])
    line = lax.broadcasted_iota(jnp.int32, (part, lanes), 0)
    for pair in range(0, len(span), 2):
        cosine = lax.dot_general(
            rows[...],
            every_ref[pair * lanes : (pair + 2) * lanes, :],
            (((1,), (1,)), ((), ())),
            preferred_element_type=jnp.float32,
        )
        for index in (pair, pair + 1):
            start = (index - pair) * lanes
            labels = label_ref[index : index + 1, :]
            total = jnp.zeros((1, lanes), jnp.float32)
            target = jnp.zeros((1, lanes), jnp.float32)
            for side in range(square):
                lines = slice(side * part, (side + 1) * part)
                hit = labels - place_ref[side] == line
                logits = logit_scale * (
                    cosine[lines, start : start + lanes] - margin * hit.astype(jnp.float32)
                )
                exps = jnp.exp(logits - logit_scale)
                exp_ref[lines, index * lanes : (index + 1) * lanes] = exps
                total = total + jnp.sum(exps, axis=0, keepdims=True)
                target = target + jnp.sum(jnp.where(hit, logits, 0.0), axis=0, keepdims=True)
            group = place_ref[square + 1] ^ span[index]
            stat_ref[pl.ds(group, 1), :] = total
            stat_ref[pl.ds(count + group, 1), :] = target


def grads_kernel(count, replicas, spans, sides, place_ref, stat_ref, *refs):
    chunks = [refs[3 * index : 3 * index + 3] for index in range(len(spans))]
    refs = refs[3 * len(spans) :]
    outs, scratch = refs[: len(sides)], refs[-len(spans) :]
    part = chunks[0][0].shape[0] // square
    lanes = stat_ref.shape[1]
    scale = logit_scale / replicas
    group = place_ref[square + 1]
    if 0 in sides:
        refs[len(sides)][...] = (
            logit_scale
            + jnp.log(stat_ref[pl.ds(group, 1), :])
            - stat_ref[pl.ds(count + group, 1), :]
        )
    line = lax.broadcasted_iota(jnp.int32, (part, lanes), 0)
    total = None
    for span, (exp_ref, every_ref, label_ref), grads in zip(spans, chunks, scratch):
        for index in range(len(span)):
            inverse = 1.0 / stat_ref[pl.ds(group ^ span[index], 1), :]
            columns = slice(index * lanes, (index + 1) * lanes)
            labels = label_ref[index : index + 1, :]
            for place, side in enumerate(sides):
                hit = labels - place_ref[side] == line
                exps = exp_ref[side * part : (side + 1) * part, columns]
                grads[place * part : (place + 1) * part, columns] = (
                    exps * inverse - jnp.where(hit, 1.0, 0.0)
                ).astype(jnp.bfloat16)
        product = jnp.dot(grads[...], every_ref[...], preferred_element_type=jnp.float32)
        total = product if total is None else total + product
    for index, out in enumerate(outs):
        out[...] = (total[index * part : (index + 1) * part, :] * scale).astype(out.dtype)


def finish_kernel(chosen_ref, own_ref, *refs):
    others, out_ref = refs[:-1], refs[-1]
    summed = own_ref[...]
    for other in others:
        summed = summed + other[...].astype(jnp.float32)
    rows = chosen_ref[...]
    inverse = lax.rsqrt(jnp.sum(rows * rows, axis=1, keepdims=True) + epsilon)
    unit = rows * inverse
    radial = jnp.sum(unit * summed, axis=1, keepdims=True)
    out_ref[...] = inverse * (summed - unit * radial)


def per_device(features, labels, weights, sampled):
    groups = lax.axis_size("cls")
    replicas = lax.axis_size("dp")
    local_rows, width = features.shape
    classes = sampled.shape[0]
    part = classes // replicas
    position = lax.axis_index("cls").astype(jnp.int32)
    replica = lax.axis_index("dp").astype(jnp.int32)
    place = jnp.stack(
        [(position ^ side) * classes + replica * part for side in range(square)]
        + [replica, position // square * replicas + replica]
    )

    def swap(value, chip_mask, core_mask):
        mask = chip_mask * replicas + core_mask
        return lax.ppermute(
            value, ("cls", "dp"), [(i, i ^ mask) for i in range(groups * replicas)]
        )

    bits = [(0, 1 << bit) for bit in range(replicas.bit_length() - 1)]
    far_bits = [(1 << bit, 0) for bit in range(2, groups.bit_length() - 1)]

    unit_feats = pl.pallas_call(
        normalize_kernel,
        out_shape=jax.ShapeDtypeStruct((local_rows + extra, width), jnp.bfloat16),
        in_specs=[hbm_spec] * 2,
        out_specs=vmem_spec,
        scratch_shapes=[
            pltpu.VMEM((local_rows, width), jnp.bfloat16),
            pltpu.VMEM((1, local_rows), jnp.int32),
            pltpu.SemaphoreType.DMA((2,)),
        ],
        compiler_params=params(10240),
        name="normalize",
    )(features, labels.reshape(1, local_rows))
    low_rows, chosen = pl.pallas_call(
        choose_kernel,
        out_shape=[
            jax.ShapeDtypeStruct((part, width), jnp.bfloat16),
            jax.ShapeDtypeStruct((part, width), jnp.float32),
        ],
        in_specs=[smem_spec, hbm_spec, hbm_spec],
        out_specs=[vmem_spec] * 2,
        scratch_shapes=[pltpu.SMEM((classes,), jnp.int32), pltpu.SemaphoreType.DMA((2,))],
        compiler_params=params(11264),
        name="choose",
    )(place, sampled, weights)
    rows = [low_rows] + [swap(low_rows, side, 0) for side in range(1, square)]

    def spread(block):
        near = [block]
        for _, bit in bits:
            near = near + [swap(value, 0, bit) for value in near]
        return near

    tie = lax.optimization_barrier
    top = groups // 2
    own = spread(unit_feats)
    high, low = {top: swap(unit_feats, top, 0)}, {0: unit_feats}
    for bit, _ in far_bits[:-1]:
        low.update({mask | bit: swap(block, bit, 0) for mask, block in list(low.items())})
    high, low, own, rows[1], rows[2] = tie((high, low, own, rows[1], rows[2]))
    far = {mask: spread(block) for mask, block in [*low.items(), *high.items()] if mask}
    for bit, _ in far_bits[:-1]:
        high.update({mask | bit: swap(block, bit, 0) for mask, block in list(high.items())})
    high, rows = tie((high, rows))
    far = {mask: spread(block) for mask, block in high.items()} | far | {0: own}
    blocks = [block for mask in range(0, groups, square) for block in far[mask]]
    count = len(blocks)
    spans = [tuple(range(count - replicas)), tuple(range(count - replicas, count))]
    chunks, stats = [], []
    for span in spans:
        exps, stats_now, every, marks = pl.pallas_call(
            functools.partial(logits_kernel, count, span),
            out_shape=[
                jax.ShapeDtypeStruct((square * part, len(span) * local_rows), jnp.float32),
                jax.ShapeDtypeStruct((2 * count, local_rows), jnp.float32),
                jax.ShapeDtypeStruct((len(span) * local_rows, width), jnp.bfloat16),
                jax.ShapeDtypeStruct((len(span), local_rows), jnp.int32),
            ],
            in_specs=[smem_spec] + [vmem_spec] * (square + len(span) + len(stats)),
            out_specs=[vmem_spec] * 4,
            scratch_shapes=[pltpu.VMEM((square * part, width), jnp.bfloat16)],
            compiler_params=params(16 * 1024),
            name="logits",
        )(place, *rows, *blocks[span[0] : span[-1] + 1], *stats)
        chunks, stats = chunks + [exps, every, marks], [stats_now]
    stats = stats[0]
    for chip_mask, core_mask in bits + far_bits:
        stats = stats + swap(stats, chip_mask, core_mask)

    def grads(sides):
        kinds = [jnp.bfloat16 if side else jnp.float32 for side in sides]
        shapes = [jax.ShapeDtypeStruct((part, width), kind) for kind in kinds]
        if 0 in sides:
            shapes.append(jax.ShapeDtypeStruct((1, local_rows), jnp.float32))
        return pl.pallas_call(
            functools.partial(grads_kernel, count, replicas, spans, sides),
            out_shape=shapes,
            in_specs=[smem_spec] + [vmem_spec] * (1 + len(chunks)),
            out_specs=[vmem_spec] * len(shapes),
            scratch_shapes=[
                pltpu.VMEM((len(sides) * part, len(span) * local_rows), jnp.bfloat16)
                for span in spans
            ],
            compiler_params=params(16 * 1024),
            name="grads",
        )(place, stats, *chunks)

    diagonal = swap(grads((3,))[0], 3, 0)
    away = [swap(block, side, 0) for side, block in enumerate(grads((1, 2)), 1)] + [diagonal]
    mine, loss = grads((0,))
    weight_grad = pl.pallas_call(
        finish_kernel,
        out_shape=jax.ShapeDtypeStruct((part, width), jnp.float32),
        in_specs=[vmem_spec] * (2 + len(away)),
        out_specs=vmem_spec,
        compiler_params=params(56 * 1024),
        name="finish",
    )(chosen, mine, *away)
    return (loss.reshape(local_rows), weight_grad)


def solution(mesh):
    in_specs = (P(("cls", "dp"), None), P(("cls", "dp")), P("cls", None), P("cls"))
    out_specs = (P(("cls", "dp")), P(("cls", "dp"), None))
    return jax.shard_map(
        per_device, mesh=mesh, in_specs=in_specs, out_specs=out_specs, check_vma=False
    )
```

```python
import functools

import jax
import jax.numpy as jnp
from jax import lax
from jax.experimental import pallas as pl
from jax.experimental.pallas import tpu as pltpu
from jax.sharding import PartitionSpec as P

logit_scale = 64.0
margin = 0.35
epsilon = 1e-06
digit = 256
extra = 16
square = 4

vmem_spec = pl.BlockSpec(memory_space=pltpu.VMEM)
smem_spec = pl.BlockSpec(memory_space=pltpu.SMEM)
hbm_spec = pl.BlockSpec(memory_space=pltpu.HBM)


vmem_bytes = 64 * 1024 * 1024


def params(room):
    return pltpu.CompilerParams(vmem_limit_bytes=vmem_bytes - room * 1024)


def prepare_kernel(
    place_ref, sampled_hbm, label_hbm, feat_hbm, weight_hbm, unit_hbm, low_hbm, chosen_hbm,
    sampled_ref, label_ref, feat_ref, unit_ref, low_ref, chosen_ref, sems,
):
    part = low_ref.shape[0]
    first = place_ref[square] * part
    reads = [
        pltpu.make_async_copy(sampled_hbm, sampled_ref, sems.at[0]),
        pltpu.make_async_copy(feat_hbm, feat_ref, sems.at[1]),
        pltpu.make_async_copy(label_hbm, label_ref, sems.at[2]),
    ]
    for read in reads:
        read.start()
    reads[0].wait()

    def start_row(row, carry):
        pltpu.make_async_copy(
            weight_hbm.at[pl.ds(sampled_ref[first + row], 1), :],
            chosen_ref.at[pl.ds(row, 1), :],
            sems.at[3],
        ).start()
        return carry

    lax.fori_loop(0, part, start_row, 0, unroll=16)
    reads[1].wait()
    reads[2].wait()
    rows = feat_ref.shape[0]
    wide = feat_ref[...].astype(jnp.float32)
    squares = jnp.sum(wide * wide, axis=1, keepdims=True)
    unit_ref[:rows, :] = (wide * lax.rsqrt(squares + epsilon)).astype(jnp.bfloat16)
    labels = label_ref[...]
    digits = jnp.concatenate([labels // digit, labels % digit], axis=1).astype(jnp.float32)
    blank = jnp.zeros((extra, feat_ref.shape[1]), jnp.float32)
    digits = jnp.concatenate([digits, blank[:1, digits.shape[1] :]], axis=1)
    line = lax.broadcasted_iota(jnp.int32, blank.shape, 0)
    unit_ref[rows:, :] = jnp.where(line == 0, digits, blank).astype(jnp.bfloat16)
    writes = [pltpu.make_async_copy(unit_ref, unit_hbm, sems.at[0])]
    writes[0].start()
    pltpu.make_async_copy(weight_hbm.at[pl.ds(0, part), :], chosen_ref, sems.at[3]).wait()
    writes.append(pltpu.make_async_copy(chosen_ref, chosen_hbm, sems.at[1]))
    writes[1].start()
    bank = chosen_ref[...]
    inverse = lax.rsqrt(jnp.sum(bank * bank, axis=1, keepdims=True) + epsilon)
    low_ref[...] = (bank * inverse).astype(jnp.bfloat16)
    writes.append(pltpu.make_async_copy(low_ref, low_hbm, sems.at[2]))
    writes[2].start()
    for write in writes:
        write.wait()


def labels_of(feat_ref):
    rows = feat_ref.shape[0] - extra
    digits = feat_ref[rows:, :].astype(jnp.float32)[:1, :].astype(jnp.int32)
    return digits[:, :rows] * digit + digits[:, rows : 2 * rows]


def logits_kernel(count, span, place_ref, *refs):
    classes, feats = refs[:square], refs[square : square + len(span)]
    exp_ref, stat_ref, every_ref, label_ref, rows = refs[-5:]
    part = classes[0].shape[0]
    lanes = feats[0].shape[0] - extra
    if span[0] > 0:
        stat_ref[...] = refs[square + len(span)][...]
    for side in range(square):
        rows[side * part : (side + 1) * part, :] = classes[side][...]
    for index in range(len(span)):
        every_ref[index * lanes : (index + 1) * lanes, :] = feats[index][:lanes, :]
        label_ref[index : index + 1, :] = labels_of(feats[index])
    line = lax.broadcasted_iota(jnp.int32, (part, lanes), 0)
    for pair in range(0, len(span), 2):
        cosine = lax.dot_general(
            rows[...],
            every_ref[pair * lanes : (pair + 2) * lanes, :],
            (((1,), (1,)), ((), ())),
            preferred_element_type=jnp.float32,
        )
        for index in (pair, pair + 1):
            start = (index - pair) * lanes
            labels = label_ref[index : index + 1, :]
            total = jnp.zeros((1, lanes), jnp.float32)
            target = jnp.zeros((1, lanes), jnp.float32)
            for side in range(square):
                lines = slice(side * part, (side + 1) * part)
                hit = labels - place_ref[side] == line
                logits = logit_scale * (
                    cosine[lines, start : start + lanes] - margin * hit.astype(jnp.float32)
                )
                exps = jnp.exp(logits - logit_scale)
                exp_ref[lines, index * lanes : (index + 1) * lanes] = exps
                total = total + jnp.sum(exps, axis=0, keepdims=True)
                target = target + jnp.sum(jnp.where(hit, logits, 0.0), axis=0, keepdims=True)
            group = place_ref[square + 1] ^ span[index]
            stat_ref[pl.ds(group, 1), :] = total
            stat_ref[pl.ds(count + group, 1), :] = target


def grads_kernel(count, replicas, spans, sides, place_ref, stat_ref, *refs):
    chunks = [refs[3 * index : 3 * index + 3] for index in range(len(spans))]
    refs = refs[3 * len(spans) :]
    outs, scratch = refs[: len(sides)], refs[-len(spans) :]
    part = chunks[0][0].shape[0] // square
    lanes = stat_ref.shape[1]
    scale = logit_scale / replicas
    group = place_ref[square + 1]
    if 0 in sides:
        refs[len(sides)][...] = (
            logit_scale
            + jnp.log(stat_ref[pl.ds(group, 1), :])
            - stat_ref[pl.ds(count + group, 1), :]
        )
    line = lax.broadcasted_iota(jnp.int32, (part, lanes), 0)
    total = None
    for span, (exp_ref, every_ref, label_ref), grads in zip(spans, chunks, scratch):
        for index in range(len(span)):
            inverse = 1.0 / stat_ref[pl.ds(group ^ span[index], 1), :]
            columns = slice(index * lanes, (index + 1) * lanes)
            labels = label_ref[index : index + 1, :]
            for place, side in enumerate(sides):
                hit = labels - place_ref[side] == line
                exps = exp_ref[side * part : (side + 1) * part, columns]
                grads[place * part : (place + 1) * part, columns] = (
                    exps * inverse - jnp.where(hit, 1.0, 0.0)
                ).astype(jnp.bfloat16)
        product = jnp.dot(grads[...], every_ref[...], preferred_element_type=jnp.float32)
        total = product if total is None else total + product
    for index, out in enumerate(outs):
        out[...] = (total[index * part : (index + 1) * part, :] * scale).astype(out.dtype)


def hold_kernel(unit_ref, low_ref, unit_out, low_out):
    unit_out[...] = unit_ref[...]
    low_out[...] = low_ref[...]


def finish_kernel(chosen_ref, own_ref, *refs):
    others, out_ref = refs[:-1], refs[-1]
    summed = own_ref[...]
    for other in others:
        summed = summed + other[...].astype(jnp.float32)
    rows = chosen_ref[...]
    inverse = lax.rsqrt(jnp.sum(rows * rows, axis=1, keepdims=True) + epsilon)
    unit = rows * inverse
    radial = jnp.sum(unit * summed, axis=1, keepdims=True)
    out_ref[...] = inverse * (summed - unit * radial)


def per_device(features, labels, weights, sampled):
    groups = lax.axis_size("cls")
    replicas = lax.axis_size("dp")
    local_rows, width = features.shape
    classes = sampled.shape[0]
    part = classes // replicas
    position = lax.axis_index("cls").astype(jnp.int32)
    replica = lax.axis_index("dp").astype(jnp.int32)
    place = jnp.stack(
        [(position ^ side) * classes + replica * part for side in range(square)]
        + [replica, position // square * replicas + replica]
    )

    def swap(value, chip_mask, core_mask):
        mask = chip_mask * replicas + core_mask
        return lax.ppermute(
            value, ("cls", "dp"), [(i, i ^ mask) for i in range(groups * replicas)]
        )

    bits = [(0, 1 << bit) for bit in range(replicas.bit_length() - 1)]
    far_bits = [(1 << bit, 0) for bit in range(2, groups.bit_length() - 1)]

    unit_feats, low_rows, chosen = pl.pallas_call(
        prepare_kernel,
        out_shape=[
            jax.ShapeDtypeStruct((local_rows + extra, width), jnp.bfloat16),
            jax.ShapeDtypeStruct((part, width), jnp.bfloat16),
            jax.ShapeDtypeStruct((part, width), jnp.float32),
        ],
        in_specs=[smem_spec] + [hbm_spec] * 4,
        out_specs=[hbm_spec] * 3,
        scratch_shapes=[
            pltpu.SMEM((classes,), jnp.int32),
            pltpu.VMEM((1, local_rows), jnp.int32),
            pltpu.VMEM((local_rows, width), jnp.bfloat16),
            pltpu.VMEM((local_rows + extra, width), jnp.bfloat16),
            pltpu.VMEM((part, width), jnp.bfloat16),
            pltpu.VMEM((part, width), jnp.float32),
            pltpu.SemaphoreType.DMA((4,)),
        ],
        compiler_params=params(10 * 1024),
        name="prepare",
    )(place, sampled, labels.reshape(1, local_rows), features, weights)
    held_unit, held_low = pl.pallas_call(
        hold_kernel,
        out_shape=[
            jax.ShapeDtypeStruct(unit_feats.shape, unit_feats.dtype),
            jax.ShapeDtypeStruct(low_rows.shape, low_rows.dtype),
        ],
        in_specs=[vmem_spec] * 2,
        out_specs=[vmem_spec] * 2,
        compiler_params=params(56 * 1024),
        name="hold",
    )(unit_feats, low_rows)
    rows = [held_low] + [swap(low_rows, side, 0) for side in range(1, square)]

    def spread(block):
        near = [block]
        for _, bit in bits:
            near = near + [swap(value, 0, bit) for value in near]
        return near

    tie = lax.optimization_barrier
    top = groups // 2
    own = [held_unit] + spread(unit_feats)[1:]
    high, low = {top: swap(unit_feats, top, 0)}, {0: unit_feats}
    for bit, _ in far_bits[:-1]:
        low.update({mask | bit: swap(block, bit, 0) for mask, block in list(low.items())})
    high, low, rows, own[0] = tie((high, low, rows, own[0]))
    far = {mask: spread(block) for mask, block in [*low.items(), *high.items()] if mask}
    for bit, _ in far_bits[:-1]:
        high.update({mask | bit: swap(block, bit, 0) for mask, block in list(high.items())})
    far = {mask: spread(block) for mask, block in high.items()} | far | {0: own}
    blocks = [block for mask in range(0, groups, square) for block in far[mask]]
    count = len(blocks)
    spans = [tuple(range(count - replicas)), tuple(range(count - replicas, count))]
    chunks, stats = [], []
    for span in spans:
        exps, stats_now, every, marks = pl.pallas_call(
            functools.partial(logits_kernel, count, span),
            out_shape=[
                jax.ShapeDtypeStruct((square * part, len(span) * local_rows), jnp.float32),
                jax.ShapeDtypeStruct((2 * count, local_rows), jnp.float32),
                jax.ShapeDtypeStruct((len(span) * local_rows, width), jnp.bfloat16),
                jax.ShapeDtypeStruct((len(span), local_rows), jnp.int32),
            ],
            in_specs=[smem_spec] + [vmem_spec] * (square + len(span) + len(stats)),
            out_specs=[vmem_spec] * 4,
            scratch_shapes=[pltpu.VMEM((square * part, width), jnp.bfloat16)],
            compiler_params=params(16 * 1024),
            name="logits",
        )(place, *rows, *blocks[span[0] : span[-1] + 1], *stats)
        chunks, stats = chunks + [exps, every, marks], [stats_now]
    stats = stats[0]
    for chip_mask, core_mask in bits + far_bits:
        stats = stats + swap(stats, chip_mask, core_mask)

    def grads(sides):
        kinds = [jnp.bfloat16 if side else jnp.float32 for side in sides]
        shapes = [jax.ShapeDtypeStruct((part, width), kind) for kind in kinds]
        if 0 in sides:
            shapes.append(jax.ShapeDtypeStruct((1, local_rows), jnp.float32))
        return pl.pallas_call(
            functools.partial(grads_kernel, count, replicas, spans, sides),
            out_shape=shapes,
            in_specs=[smem_spec] + [vmem_spec] * (1 + len(chunks)),
            out_specs=[vmem_spec] * len(shapes),
            scratch_shapes=[
                pltpu.VMEM((len(sides) * part, len(span) * local_rows), jnp.bfloat16)
                for span in spans
            ],
            compiler_params=params(16 * 1024),
            name="grads",
        )(place, stats, *chunks)

    away = [swap(block, side, 0) for side, block in enumerate(grads((1, 2, 3)), 1)]
    mine, loss = grads((0,))
    weight_grad = pl.pallas_call(
        finish_kernel,
        out_shape=jax.ShapeDtypeStruct((part, width), jnp.float32),
        in_specs=[vmem_spec] * (2 + len(away)),
        out_specs=vmem_spec,
        compiler_params=params(56 * 1024),
        name="finish",
    )(chosen, mine, *away)
    return (loss.reshape(local_rows), weight_grad)


def solution(mesh):
    in_specs = (P(("cls", "dp"), None), P(("cls", "dp")), P("cls", None), P("cls"))
    out_specs = (P(("cls", "dp")), P(("cls", "dp"), None))
    return jax.shard_map(
        per_device, mesh=mesh, in_specs=in_specs, out_specs=out_specs, check_vma=False
    )
```

```python
import functools

import jax
import jax.numpy as jnp
from jax import lax
from jax.experimental import pallas as pl
from jax.experimental.pallas import tpu as pltpu
from jax.sharding import PartitionSpec as P

logit_scale = 64.0
margin = 0.35
epsilon = 1e-06
digit = 256
extra = 16
square = 4

vmem_spec = pl.BlockSpec(memory_space=pltpu.VMEM)
smem_spec = pl.BlockSpec(memory_space=pltpu.SMEM)
hbm_spec = pl.BlockSpec(memory_space=pltpu.HBM)


vmem_bytes = 64 * 1024 * 1024


def params(room):
    return pltpu.CompilerParams(vmem_limit_bytes=vmem_bytes - room * 1024)


def normalize_kernel(feat_hbm, label_hbm, out_ref, feat_ref, label_ref, sems):
    copies = [
        pltpu.make_async_copy(feat_hbm, feat_ref, sems.at[0]),
        pltpu.make_async_copy(label_hbm, label_ref, sems.at[1]),
    ]
    for copy in copies:
        copy.start()
    for copy in copies:
        copy.wait()
    rows = feat_ref.shape[0]
    wide = feat_ref[...].astype(jnp.float32)
    squares = jnp.sum(wide * wide, axis=1, keepdims=True)
    out_ref[:rows, :] = (wide * lax.rsqrt(squares + epsilon)).astype(jnp.bfloat16)
    labels = label_ref[...]
    digits = jnp.concatenate([labels // digit, labels % digit], axis=1).astype(jnp.float32)
    blank = jnp.zeros((extra, feat_ref.shape[1]), jnp.float32)
    digits = jnp.concatenate([digits, blank[:1, digits.shape[1] :]], axis=1)
    line = lax.broadcasted_iota(jnp.int32, blank.shape, 0)
    out_ref[rows:, :] = jnp.where(line == 0, digits, blank).astype(jnp.bfloat16)


def labels_of(feat_ref):
    rows = feat_ref.shape[0] - extra
    digits = feat_ref[rows:, :].astype(jnp.float32)[:1, :].astype(jnp.int32)
    return digits[:, :rows] * digit + digits[:, rows : 2 * rows]


def choose_kernel(place_ref, sampled_hbm, weight_hbm, low_ref, chosen_ref, sampled_ref, weight_ref, sems):
    part = chosen_ref.shape[0]
    first = place_ref[square] * part
    reads = [
        pltpu.make_async_copy(sampled_hbm, sampled_ref, sems.at[0]),
        pltpu.make_async_copy(weight_hbm, weight_ref, sems.at[1]),
    ]
    for read in reads:
        read.start()
    for read in reads:
        read.wait()

    def copy_rows(step, carry):
        for lane in range(16):
            row = step * 16 + lane
            chosen_ref[pl.ds(row, 1), :] = weight_ref[pl.ds(sampled_ref[first + row], 1), :]
        return carry

    lax.fori_loop(0, part // 16, copy_rows, 0)
    rows = chosen_ref[...]
    inverse = lax.rsqrt(jnp.sum(rows * rows, axis=1, keepdims=True) + epsilon)
    low = (rows * inverse).astype(jnp.bfloat16)
    for side in range(square):
        low_ref[side * part : (side + 1) * part, :] = low


def logits_kernel(count, span, place_ref, *refs):
    rows, feats = refs[0], refs[1 : 1 + len(span)]
    exp_ref, stat_ref, every_ref, label_ref = refs[-4:]
    part = rows.shape[0] // square
    lanes = feats[0].shape[0] - extra
    if len(refs) > 5 + len(span):
        stat_ref[...] = refs[1 + len(span)][...]
    for index in range(len(span)):
        every_ref[index * lanes : (index + 1) * lanes, :] = feats[index][:lanes, :]
        label_ref[index : index + 1, :] = labels_of(feats[index])
    line = lax.broadcasted_iota(jnp.int32, (part, lanes), 0)
    for pair in range(0, len(span), 2):
        cosine = lax.dot_general(
            rows[...],
            every_ref[pair * lanes : (pair + 2) * lanes, :],
            (((1,), (1,)), ((), ())),
            preferred_element_type=jnp.float32,
        )
        for index in (pair, pair + 1):
            start = (index - pair) * lanes
            labels = label_ref[index : index + 1, :]
            total = jnp.zeros((1, lanes), jnp.float32)
            target = jnp.zeros((1, lanes), jnp.float32)
            for side in range(square):
                lines = slice(side * part, (side + 1) * part)
                hit = labels - place_ref[side] == line
                logits = logit_scale * (
                    cosine[lines, start : start + lanes] - margin * hit.astype(jnp.float32)
                )
                exps = jnp.exp(logits - logit_scale)
                exp_ref[lines, index * lanes : (index + 1) * lanes] = exps
                total = total + jnp.sum(exps, axis=0, keepdims=True)
                target = target + jnp.sum(jnp.where(hit, logits, 0.0), axis=0, keepdims=True)
            group = place_ref[square + 1] ^ span[index]
            stat_ref[pl.ds(group, 1), :] = total
            stat_ref[pl.ds(count + group, 1), :] = target


def grads_kernel(count, replicas, spans, sides, place_ref, stat_ref, *refs):
    chunks = [refs[3 * index : 3 * index + 3] for index in range(len(spans))]
    refs = refs[3 * len(spans) :]
    outs, scratch = refs[: len(sides)], refs[-len(spans) :]
    part = chunks[0][0].shape[0] // square
    lanes = stat_ref.shape[1]
    scale = logit_scale / replicas
    group = place_ref[square + 1]
    if 0 in sides:
        refs[len(sides)][...] = (
            logit_scale
            + jnp.log(stat_ref[pl.ds(group, 1), :])
            - stat_ref[pl.ds(count + group, 1), :]
        )
    line = lax.broadcasted_iota(jnp.int32, (part, lanes), 0)
    total = None
    for span, (exp_ref, every_ref, label_ref), grads in zip(spans, chunks, scratch):
        for index in range(len(span)):
            inverse = 1.0 / stat_ref[pl.ds(group ^ span[index], 1), :]
            columns = slice(index * lanes, (index + 1) * lanes)
            labels = label_ref[index : index + 1, :]
            for place, side in enumerate(sides):
                corner = place_ref[square + 2] ^ side
                hit = labels - place_ref[corner] == line
                exps = exp_ref[pl.ds(pl.multiple_of(corner * part, part), part), columns]
                grads[place * part : (place + 1) * part, columns] = (
                    exps * inverse - jnp.where(hit, 1.0, 0.0)
                ).astype(jnp.bfloat16)
        product = jnp.dot(grads[...], every_ref[...], preferred_element_type=jnp.float32)
        total = product if total is None else total + product
    for index, out in enumerate(outs):
        out[...] = (total[index * part : (index + 1) * part, :] * scale).astype(out.dtype)


def finish_kernel(chosen_ref, own_ref, *refs):
    others, out_ref = refs[:-1], refs[-1]
    summed = own_ref[...]
    for other in others:
        summed = summed + other[...].astype(jnp.float32)
    rows = chosen_ref[...]
    inverse = lax.rsqrt(jnp.sum(rows * rows, axis=1, keepdims=True) + epsilon)
    unit = rows * inverse
    radial = jnp.sum(unit * summed, axis=1, keepdims=True)
    out_ref[...] = inverse * (summed - unit * radial)


def per_device(features, labels, weights, sampled):
    groups = lax.axis_size("cls")
    replicas = lax.axis_size("dp")
    local_rows, width = features.shape
    classes = sampled.shape[0]
    part = classes // replicas
    position = lax.axis_index("cls").astype(jnp.int32)
    replica = lax.axis_index("dp").astype(jnp.int32)
    place = jnp.stack(
        [(position // square * square + side) * classes + replica * part for side in range(square)]
        + [replica, position // square * replicas + replica, position % square]
    )

    def swap(value, chip_mask, core_mask):
        mask = chip_mask * replicas + core_mask
        return lax.ppermute(
            value, ("cls", "dp"), [(i, i ^ mask) for i in range(groups * replicas)]
        )

    bits = [(0, 1 << bit) for bit in range(replicas.bit_length() - 1)]
    far_bits = [(1 << bit, 0) for bit in range(2, groups.bit_length() - 1)]

    unit_feats = pl.pallas_call(
        normalize_kernel,
        out_shape=jax.ShapeDtypeStruct((local_rows + extra, width), jnp.bfloat16),
        in_specs=[hbm_spec] * 2,
        out_specs=vmem_spec,
        scratch_shapes=[
            pltpu.VMEM((local_rows, width), jnp.bfloat16),
            pltpu.VMEM((1, local_rows), jnp.int32),
            pltpu.SemaphoreType.DMA((2,)),
        ],
        compiler_params=params(10 * 1024),
        name="normalize",
    )(features, labels.reshape(1, local_rows))
    copies, chosen = pl.pallas_call(
        choose_kernel,
        out_shape=[
            jax.ShapeDtypeStruct((square * part, width), jnp.bfloat16),
            jax.ShapeDtypeStruct((part, width), jnp.float32),
        ],
        in_specs=[smem_spec, hbm_spec, hbm_spec],
        out_specs=[vmem_spec] * 2,
        scratch_shapes=[
            pltpu.SMEM((classes,), jnp.int32),
            pltpu.VMEM(weights.shape, jnp.float32),
            pltpu.SemaphoreType.DMA((2,)),
        ],
        compiler_params=params(11 * 1024),
        name="choose",
    )(place, sampled, weights)
    corners = [list(range(first, first + square)) for first in range(0, groups, square)]
    rows = lax.all_to_all(
        copies.reshape(square, part, width), "cls", split_axis=0, concat_axis=0, axis_index_groups=corners, tiled=True
    )

    def spread(block):
        near = [block]
        for _, bit in bits:
            near = near + [swap(value, 0, bit) for value in near]
        return near

    far = {mask: swap(unit_feats, mask, 0) for mask in range(square, groups, square)}
    last = groups // 2
    final = far.pop(last)
    own = spread(unit_feats)
    far, rows, own = lax.optimization_barrier((far, rows, own))
    far = {mask: spread(block) for mask, block in {last: final, **far}.items()} | {0: own}
    blocks = [block for mask in range(0, groups, square) for block in far[mask]]
    count = len(blocks)
    first = last // square * replicas
    late = tuple(range(first, first + replicas))
    spans = [tuple(index for index in range(count) if index not in late), late]
    chunks, stats = [], []
    for span in spans:
        exps, stats_now, every, marks = pl.pallas_call(
            functools.partial(logits_kernel, count, span),
            out_shape=[
                jax.ShapeDtypeStruct((square * part, len(span) * local_rows), jnp.float32),
                jax.ShapeDtypeStruct((2 * count, local_rows), jnp.float32),
                jax.ShapeDtypeStruct((len(span) * local_rows, width), jnp.bfloat16),
                jax.ShapeDtypeStruct((len(span), local_rows), jnp.int32),
            ],
            in_specs=[smem_spec] + [vmem_spec] * (1 + len(span) + len(stats)),
            out_specs=[vmem_spec] * 4,
            compiler_params=params(16 * 1024),
            name="logits",
        )(place, rows.reshape(square * part, width), *[blocks[index] for index in span], *stats)
        chunks, stats = chunks + [exps, every, marks], [stats_now]
    stats = stats[0]
    for chip_mask, core_mask in bits + far_bits:
        stats = stats + swap(stats, chip_mask, core_mask)

    def grads(sides):
        kinds = [jnp.bfloat16 if side else jnp.float32 for side in sides]
        shapes = [jax.ShapeDtypeStruct((part, width), kind) for kind in kinds]
        if 0 in sides:
            shapes.append(jax.ShapeDtypeStruct((1, local_rows), jnp.float32))
        return pl.pallas_call(
            functools.partial(grads_kernel, count, replicas, spans, sides),
            out_shape=shapes,
            in_specs=[smem_spec] + [vmem_spec] * (1 + len(chunks)),
            out_specs=[vmem_spec] * len(shapes),
            scratch_shapes=[
                pltpu.VMEM((len(sides) * part, len(span) * local_rows), jnp.bfloat16)
                for span in spans
            ],
            compiler_params=params(16 * 1024),
            name="grads",
        )(place, stats, *chunks)

    away = [swap(block, side, 0) for side, block in enumerate(grads((1, 2, 3)), 1)]
    mine, loss = grads((0,))
    weight_grad = pl.pallas_call(
        finish_kernel,
        out_shape=jax.ShapeDtypeStruct((part, width), jnp.float32),
        in_specs=[vmem_spec] * (2 + len(away)),
        out_specs=vmem_spec,
        compiler_params=params(56 * 1024),
        name="finish",
    )(chosen, mine, *away)
    return (loss.reshape(local_rows), weight_grad)


def solution(mesh):
    in_specs = (P(("cls", "dp"), None), P(("cls", "dp")), P("cls", None), P("cls"))
    out_specs = (P(("cls", "dp")), P(("cls", "dp"), None))
    return jax.shard_map(
        per_device, mesh=mesh, in_specs=in_specs, out_specs=out_specs, check_vma=False
    )
```

```python
import functools

import jax
import jax.numpy as jnp
from jax import lax
from jax.experimental import pallas as pl
from jax.experimental.pallas import tpu as pltpu
from jax.sharding import PartitionSpec as P

logit_scale = 64.0
margin = 0.35
epsilon = 1e-06
digit = 256
extra = 16
square = 4

vmem_spec = pl.BlockSpec(memory_space=pltpu.VMEM)
smem_spec = pl.BlockSpec(memory_space=pltpu.SMEM)
hbm_spec = pl.BlockSpec(memory_space=pltpu.HBM)


vmem_bytes = 64 * 1024 * 1024


def params(room):
    return pltpu.CompilerParams(vmem_limit_bytes=vmem_bytes - room * 1024)


def normalize_kernel(feat_hbm, label_hbm, out_ref, feat_ref, label_ref, sems):
    copies = [
        pltpu.make_async_copy(feat_hbm, feat_ref, sems.at[0]),
        pltpu.make_async_copy(label_hbm, label_ref, sems.at[1]),
    ]
    for copy in copies:
        copy.start()
    for copy in copies:
        copy.wait()
    rows = feat_ref.shape[0]
    wide = feat_ref[...].astype(jnp.float32)
    squares = jnp.sum(wide * wide, axis=1, keepdims=True)
    out_ref[:rows, :] = (wide * lax.rsqrt(squares + epsilon)).astype(jnp.bfloat16)
    labels = label_ref[...]
    digits = jnp.concatenate([labels // digit, labels % digit], axis=1).astype(jnp.float32)
    blank = jnp.zeros((extra, feat_ref.shape[1]), jnp.float32)
    digits = jnp.concatenate([digits, blank[:1, digits.shape[1] :]], axis=1)
    line = lax.broadcasted_iota(jnp.int32, blank.shape, 0)
    out_ref[rows:, :] = jnp.where(line == 0, digits, blank).astype(jnp.bfloat16)


def labels_of(feat_ref):
    rows = feat_ref.shape[0] - extra
    digits = feat_ref[rows:, :].astype(jnp.float32)[:1, :].astype(jnp.int32)
    return digits[:, :rows] * digit + digits[:, rows : 2 * rows]


def choose_kernel(place_ref, sampled_hbm, weight_hbm, low_ref, chosen_ref, sampled_ref, sems):
    part = low_ref.shape[0]
    first = place_ref[square] * part
    copy = pltpu.make_async_copy(sampled_hbm, sampled_ref, sems.at[0])
    copy.start()
    copy.wait()

    def start_row(row, carry):
        pltpu.make_async_copy(
            weight_hbm.at[pl.ds(sampled_ref[first + row], 1), :],
            chosen_ref.at[pl.ds(row, 1), :],
            sems.at[1],
        ).start()
        return carry

    lax.fori_loop(0, part, start_row, 0, unroll=8)
    pltpu.make_async_copy(weight_hbm.at[pl.ds(0, part), :], chosen_ref, sems.at[1]).wait()
    rows = chosen_ref[...]
    inverse = lax.rsqrt(jnp.sum(rows * rows, axis=1, keepdims=True) + epsilon)
    low_ref[...] = (rows * inverse).astype(jnp.bfloat16)


def logits_kernel(count, span, place_ref, *refs):
    classes, feats = refs[:square], refs[square : square + len(span)]
    exp_ref, stat_ref, every_ref, label_ref, rows = refs[-5:]
    part = classes[0].shape[0]
    lanes = feats[0].shape[0] - extra
    if len(refs) > square + 5 + len(span):
        stat_ref[...] = refs[square + len(span)][...]
    for side in range(square):
        rows[side * part : (side + 1) * part, :] = classes[side][...]
    for index in range(len(span)):
        every_ref[index * lanes : (index + 1) * lanes, :] = feats[index][:lanes, :]
        label_ref[index : index + 1, :] = labels_of(feats[index])
    line = lax.broadcasted_iota(jnp.int32, (part, lanes), 0)
    for pair in range(0, len(span), 2):
        cosine = lax.dot_general(
            rows[...],
            every_ref[pair * lanes : (pair + 2) * lanes, :],
            (((1,), (1,)), ((), ())),
            preferred_element_type=jnp.float32,
        )
        for index in (pair, pair + 1):
            start = (index - pair) * lanes
            labels = label_ref[index : index + 1, :]
            total = jnp.zeros((1, lanes), jnp.float32)
            target = jnp.zeros((1, lanes), jnp.float32)
            for side in range(square):
                lines = slice(side * part, (side + 1) * part)
                hit = labels - place_ref[side] == line
                logits = logit_scale * (
                    cosine[lines, start : start + lanes] - margin * hit.astype(jnp.float32)
                )
                exps = jnp.exp(logits - logit_scale)
                exp_ref[lines, index * lanes : (index + 1) * lanes] = exps
                total = total + jnp.sum(exps, axis=0, keepdims=True)
                target = target + jnp.sum(jnp.where(hit, logits, 0.0), axis=0, keepdims=True)
            group = place_ref[square + 1] ^ span[index]
            stat_ref[pl.ds(group, 1), :] = total
            stat_ref[pl.ds(count + group, 1), :] = target


def grads_kernel(count, replicas, spans, sides, place_ref, stat_ref, *refs):
    chunks = [refs[3 * index : 3 * index + 3] for index in range(len(spans))]
    refs = refs[3 * len(spans) :]
    outs, scratch = refs[: len(sides)], refs[-len(spans) :]
    part = chunks[0][0].shape[0] // square
    lanes = stat_ref.shape[1]
    scale = logit_scale / replicas
    group = place_ref[square + 1]
    if 0 in sides:
        refs[len(sides)][...] = (
            logit_scale
            + jnp.log(stat_ref[pl.ds(group, 1), :])
            - stat_ref[pl.ds(count + group, 1), :]
        )
    line = lax.broadcasted_iota(jnp.int32, (part, lanes), 0)
    total = None
    for span, (exp_ref, every_ref, label_ref), grads in zip(spans, chunks, scratch):
        for index in range(len(span)):
            inverse = 1.0 / stat_ref[pl.ds(group ^ span[index], 1), :]
            columns = slice(index * lanes, (index + 1) * lanes)
            labels = label_ref[index : index + 1, :]
            for place, side in enumerate(sides):
                hit = labels - place_ref[side] == line
                exps = exp_ref[side * part : (side + 1) * part, columns]
                grads[place * part : (place + 1) * part, columns] = (
                    exps * inverse - jnp.where(hit, 1.0, 0.0)
                ).astype(jnp.bfloat16)
        product = jnp.dot(grads[...], every_ref[...], preferred_element_type=jnp.float32)
        total = product if total is None else total + product
    for index, out in enumerate(outs):
        out[...] = (total[index * part : (index + 1) * part, :] * scale).astype(out.dtype)


def finish_kernel(chosen_ref, own_ref, *refs):
    others, out_ref = refs[:-1], refs[-1]
    summed = own_ref[...]
    for other in others:
        summed = summed + other[...].astype(jnp.float32)
    rows = chosen_ref[...]
    inverse = lax.rsqrt(jnp.sum(rows * rows, axis=1, keepdims=True) + epsilon)
    unit = rows * inverse
    radial = jnp.sum(unit * summed, axis=1, keepdims=True)
    out_ref[...] = inverse * (summed - unit * radial)


def per_device(features, labels, weights, sampled):
    groups = lax.axis_size("cls")
    replicas = lax.axis_size("dp")
    local_rows, width = features.shape
    classes = sampled.shape[0]
    part = classes // replicas
    position = lax.axis_index("cls").astype(jnp.int32)
    replica = lax.axis_index("dp").astype(jnp.int32)
    place = jnp.stack(
        [(position ^ side) * classes + replica * part for side in range(square)]
        + [replica, position // square * replicas + replica]
    )

    def swap(value, chip_mask, core_mask):
        mask = chip_mask * replicas + core_mask
        return lax.ppermute(
            value, ("cls", "dp"), [(i, i ^ mask) for i in range(groups * replicas)]
        )

    bits = [(0, 1 << bit) for bit in range(replicas.bit_length() - 1)]
    far_bits = [(1 << bit, 0) for bit in range(2, groups.bit_length() - 1)]

    unit_feats = pl.pallas_call(
        normalize_kernel,
        out_shape=jax.ShapeDtypeStruct((local_rows + extra, width), jnp.bfloat16),
        in_specs=[hbm_spec] * 2,
        out_specs=vmem_spec,
        scratch_shapes=[
            pltpu.VMEM((local_rows, width), jnp.bfloat16),
            pltpu.VMEM((1, local_rows), jnp.int32),
            pltpu.SemaphoreType.DMA((2,)),
        ],
        compiler_params=params(10240),
        name="normalize",
    )(features, labels.reshape(1, local_rows))
    low_rows, chosen = pl.pallas_call(
        choose_kernel,
        out_shape=[
            jax.ShapeDtypeStruct((part, width), jnp.bfloat16),
            jax.ShapeDtypeStruct((part, width), jnp.float32),
        ],
        in_specs=[smem_spec, hbm_spec, hbm_spec],
        out_specs=[vmem_spec] * 2,
        scratch_shapes=[pltpu.SMEM((classes,), jnp.int32), pltpu.SemaphoreType.DMA((2,))],
        compiler_params=params(11264),
        name="choose",
    )(place, sampled, weights)
    def spread(block):
        near = [block]
        for _, bit in bits:
            near = near + [swap(value, 0, bit) for value in near]
        return near

    tie = lax.optimization_barrier
    own = spread(unit_feats)
    low_rows, own = tie((low_rows, own))
    far = {mask: swap(unit_feats, mask, 0) for mask in range(square, groups, square)}
    side_rows = low_rows
    side_rows, far[square] = tie((side_rows, far[square]))
    rows = [low_rows, swap(low_rows, 1, 0), swap(low_rows, 2, 0), swap(side_rows, 3, 0)]
    near = far.pop(square)
    far, rows = tie((far, rows))
    far = {mask: spread(block) for mask, block in far.items()} | {0: own, square: spread(near)}
    blocks = [block for mask in range(0, groups, square) for block in far[mask]]
    count = len(blocks)
    early = tuple(
        index
        for index in range(count)
        if index < replicas or (index % replicas == 0 and index // replicas > 1)
    )
    spans = [early, tuple(index for index in range(count) if index not in early)]
    chunks, stats = [], []
    for span in spans:
        exps, stats_now, every, marks = pl.pallas_call(
            functools.partial(logits_kernel, count, span),
            out_shape=[
                jax.ShapeDtypeStruct((square * part, len(span) * local_rows), jnp.float32),
                jax.ShapeDtypeStruct((2 * count, local_rows), jnp.float32),
                jax.ShapeDtypeStruct((len(span) * local_rows, width), jnp.bfloat16),
                jax.ShapeDtypeStruct((len(span), local_rows), jnp.int32),
            ],
            in_specs=[smem_spec] + [vmem_spec] * (square + len(span) + len(stats)),
            out_specs=[vmem_spec] * 4,
            scratch_shapes=[pltpu.VMEM((square * part, width), jnp.bfloat16)],
            compiler_params=params(16 * 1024),
            name="logits",
        )(place, *rows, *[blocks[index] for index in span], *stats)
        chunks, stats = chunks + [exps, every, marks], [stats_now]
    stats = stats[0]
    for chip_mask, core_mask in bits + far_bits:
        stats = stats + swap(stats, chip_mask, core_mask)

    def grads(sides):
        kinds = [jnp.bfloat16 if side else jnp.float32 for side in sides]
        shapes = [jax.ShapeDtypeStruct((part, width), kind) for kind in kinds]
        if 0 in sides:
            shapes.append(jax.ShapeDtypeStruct((1, local_rows), jnp.float32))
        return pl.pallas_call(
            functools.partial(grads_kernel, count, replicas, spans, sides),
            out_shape=shapes,
            in_specs=[smem_spec] + [vmem_spec] * (1 + len(chunks)),
            out_specs=[vmem_spec] * len(shapes),
            scratch_shapes=[
                pltpu.VMEM((len(sides) * part, len(span) * local_rows), jnp.bfloat16)
                for span in spans
            ],
            compiler_params=params(16 * 1024),
            name="grads",
        )(place, stats, *chunks)

    away = [swap(block, side, 0) for side, block in enumerate(grads((1, 2, 3)), 1)]
    mine, loss = grads((0,))
    weight_grad = pl.pallas_call(
        finish_kernel,
        out_shape=jax.ShapeDtypeStruct((part, width), jnp.float32),
        in_specs=[vmem_spec] * (2 + len(away)),
        out_specs=vmem_spec,
        compiler_params=params(56 * 1024),
        name="finish",
    )(chosen, mine, *away)
    return (loss.reshape(local_rows), weight_grad)


def solution(mesh):
    in_specs = (P(("cls", "dp"), None), P(("cls", "dp")), P("cls", None), P("cls"))
    out_specs = (P(("cls", "dp")), P(("cls", "dp"), None))
    return jax.shard_map(
        per_device, mesh=mesh, in_specs=in_specs, out_specs=out_specs, check_vma=False
    )
```

```python
import functools

import jax
import jax.numpy as jnp
from jax import lax
from jax.experimental import pallas as pl
from jax.experimental.pallas import tpu as pltpu
from jax.sharding import PartitionSpec as P

logit_scale = 64.0
margin = 0.35
epsilon = 1e-06
digit = 256
extra = 16
square = 4

vmem_spec = pl.BlockSpec(memory_space=pltpu.VMEM)
smem_spec = pl.BlockSpec(memory_space=pltpu.SMEM)
hbm_spec = pl.BlockSpec(memory_space=pltpu.HBM)


vmem_bytes = 64 * 1024 * 1024


def params(room):
    return pltpu.CompilerParams(vmem_limit_bytes=vmem_bytes - room * 1024)


def normalize_kernel(feat_hbm, label_hbm, out_ref, feat_ref, label_ref, sems):
    copies = [
        pltpu.make_async_copy(feat_hbm, feat_ref, sems.at[0]),
        pltpu.make_async_copy(label_hbm, label_ref, sems.at[1]),
    ]
    for copy in copies:
        copy.start()
    for copy in copies:
        copy.wait()
    rows = feat_ref.shape[0]
    wide = feat_ref[...].astype(jnp.float32)
    squares = jnp.sum(wide * wide, axis=1, keepdims=True)
    out_ref[:rows, :] = (wide * lax.rsqrt(squares + epsilon)).astype(jnp.bfloat16)
    labels = label_ref[...]
    digits = jnp.concatenate([labels // digit, labels % digit], axis=1).astype(jnp.float32)
    blank = jnp.zeros((extra, feat_ref.shape[1]), jnp.float32)
    digits = jnp.concatenate([digits, blank[:1, digits.shape[1] :]], axis=1)
    line = lax.broadcasted_iota(jnp.int32, blank.shape, 0)
    out_ref[rows:, :] = jnp.where(line == 0, digits, blank).astype(jnp.bfloat16)


def labels_of(feat_ref):
    rows = feat_ref.shape[0] - extra
    digits = feat_ref[rows:, :].astype(jnp.float32)[:1, :].astype(jnp.int32)
    return digits[:, :rows] * digit + digits[:, rows : 2 * rows]


def choose_kernel(place_ref, sampled_hbm, weight_hbm, low_ref, chosen_ref, sampled_ref, sems):
    part = chosen_ref.shape[0]
    first = place_ref[square] * part
    copy = pltpu.make_async_copy(sampled_hbm, sampled_ref, sems.at[0])
    copy.start()
    copy.wait()

    def start_row(row, carry):
        pltpu.make_async_copy(
            weight_hbm.at[pl.ds(sampled_ref[first + row], 1), :],
            chosen_ref.at[pl.ds(row, 1), :],
            sems.at[1],
        ).start()
        return carry

    lax.fori_loop(0, part, start_row, 0, unroll=8)
    pltpu.make_async_copy(weight_hbm.at[pl.ds(0, part), :], chosen_ref, sems.at[1]).wait()
    rows = chosen_ref[...]
    inverse = lax.rsqrt(jnp.sum(rows * rows, axis=1, keepdims=True) + epsilon)
    low_ref[:part, :] = (rows * inverse).astype(jnp.bfloat16)
    low_ref[part:, :] = jnp.zeros_like(low_ref[part:, :])


def logits_kernel(count, span, place_ref, *refs):
    classes, feats = refs[:square], refs[square : square + len(span)]
    exp_ref, stat_ref, every_ref, label_ref, rows = refs[-5:]
    part = rows.shape[0] // square
    lanes = feats[0].shape[0] - extra
    if len(refs) > square + 5 + len(span):
        stat_ref[...] = refs[square + len(span)][...]
    for side in range(square):
        rows[side * part : (side + 1) * part, :] = classes[side][:part, :]
    for index in range(len(span)):
        every_ref[index * lanes : (index + 1) * lanes, :] = feats[index][:lanes, :]
        label_ref[index : index + 1, :] = labels_of(feats[index])
    line = lax.broadcasted_iota(jnp.int32, (part, lanes), 0)
    for pair in range(0, len(span), 2):
        cosine = lax.dot_general(
            rows[...],
            every_ref[pair * lanes : (pair + 2) * lanes, :],
            (((1,), (1,)), ((), ())),
            preferred_element_type=jnp.float32,
        )
        for index in (pair, pair + 1):
            start = (index - pair) * lanes
            labels = label_ref[index : index + 1, :]
            total = jnp.zeros((1, lanes), jnp.float32)
            target = jnp.zeros((1, lanes), jnp.float32)
            for side in range(square):
                lines = slice(side * part, (side + 1) * part)
                hit = labels - place_ref[side] == line
                logits = logit_scale * (
                    cosine[lines, start : start + lanes] - margin * hit.astype(jnp.float32)
                )
                exps = jnp.exp(logits - logit_scale)
                exp_ref[lines, index * lanes : (index + 1) * lanes] = exps
                total = total + jnp.sum(exps, axis=0, keepdims=True)
                target = target + jnp.sum(jnp.where(hit, logits, 0.0), axis=0, keepdims=True)
            group = place_ref[square + 1] ^ span[index]
            stat_ref[pl.ds(group, 1), :] = total
            stat_ref[pl.ds(count + group, 1), :] = target


def grads_kernel(count, replicas, spans, sides, place_ref, stat_ref, *refs):
    chunks = [refs[3 * index : 3 * index + 3] for index in range(len(spans))]
    refs = refs[3 * len(spans) :]
    outs, scratch = refs[: len(sides)], refs[-len(spans) :]
    part = chunks[0][0].shape[0] // square
    lanes = stat_ref.shape[1]
    scale = logit_scale / replicas
    group = place_ref[square + 1]
    if 0 in sides:
        refs[len(sides)][...] = (
            logit_scale
            + jnp.log(stat_ref[pl.ds(group, 1), :])
            - stat_ref[pl.ds(count + group, 1), :]
        )
    line = lax.broadcasted_iota(jnp.int32, (part, lanes), 0)
    total = None
    for span, (exp_ref, every_ref, label_ref), grads in zip(spans, chunks, scratch):
        for index in range(len(span)):
            inverse = 1.0 / stat_ref[pl.ds(group ^ span[index], 1), :]
            columns = slice(index * lanes, (index + 1) * lanes)
            labels = label_ref[index : index + 1, :]
            for place, side in enumerate(sides):
                hit = labels - place_ref[side] == line
                exps = exp_ref[side * part : (side + 1) * part, columns]
                grads[place * part : (place + 1) * part, columns] = (
                    exps * inverse - jnp.where(hit, 1.0, 0.0)
                ).astype(jnp.bfloat16)
        product = jnp.dot(grads[...], every_ref[...], preferred_element_type=jnp.float32)
        total = product if total is None else total + product
    for index, out in enumerate(outs):
        out[...] = (total[index * part : (index + 1) * part, :] * scale).astype(out.dtype)


def finish_kernel(chosen_ref, own_ref, *refs):
    others, out_ref = refs[:-1], refs[-1]
    summed = own_ref[...]
    for other in others:
        summed = summed + other[...].astype(jnp.float32)
    rows = chosen_ref[...]
    inverse = lax.rsqrt(jnp.sum(rows * rows, axis=1, keepdims=True) + epsilon)
    unit = rows * inverse
    radial = jnp.sum(unit * summed, axis=1, keepdims=True)
    out_ref[...] = inverse * (summed - unit * radial)


def per_device(features, labels, weights, sampled):
    groups = lax.axis_size("cls")
    replicas = lax.axis_size("dp")
    local_rows, width = features.shape
    classes = sampled.shape[0]
    part = classes // replicas
    position = lax.axis_index("cls").astype(jnp.int32)
    replica = lax.axis_index("dp").astype(jnp.int32)
    place = jnp.stack(
        [(position ^ side) * classes + replica * part for side in range(square)]
        + [replica, position // square * replicas + replica]
    )

    def swap(value, chip_mask, core_mask):
        mask = chip_mask * replicas + core_mask
        return lax.ppermute(
            value, ("cls", "dp"), [(i, i ^ mask) for i in range(groups * replicas)]
        )

    bits = [(0, 1 << bit) for bit in range(replicas.bit_length() - 1)]
    far_bits = [(1 << bit, 0) for bit in range(2, groups.bit_length() - 1)]

    unit_feats = pl.pallas_call(
        normalize_kernel,
        out_shape=jax.ShapeDtypeStruct((local_rows + extra, width), jnp.bfloat16),
        in_specs=[hbm_spec] * 2,
        out_specs=vmem_spec,
        scratch_shapes=[
            pltpu.VMEM((local_rows, width), jnp.bfloat16),
            pltpu.VMEM((1, local_rows), jnp.int32),
            pltpu.SemaphoreType.DMA((2,)),
        ],
        compiler_params=params(10240),
        name="normalize",
    )(features, labels.reshape(1, local_rows))
    low_rows, chosen = pl.pallas_call(
        choose_kernel,
        out_shape=[
            jax.ShapeDtypeStruct((part + 16, width), jnp.bfloat16),
            jax.ShapeDtypeStruct((part, width), jnp.float32),
        ],
        in_specs=[smem_spec, hbm_spec, hbm_spec],
        out_specs=[vmem_spec] * 2,
        scratch_shapes=[pltpu.SMEM((classes,), jnp.int32), pltpu.SemaphoreType.DMA((2,))],
        compiler_params=params(11264),
        name="choose",
    )(place, sampled, weights)
    def spread(block):
        near = [block]
        for _, bit in bits:
            near = near + [swap(value, 0, bit) for value in near]
        return near

    tie = lax.optimization_barrier
    own = spread(unit_feats)
    low_rows, own = tie((low_rows, own))
    top = groups // 2
    high, low = {top: swap(unit_feats, top, 0)}, {0: unit_feats}
    for bit, _ in far_bits[:-1]:
        low.update({mask | bit: swap(block, bit, 0) for mask, block in list(low.items())})
    low_rows, low = tie((low_rows, low))
    rows = [low_rows] + [swap(low_rows, side, 0) for side in range(1, square)]
    for bit, _ in far_bits[:-1]:
        high.update({mask | bit: swap(block, bit, 0) for mask, block in list(high.items())})
    rows = tie(rows)
    high, rows = tie((high, rows))
    far = {mask: spread(block) for mask, block in [*low.items(), *high.items()]} | {0: own}
    blocks = [block for mask in range(0, groups, square) for block in far[mask]]
    count = len(blocks)
    early = tuple(
        index
        for index in range(count)
        if index < replicas or (index % replicas == 0 and index // replicas > 1)
    )
    spans = [early, tuple(index for index in range(count) if index not in early)]
    chunks, stats = [], []
    for span in spans:
        exps, stats_now, every, marks = pl.pallas_call(
            functools.partial(logits_kernel, count, span),
            out_shape=[
                jax.ShapeDtypeStruct((square * part, len(span) * local_rows), jnp.float32),
                jax.ShapeDtypeStruct((2 * count, local_rows), jnp.float32),
                jax.ShapeDtypeStruct((len(span) * local_rows, width), jnp.bfloat16),
                jax.ShapeDtypeStruct((len(span), local_rows), jnp.int32),
            ],
            in_specs=[smem_spec] + [vmem_spec] * (square + len(span) + len(stats)),
            out_specs=[vmem_spec] * 4,
            scratch_shapes=[pltpu.VMEM((square * part, width), jnp.bfloat16)],
            compiler_params=params(16 * 1024),
            name="logits",
        )(place, *rows, *[blocks[index] for index in span], *stats)
        chunks, stats = chunks + [exps, every, marks], [stats_now]
    stats = stats[0]
    for chip_mask, core_mask in bits + far_bits:
        stats = stats + swap(stats, chip_mask, core_mask)

    def grads(sides):
        kinds = [jnp.bfloat16 if side else jnp.float32 for side in sides]
        shapes = [jax.ShapeDtypeStruct((part, width), kind) for kind in kinds]
        if 0 in sides:
            shapes.append(jax.ShapeDtypeStruct((1, local_rows), jnp.float32))
        return pl.pallas_call(
            functools.partial(grads_kernel, count, replicas, spans, sides),
            out_shape=shapes,
            in_specs=[smem_spec] + [vmem_spec] * (1 + len(chunks)),
            out_specs=[vmem_spec] * len(shapes),
            scratch_shapes=[
                pltpu.VMEM((len(sides) * part, len(span) * local_rows), jnp.bfloat16)
                for span in spans
            ],
            compiler_params=params(16 * 1024),
            name="grads",
        )(place, stats, *chunks)

    away = [swap(block, side, 0) for side, block in enumerate(grads((1, 2, 3)), 1)]
    mine, loss = grads((0,))
    weight_grad = pl.pallas_call(
        finish_kernel,
        out_shape=jax.ShapeDtypeStruct((part, width), jnp.float32),
        in_specs=[vmem_spec] * (2 + len(away)),
        out_specs=vmem_spec,
        compiler_params=params(56 * 1024),
        name="finish",
    )(chosen, mine, *away)
    return (loss.reshape(local_rows), weight_grad)


def solution(mesh):
    in_specs = (P(("cls", "dp"), None), P(("cls", "dp")), P("cls", None), P("cls"))
    out_specs = (P(("cls", "dp")), P(("cls", "dp"), None))
    return jax.shard_map(
        per_device, mesh=mesh, in_specs=in_specs, out_specs=out_specs, check_vma=False
    )
```

```python
import functools

import jax
import jax.numpy as jnp
from jax import lax
from jax.experimental import pallas as pl
from jax.experimental.pallas import tpu as pltpu
from jax.sharding import PartitionSpec as P

logit_scale = 64.0
margin = 0.35
epsilon = 1e-06
digit = 256
extra = 16
square = 4

vmem_spec = pl.BlockSpec(memory_space=pltpu.VMEM)
smem_spec = pl.BlockSpec(memory_space=pltpu.SMEM)
hbm_spec = pl.BlockSpec(memory_space=pltpu.HBM)


vmem_bytes = 64 * 1024 * 1024


def params(room):
    return pltpu.CompilerParams(vmem_limit_bytes=vmem_bytes - room * 1024)


def normalize_kernel(feat_hbm, label_hbm, out_ref, feat_ref, label_ref, sems):
    copies = [
        pltpu.make_async_copy(feat_hbm, feat_ref, sems.at[0]),
        pltpu.make_async_copy(label_hbm, label_ref, sems.at[1]),
    ]
    for copy in copies:
        copy.start()
    for copy in copies:
        copy.wait()
    rows = feat_ref.shape[0]
    wide = feat_ref[...].astype(jnp.float32)
    squares = jnp.sum(wide * wide, axis=1, keepdims=True)
    out_ref[:rows, :] = (wide * lax.rsqrt(squares + epsilon)).astype(jnp.bfloat16)
    labels = label_ref[...]
    digits = jnp.concatenate([labels // digit, labels % digit], axis=1).astype(jnp.float32)
    blank = jnp.zeros((extra, feat_ref.shape[1]), jnp.float32)
    digits = jnp.concatenate([digits, blank[:1, digits.shape[1] :]], axis=1)
    line = lax.broadcasted_iota(jnp.int32, blank.shape, 0)
    out_ref[rows:, :] = jnp.where(line == 0, digits, blank).astype(jnp.bfloat16)


def labels_of(feat_ref):
    rows = feat_ref.shape[0] - extra
    digits = feat_ref[rows:, :].astype(jnp.float32)[:1, :].astype(jnp.int32)
    return digits[:, :rows] * digit + digits[:, rows : 2 * rows]


def choose_kernel(place_ref, sampled_hbm, weight_hbm, low_ref, chosen_ref, sampled_ref, sems):
    part = chosen_ref.shape[0]
    first = place_ref[square] * part
    copy = pltpu.make_async_copy(sampled_hbm, sampled_ref, sems.at[0])
    copy.start()
    copy.wait()

    def start_row(row, carry):
        pltpu.make_async_copy(
            weight_hbm.at[pl.ds(sampled_ref[first + row], 1), :],
            chosen_ref.at[pl.ds(row, 1), :],
            sems.at[1],
        ).start()
        return carry

    lax.fori_loop(0, part, start_row, 0, unroll=8)
    pltpu.make_async_copy(weight_hbm.at[pl.ds(0, part), :], chosen_ref, sems.at[1]).wait()
    rows = chosen_ref[...]
    inverse = lax.rsqrt(jnp.sum(rows * rows, axis=1, keepdims=True) + epsilon)
    low_ref[:part, :] = (rows * inverse).astype(jnp.bfloat16)
    low_ref[part:, :] = jnp.zeros_like(low_ref[part:, :])


def logits_kernel(count, span, place_ref, *refs):
    classes, feats = refs[:square], refs[square : square + len(span)]
    exp_ref, stat_ref, every_ref, label_ref, rows = refs[-5:]
    part = rows.shape[0] // square
    lanes = feats[0].shape[0] - extra
    if len(refs) > square + 5 + len(span):
        stat_ref[...] = refs[square + len(span)][...]
    for side in range(square):
        rows[side * part : (side + 1) * part, :] = classes[side][:part, :]
    for index in range(len(span)):
        every_ref[index * lanes : (index + 1) * lanes, :] = feats[index][:lanes, :]
        label_ref[index : index + 1, :] = labels_of(feats[index])
    line = lax.broadcasted_iota(jnp.int32, (part, lanes), 0)
    for pair in range(0, len(span), 2):
        cosine = lax.dot_general(
            rows[...],
            every_ref[pair * lanes : (pair + 2) * lanes, :],
            (((1,), (1,)), ((), ())),
            preferred_element_type=jnp.float32,
        )
        for index in (pair, pair + 1):
            start = (index - pair) * lanes
            labels = label_ref[index : index + 1, :]
            total = jnp.zeros((1, lanes), jnp.float32)
            target = jnp.zeros((1, lanes), jnp.float32)
            for side in range(square):
                lines = slice(side * part, (side + 1) * part)
                hit = labels - place_ref[side] == line
                logits = logit_scale * (
                    cosine[lines, start : start + lanes] - margin * hit.astype(jnp.float32)
                )
                exps = jnp.exp(logits - logit_scale)
                exp_ref[lines, index * lanes : (index + 1) * lanes] = exps
                total = total + jnp.sum(exps, axis=0, keepdims=True)
                target = target + jnp.sum(jnp.where(hit, logits, 0.0), axis=0, keepdims=True)
            group = place_ref[square + 1] ^ span[index]
            stat_ref[pl.ds(group, 1), :] = total
            stat_ref[pl.ds(count + group, 1), :] = target


def grads_kernel(count, replicas, spans, sides, place_ref, stat_ref, *refs):
    chunks = [refs[3 * index : 3 * index + 3] for index in range(len(spans))]
    refs = refs[3 * len(spans) :]
    outs, scratch = refs[: len(sides)], refs[-len(spans) :]
    part = chunks[0][0].shape[0] // square
    lanes = stat_ref.shape[1]
    scale = logit_scale / replicas
    group = place_ref[square + 1]
    if 0 in sides:
        refs[len(sides)][...] = (
            logit_scale
            + jnp.log(stat_ref[pl.ds(group, 1), :])
            - stat_ref[pl.ds(count + group, 1), :]
        )
    line = lax.broadcasted_iota(jnp.int32, (part, lanes), 0)
    total = None
    for span, (exp_ref, every_ref, label_ref), grads in zip(spans, chunks, scratch):
        for index in range(len(span)):
            inverse = 1.0 / stat_ref[pl.ds(group ^ span[index], 1), :]
            columns = slice(index * lanes, (index + 1) * lanes)
            labels = label_ref[index : index + 1, :]
            for place, side in enumerate(sides):
                hit = labels - place_ref[side] == line
                exps = exp_ref[side * part : (side + 1) * part, columns]
                grads[place * part : (place + 1) * part, columns] = (
                    exps * inverse - jnp.where(hit, 1.0, 0.0)
                ).astype(jnp.bfloat16)
        product = jnp.dot(grads[...], every_ref[...], preferred_element_type=jnp.float32)
        total = product if total is None else total + product
    for index, out in enumerate(outs):
        out[...] = (total[index * part : (index + 1) * part, :] * scale).astype(out.dtype)


def finish_kernel(chosen_ref, own_ref, *refs):
    others, out_ref = refs[:-1], refs[-1]
    summed = own_ref[...]
    for other in others:
        summed = summed + other[...].astype(jnp.float32)
    rows = chosen_ref[...]
    inverse = lax.rsqrt(jnp.sum(rows * rows, axis=1, keepdims=True) + epsilon)
    unit = rows * inverse
    radial = jnp.sum(unit * summed, axis=1, keepdims=True)
    out_ref[...] = inverse * (summed - unit * radial)


def per_device(features, labels, weights, sampled):
    groups = lax.axis_size("cls")
    replicas = lax.axis_size("dp")
    local_rows, width = features.shape
    classes = sampled.shape[0]
    part = classes // replicas
    position = lax.axis_index("cls").astype(jnp.int32)
    replica = lax.axis_index("dp").astype(jnp.int32)
    place = jnp.stack(
        [(position ^ side) * classes + replica * part for side in range(square)]
        + [replica, position // square * replicas + replica]
    )

    def swap(value, chip_mask, core_mask):
        mask = chip_mask * replicas + core_mask
        return lax.ppermute(
            value, ("cls", "dp"), [(i, i ^ mask) for i in range(groups * replicas)]
        )

    bits = [(0, 1 << bit) for bit in range(replicas.bit_length() - 1)]
    far_bits = [(1 << bit, 0) for bit in range(2, groups.bit_length() - 1)]

    unit_feats = pl.pallas_call(
        normalize_kernel,
        out_shape=jax.ShapeDtypeStruct((local_rows + extra, width), jnp.bfloat16),
        in_specs=[hbm_spec] * 2,
        out_specs=vmem_spec,
        scratch_shapes=[
            pltpu.VMEM((local_rows, width), jnp.bfloat16),
            pltpu.VMEM((1, local_rows), jnp.int32),
            pltpu.SemaphoreType.DMA((2,)),
        ],
        compiler_params=params(10240),
        name="normalize",
    )(features, labels.reshape(1, local_rows))
    low_rows, chosen = pl.pallas_call(
        choose_kernel,
        out_shape=[
            jax.ShapeDtypeStruct((part + 16, width), jnp.bfloat16),
            jax.ShapeDtypeStruct((part, width), jnp.float32),
        ],
        in_specs=[smem_spec, hbm_spec, hbm_spec],
        out_specs=[vmem_spec] * 2,
        scratch_shapes=[pltpu.SMEM((classes,), jnp.int32), pltpu.SemaphoreType.DMA((2,))],
        compiler_params=params(11264),
        name="choose",
    )(place, sampled, weights)
    def spread(block):
        near = [block]
        for _, bit in bits:
            near = near + [swap(value, 0, bit) for value in near]
        return near

    tie = lax.optimization_barrier
    own = spread(unit_feats)
    low_rows, own = tie((low_rows, own))
    top = groups // 2
    high, low = {top: swap(unit_feats, top, 0)}, {0: unit_feats}
    for bit, _ in far_bits[:-1]:
        low.update({mask | bit: swap(block, bit, 0) for mask, block in list(low.items())})
    rows = [low_rows] + [swap(low_rows, side, 0) for side in range(1, square)]
    for bit, _ in far_bits[:-1]:
        high.update({mask | bit: swap(block, bit, 0) for mask, block in list(high.items())})
    rows = tie(rows[::-1])[::-1]
    high, rows = tie((high, rows))
    far = {mask: spread(block) for mask, block in [*low.items(), *high.items()]} | {0: own}
    blocks = [block for mask in range(0, groups, square) for block in far[mask]]
    count = len(blocks)
    early = tuple(
        index
        for index in range(count)
        if index < replicas or (index % replicas == 0 and index // replicas > 1)
    )
    spans = [early, tuple(index for index in range(count) if index not in early)]
    chunks, stats = [], []
    for span in spans:
        exps, stats_now, every, marks = pl.pallas_call(
            functools.partial(logits_kernel, count, span),
            out_shape=[
                jax.ShapeDtypeStruct((square * part, len(span) * local_rows), jnp.float32),
                jax.ShapeDtypeStruct((2 * count, local_rows), jnp.float32),
                jax.ShapeDtypeStruct((len(span) * local_rows, width), jnp.bfloat16),
                jax.ShapeDtypeStruct((len(span), local_rows), jnp.int32),
            ],
            in_specs=[smem_spec] + [vmem_spec] * (square + len(span) + len(stats)),
            out_specs=[vmem_spec] * 4,
            scratch_shapes=[pltpu.VMEM((square * part, width), jnp.bfloat16)],
            compiler_params=params(16 * 1024),
            name="logits",
        )(place, *rows, *[blocks[index] for index in span], *stats)
        chunks, stats = chunks + [exps, every, marks], [stats_now]
    stats = stats[0]
    near = [(0, 0)]
    for chip_bit, core_bit in bits[:1] + far_bits[:1]:
        near = near + [(chip_mask | chip_bit, core_mask | core_bit) for chip_mask, core_mask in near]
    stats = sum((swap(stats, *masks) for masks in near[1:]), stats)
    for chip_mask, core_mask in bits[1:] + far_bits[1:]:
        stats = stats + swap(stats, chip_mask, core_mask)

    def grads(sides):
        kinds = [jnp.bfloat16 if side else jnp.float32 for side in sides]
        shapes = [jax.ShapeDtypeStruct((part, width), kind) for kind in kinds]
        if 0 in sides:
            shapes.append(jax.ShapeDtypeStruct((1, local_rows), jnp.float32))
        return pl.pallas_call(
            functools.partial(grads_kernel, count, replicas, spans, sides),
            out_shape=shapes,
            in_specs=[smem_spec] + [vmem_spec] * (1 + len(chunks)),
            out_specs=[vmem_spec] * len(shapes),
            scratch_shapes=[
                pltpu.VMEM((len(sides) * part, len(span) * local_rows), jnp.bfloat16)
                for span in spans
            ],
            compiler_params=params(16 * 1024),
            name="grads",
        )(place, stats, *chunks)

    away = [swap(block, side, 0) for side, block in enumerate(grads((1, 2, 3)), 1)]
    mine, loss = grads((0,))
    weight_grad = pl.pallas_call(
        finish_kernel,
        out_shape=jax.ShapeDtypeStruct((part, width), jnp.float32),
        in_specs=[vmem_spec] * (2 + len(away)),
        out_specs=vmem_spec,
        compiler_params=params(56 * 1024),
        name="finish",
    )(chosen, mine, *away)
    return (loss.reshape(local_rows), weight_grad)


def solution(mesh):
    in_specs = (P(("cls", "dp"), None), P(("cls", "dp")), P("cls", None), P("cls"))
    out_specs = (P(("cls", "dp")), P(("cls", "dp"), None))
    return jax.shard_map(
        per_device, mesh=mesh, in_specs=in_specs, out_specs=out_specs, check_vma=False
    )
```

```python
import functools

import jax
import jax.numpy as jnp
from jax import lax
from jax.experimental import pallas as pl
from jax.experimental.pallas import tpu as pltpu
from jax.sharding import PartitionSpec as P

logit_scale = 64.0
margin = 0.35
epsilon = 1e-06
digit = 256
extra = 8
square = 4

vmem_spec = pl.BlockSpec(memory_space=pltpu.VMEM)
smem_spec = pl.BlockSpec(memory_space=pltpu.SMEM)
hbm_spec = pl.BlockSpec(memory_space=pltpu.HBM)


vmem_bytes = 64 * 1024 * 1024


def params(room):
    return pltpu.CompilerParams(vmem_limit_bytes=vmem_bytes - room * 1024)


def normalize_kernel(feat_hbm, label_hbm, out_ref, feat_ref, label_ref, sems):
    copies = [
        pltpu.make_async_copy(feat_hbm, feat_ref, sems.at[0]),
        pltpu.make_async_copy(label_hbm, label_ref, sems.at[1]),
    ]
    for copy in copies:
        copy.start()
    for copy in copies:
        copy.wait()
    rows = feat_ref.shape[0]
    wide = feat_ref[...].astype(jnp.float32)
    squares = jnp.sum(wide * wide, axis=1, keepdims=True)
    out_ref[:rows, :] = (wide * lax.rsqrt(squares + epsilon)).astype(jnp.bfloat16)
    labels = label_ref[...]
    digits = jnp.concatenate([labels // digit, labels % digit], axis=1).astype(jnp.float32)
    blank = jnp.zeros((extra, feat_ref.shape[1]), jnp.float32)
    digits = jnp.concatenate([digits, blank[:1, digits.shape[1] :]], axis=1)
    line = lax.broadcasted_iota(jnp.int32, blank.shape, 0)
    out_ref[rows:, :] = jnp.where(line == 0, digits, blank).astype(jnp.bfloat16)


def labels_of(feat_ref):
    rows = feat_ref.shape[0] - extra
    digits = feat_ref[rows:, :].astype(jnp.float32)[:1, :].astype(jnp.int32)
    return digits[:, :rows] * digit + digits[:, rows : 2 * rows]


def choose_kernel(place_ref, sampled_hbm, weight_hbm, low_ref, chosen_ref, sampled_ref, sems):
    part = chosen_ref.shape[0]
    first = place_ref[square] * part
    copy = pltpu.make_async_copy(sampled_hbm, sampled_ref, sems.at[0])
    copy.start()
    copy.wait()

    def start_row(row, carry):
        pltpu.make_async_copy(
            weight_hbm.at[pl.ds(sampled_ref[first + row], 1), :],
            chosen_ref.at[pl.ds(row, 1), :],
            sems.at[1],
        ).start()
        return carry

    lax.fori_loop(0, part, start_row, 0, unroll=32)
    pltpu.make_async_copy(weight_hbm.at[pl.ds(0, part), :], chosen_ref, sems.at[1]).wait()
    rows = chosen_ref[...]
    inverse = lax.rsqrt(jnp.sum(rows * rows, axis=1, keepdims=True) + epsilon)
    low_ref[:part, :] = (rows * inverse).astype(jnp.bfloat16) * logit_scale
    low_ref[part:, :] = jnp.zeros_like(low_ref[part:, :])


def logits_kernel(count, span, joined, place_ref, *refs):
    feats = refs[: len(span)]
    if joined:
        rows, earlier_ref = refs[len(span) : len(span) + 2]
        exp_ref, stat_ref, every_ref, label_ref = refs[-4:]
        stat_ref[...] = earlier_ref[...]
    else:
        classes = refs[len(span) : len(span) + square]
        exp_ref, stat_ref, every_ref, label_ref, rows = refs[-5:]
        part = rows.shape[0] // square
        for side in range(square):
            rows[side * part : (side + 1) * part, :] = classes[side][:part, :]
    part = rows.shape[0] // square
    lanes = feats[0].shape[0] - extra
    for index in range(len(span)):
        every_ref[index * lanes : (index + 1) * lanes, :] = feats[index][:lanes, :]
        label_ref[index : index + 1, :] = labels_of(feats[index])
    line = lax.broadcasted_iota(jnp.int32, (part, lanes), 0)
    for pair in range(0, len(span), 2):
        scaled = lax.dot_general(
            rows[...],
            every_ref[pair * lanes : (pair + 2) * lanes, :],
            (((1,), (1,)), ((), ())),
            preferred_element_type=jnp.float32,
        )
        for index in (pair, pair + 1):
            start = (index - pair) * lanes
            labels = label_ref[index : index + 1, :]
            total = jnp.zeros((1, lanes), jnp.float32)
            target = jnp.zeros((1, lanes), jnp.float32)
            for side in range(square):
                lines = slice(side * part, (side + 1) * part)
                hit = labels - place_ref[side] == line
                tile = scaled[lines, start : start + lanes]
                exps = jnp.exp(
                    tile - jnp.where(hit, logit_scale + logit_scale * margin, logit_scale)
                )
                exp_ref[lines, index * lanes : (index + 1) * lanes] = exps
                total = total + jnp.sum(exps, axis=0, keepdims=True)
                target = target + jnp.sum(jnp.where(hit, tile, 0.0), axis=0, keepdims=True)
            group = place_ref[square + 1] ^ span[index]
            stat_ref[pl.ds(group, 1), :] = total
            stat_ref[pl.ds(count + group, 1), :] = target


def grads_kernel(count, replicas, spans, sides, place_ref, stat_ref, *refs):
    chunks = [refs[3 * index : 3 * index + 3] for index in range(len(spans))]
    refs = refs[3 * len(spans) :]
    outs, scratch = refs[: len(sides)], refs[-len(spans) :]
    part = chunks[0][0].shape[0] // square
    lanes = stat_ref.shape[1]
    scale = logit_scale / replicas
    group = place_ref[square + 1]
    if 0 in sides:
        refs[len(sides)][...] = (
            logit_scale
            + jnp.log(stat_ref[pl.ds(group, 1), :])
            - (stat_ref[pl.ds(count + group, 1), :] - logit_scale * margin)
        )
    line = lax.broadcasted_iota(jnp.int32, (part, lanes), 0)
    total = None
    for span, (exp_ref, every_ref, label_ref), grads in zip(spans, chunks, scratch):
        for index in range(len(span)):
            inverse = 1.0 / stat_ref[pl.ds(group ^ span[index], 1), :]
            columns = slice(index * lanes, (index + 1) * lanes)
            labels = label_ref[index : index + 1, :]
            for place, side in enumerate(sides):
                hit = labels - place_ref[side] == line
                exps = exp_ref[side * part : (side + 1) * part, columns]
                grads[place * part : (place + 1) * part, columns] = (
                    exps * inverse - jnp.where(hit, 1.0, 0.0)
                ).astype(jnp.bfloat16)
        product = jnp.dot(grads[...], every_ref[...], preferred_element_type=jnp.float32)
        total = product if total is None else total + product
    for index, out in enumerate(outs):
        out[...] = (total[index * part : (index + 1) * part, :] * scale).astype(out.dtype)


def finish_kernel(chosen_ref, own_ref, *refs):
    others, out_ref = refs[:-1], refs[-1]
    summed = own_ref[...]
    for other in others:
        summed = summed + other[...].astype(jnp.float32)
    rows = chosen_ref[...]
    inverse = lax.rsqrt(jnp.sum(rows * rows, axis=1, keepdims=True) + epsilon)
    unit = rows * inverse
    radial = jnp.sum(unit * summed, axis=1, keepdims=True)
    out_ref[...] = inverse * (summed - unit * radial)


def per_device(features, labels, weights, sampled):
    groups = lax.axis_size("cls")
    replicas = lax.axis_size("dp")
    local_rows, width = features.shape
    classes = sampled.shape[0]
    part = classes // replicas
    position = lax.axis_index("cls").astype(jnp.int32)
    replica = lax.axis_index("dp").astype(jnp.int32)
    place = jnp.stack(
        [(position ^ side) * classes + replica * part for side in range(square)]
        + [replica, position // square * replicas + replica]
    )

    def swap(value, chip_mask, core_mask):
        mask = chip_mask * replicas + core_mask
        return lax.ppermute(
            value, ("cls", "dp"), [(i, i ^ mask) for i in range(groups * replicas)]
        )

    bits = [(0, 1 << bit) for bit in range(replicas.bit_length() - 1)]
    far_bits = [(1 << bit, 0) for bit in range(2, groups.bit_length() - 1)]

    unit_feats = pl.pallas_call(
        normalize_kernel,
        out_shape=jax.ShapeDtypeStruct((local_rows + extra, width), jnp.bfloat16),
        in_specs=[hbm_spec] * 2,
        out_specs=vmem_spec,
        scratch_shapes=[
            pltpu.VMEM((local_rows, width), jnp.bfloat16),
            pltpu.VMEM((1, local_rows), jnp.int32),
            pltpu.SemaphoreType.DMA((2,)),
        ],
        compiler_params=params(10240),
        name="normalize",
    )(features, labels.reshape(1, local_rows))
    low_rows, chosen = pl.pallas_call(
        choose_kernel,
        out_shape=[
            jax.ShapeDtypeStruct((part + extra, width), jnp.bfloat16),
            jax.ShapeDtypeStruct((part, width), jnp.float32),
        ],
        in_specs=[smem_spec, hbm_spec, hbm_spec],
        out_specs=[vmem_spec] * 2,
        scratch_shapes=[pltpu.SMEM((classes,), jnp.int32), pltpu.SemaphoreType.DMA((2,))],
        compiler_params=params(11264),
        name="choose",
    )(place, sampled, weights)
    def spread(block):
        near = [block]
        for _, bit in bits:
            near = near + [swap(value, 0, bit) for value in near]
        return near

    tie = lax.optimization_barrier
    own = spread(unit_feats)
    low_rows, own = tie((low_rows, own))
    top = groups // 2
    high, low = {top: swap(unit_feats, top, 0)}, {0: unit_feats}
    for bit, _ in far_bits[:-1]:
        low.update({mask | bit: swap(block, bit, 0) for mask, block in list(low.items())})
    rows = [low_rows] + [swap(low_rows, side, 0) for side in range(1, square)]
    for bit, _ in far_bits[:-1]:
        high.update({mask | bit: swap(block, bit, 0) for mask, block in list(high.items())})
    rows = tie(rows[::-1])[::-1]
    high, rows = tie((high, rows))
    far = {mask: spread(block) for mask, block in [*low.items(), *high.items()]} | {0: own}
    blocks = [block for mask in range(0, groups, square) for block in far[mask]]
    count = len(blocks)
    early = tuple(
        index
        for index in range(count)
        if index < replicas or (index % replicas == 0 and index // replicas > 1)
    )
    spans = [early, tuple(index for index in range(count) if index not in early)]
    chunks, carried = [], rows
    for joined, span in enumerate(spans):
        shapes = [
            jax.ShapeDtypeStruct((square * part, len(span) * local_rows), jnp.float32),
            jax.ShapeDtypeStruct((2 * count, local_rows), jnp.float32),
            jax.ShapeDtypeStruct((len(span) * local_rows, width), jnp.bfloat16),
            jax.ShapeDtypeStruct((len(span), local_rows), jnp.int32),
            jax.ShapeDtypeStruct((square * part, width), jnp.bfloat16),
        ][: 5 - joined]
        exps, stats, every, marks, *together = pl.pallas_call(
            functools.partial(logits_kernel, count, span, joined),
            out_shape=shapes,
            in_specs=[smem_spec] + [vmem_spec] * (len(span) + len(carried)),
            out_specs=[vmem_spec] * len(shapes),
            compiler_params=params(16 * 1024),
            name="logits",
        )(place, *[blocks[index] for index in span], *carried)
        chunks, carried = chunks + [exps, every, marks], together + [stats]
    near = [(0, 0)]
    for chip_bit, core_bit in bits[:1] + far_bits[:1]:
        near = near + [(chip_mask | chip_bit, core_mask | core_bit) for chip_mask, core_mask in near]
    stats = sum((swap(stats, *masks) for masks in near[1:]), stats)
    for chip_mask, core_mask in bits[1:] + far_bits[1:]:
        stats = stats + swap(stats, chip_mask, core_mask)

    def grads(sides):
        kinds = [jnp.bfloat16 if side else jnp.float32 for side in sides]
        shapes = [jax.ShapeDtypeStruct((part, width), kind) for kind in kinds]
        if 0 in sides:
            shapes.append(jax.ShapeDtypeStruct((1, local_rows), jnp.float32))
        return pl.pallas_call(
            functools.partial(grads_kernel, count, replicas, spans, sides),
            out_shape=shapes,
            in_specs=[smem_spec] + [vmem_spec] * (1 + len(chunks)),
            out_specs=[vmem_spec] * len(shapes),
            scratch_shapes=[
                pltpu.VMEM((len(sides) * part, len(span) * local_rows), jnp.bfloat16)
                for span in spans
            ],
            compiler_params=params(16 * 1024),
            name="grads",
        )(place, stats, *chunks)

    away = [swap(block, side, 0) for side, block in enumerate(grads((1, 2, 3)), 1)]
    mine, loss = grads((0,))
    weight_grad = pl.pallas_call(
        finish_kernel,
        out_shape=jax.ShapeDtypeStruct((part, width), jnp.float32),
        in_specs=[vmem_spec] * (2 + len(away)),
        out_specs=vmem_spec,
        compiler_params=params(56 * 1024),
        name="finish",
    )(chosen, mine, *away)
    return (loss.reshape(local_rows), weight_grad)


def solution(mesh):
    in_specs = (P(("cls", "dp"), None), P(("cls", "dp")), P("cls", None), P("cls"))
    out_specs = (P(("cls", "dp")), P(("cls", "dp"), None))
    return jax.shard_map(
        per_device, mesh=mesh, in_specs=in_specs, out_specs=out_specs, check_vma=False
    )
```

```python
import functools

import jax
import jax.numpy as jnp
from jax import lax
from jax.experimental import pallas as pl
from jax.experimental.pallas import tpu as pltpu
from jax.sharding import PartitionSpec as P

logit_scale = 64.0
margin = 0.35
epsilon = 1e-06
digit = 256
extra = 8
square = 4

vmem_spec = pl.BlockSpec(memory_space=pltpu.VMEM)
smem_spec = pl.BlockSpec(memory_space=pltpu.SMEM)
hbm_spec = pl.BlockSpec(memory_space=pltpu.HBM)


vmem_bytes = 64 * 1024 * 1024


def params(room):
    return pltpu.CompilerParams(vmem_limit_bytes=vmem_bytes - room * 1024)


def normalized(feat_ref):
    wide = feat_ref[...].astype(jnp.float32)
    squares = jnp.sum(wide * wide, axis=1, keepdims=True)
    return (wide * lax.rsqrt(squares + epsilon)).astype(jnp.bfloat16)


def normalize_kernel(*refs):
    rows = refs[0].shape[0]
    for index, feat_ref in enumerate(refs[:-1]):
        refs[-1][index * rows : (index + 1) * rows, :] = normalized(feat_ref)


def pack_kernel(feat_ref, label_ref, out_ref):
    rows, width = feat_ref.shape
    sets = label_ref.shape[0]
    out_ref[:rows, :] = normalized(feat_ref)
    labels = label_ref[...]
    digits = [labels // digit, labels % digit]
    line = lax.broadcasted_iota(jnp.int32, (extra, width), 0)
    packed = jnp.zeros((extra, width), jnp.float32)
    per_row = width // (2 * rows)
    for first in range(0, sets, per_row):
        pieces = [
            part[index : index + 1, :]
            for index in range(first, min(first + per_row, sets))
            for part in digits
        ]
        if len(pieces) * rows < width:
            pieces.append(jnp.zeros((1, width - len(pieces) * rows), jnp.int32))
        row = jnp.concatenate(pieces, axis=1).astype(jnp.float32)
        packed = jnp.where(line == first // per_row, row, packed)
    out_ref[rows:, :] = packed.astype(jnp.bfloat16)


def labels_of(packed_ref, index):
    rows = packed_ref.shape[0] - extra
    per_row = packed_ref.shape[1] // (2 * rows)
    line, start = index // per_row, index % per_row * 2 * rows
    digits = packed_ref[rows:, :].astype(jnp.float32)[line : line + 1, :].astype(jnp.int32)
    return digits[:, start : start + rows] * digit + digits[:, start + rows : start + 2 * rows]


def choose_kernel(place_ref, sampled_hbm, weight_hbm, low_ref, chosen_ref, sampled_ref, sems):
    part = chosen_ref.shape[0]
    first = place_ref[square] * part
    copy = pltpu.make_async_copy(sampled_hbm, sampled_ref, sems.at[0])
    copy.start()
    copy.wait()

    def start_row(row, carry):
        pltpu.make_async_copy(
            weight_hbm.at[pl.ds(sampled_ref[first + row], 1), :],
            chosen_ref.at[pl.ds(row, 1), :],
            sems.at[1],
        ).start()
        return carry

    lax.fori_loop(0, part, start_row, 0, unroll=32)
    pltpu.make_async_copy(weight_hbm.at[pl.ds(0, part), :], chosen_ref, sems.at[1]).wait()
    rows = chosen_ref[...]
    inverse = lax.rsqrt(jnp.sum(rows * rows, axis=1, keepdims=True) + epsilon)
    low_ref[:part, :] = (rows * inverse).astype(jnp.bfloat16) * logit_scale
    low_ref[part:, :] = jnp.zeros_like(low_ref[part:, :])


def logits_kernel(count, span, held, joined, place_ref, *refs):
    feats = refs[:held]
    if joined:
        rows, earlier_ref = refs[held : held + 2]
        exp_ref, stat_ref, every_ref, label_ref = refs[-4:]
        stat_ref[...] = earlier_ref[...]
    else:
        classes = refs[held : held + square]
        exp_ref, stat_ref, every_ref, label_ref, rows = refs[-5:]
        part = rows.shape[0] // square
        for side in range(square):
            rows[side * part : (side + 1) * part, :] = classes[side][:part, :]
    part = rows.shape[0] // square
    lanes = label_ref.shape[1]
    for index, (_, place, first, source, label_set) in enumerate(span):
        every_ref[index * lanes : (index + 1) * lanes, :] = feats[place][first : first + lanes, :]
        label_ref[index : index + 1, :] = labels_of(feats[source], label_set)
    line = lax.broadcasted_iota(jnp.int32, (part, lanes), 0)
    for pair in range(0, len(span), 2):
        scaled = lax.dot_general(
            rows[...],
            every_ref[pair * lanes : (pair + 2) * lanes, :],
            (((1,), (1,)), ((), ())),
            preferred_element_type=jnp.float32,
        )
        for index in (pair, pair + 1):
            start = (index - pair) * lanes
            labels = label_ref[index : index + 1, :]
            total = jnp.zeros((1, lanes), jnp.float32)
            target = jnp.zeros((1, lanes), jnp.float32)
            for side in range(square):
                lines = slice(side * part, (side + 1) * part)
                hit = labels - place_ref[side] == line
                tile = scaled[lines, start : start + lanes]
                exps = jnp.exp(
                    tile - jnp.where(hit, logit_scale + logit_scale * margin, logit_scale)
                )
                exp_ref[lines, index * lanes : (index + 1) * lanes] = exps
                total = total + jnp.sum(exps, axis=0, keepdims=True)
                target = target + jnp.sum(jnp.where(hit, tile, 0.0), axis=0, keepdims=True)
            group = place_ref[square + 1] ^ span[index][0]
            stat_ref[pl.ds(group, 1), :] = total
            stat_ref[pl.ds(count + group, 1), :] = target


def grads_kernel(count, replicas, spans, sides, place_ref, stat_ref, *refs):
    chunks = [refs[3 * index : 3 * index + 3] for index in range(len(spans))]
    refs = refs[3 * len(spans) :]
    outs, scratch = refs[: len(sides)], refs[-len(spans) :]
    part = chunks[0][0].shape[0] // square
    lanes = stat_ref.shape[1]
    scale = logit_scale / replicas
    group = place_ref[square + 1]
    if 0 in sides:
        refs[len(sides)][...] = (
            logit_scale
            + jnp.log(stat_ref[pl.ds(group, 1), :])
            - (stat_ref[pl.ds(count + group, 1), :] - logit_scale * margin)
        )
    line = lax.broadcasted_iota(jnp.int32, (part, lanes), 0)
    total = None
    for span, (exp_ref, every_ref, label_ref), grads in zip(spans, chunks, scratch):
        for index in range(len(span)):
            inverse = 1.0 / stat_ref[pl.ds(group ^ span[index][0], 1), :]
            columns = slice(index * lanes, (index + 1) * lanes)
            labels = label_ref[index : index + 1, :]
            for place, side in enumerate(sides):
                hit = labels - place_ref[side] == line
                exps = exp_ref[side * part : (side + 1) * part, columns]
                grads[place * part : (place + 1) * part, columns] = (
                    exps * inverse - jnp.where(hit, 1.0, 0.0)
                ).astype(jnp.bfloat16)
        product = jnp.dot(grads[...], every_ref[...], preferred_element_type=jnp.float32)
        total = product if total is None else total + product
    for index, out in enumerate(outs):
        out[...] = (total[index * part : (index + 1) * part, :] * scale).astype(out.dtype)


def finish_kernel(chosen_ref, own_ref, *refs):
    others, out_ref = refs[:-1], refs[-1]
    summed = own_ref[...]
    for other in others:
        summed = summed + other[...].astype(jnp.float32)
    rows = chosen_ref[...]
    inverse = lax.rsqrt(jnp.sum(rows * rows, axis=1, keepdims=True) + epsilon)
    unit = rows * inverse
    radial = jnp.sum(unit * summed, axis=1, keepdims=True)
    out_ref[...] = inverse * (summed - unit * radial)


def per_device(features, labels, weights, sampled):
    groups = lax.axis_size("cls")
    replicas = lax.axis_size("dp")
    local_rows, width = features.shape
    classes = sampled.shape[0]
    part = classes // replicas
    position = lax.axis_index("cls").astype(jnp.int32)
    replica = lax.axis_index("dp").astype(jnp.int32)
    place = jnp.stack(
        [(position ^ side) * classes + replica * part for side in range(square)]
        + [replica, position // square * replicas + replica]
    )

    def swap(value, chip_mask, core_mask):
        mask = chip_mask * replicas + core_mask
        return lax.ppermute(
            value, ("cls", "dp"), [(i, i ^ mask) for i in range(groups * replicas)]
        )

    bits = [(0, 1 << bit) for bit in range(replicas.bit_length() - 1)]
    far_bits = [(1 << bit, 0) for bit in range(2, groups.bit_length() - 1)]

    upper, marks = {0: features}, labels.reshape(1, local_rows)
    for bit, _ in far_bits[1:]:
        upper.update({mask | bit: swap(block, bit, 0) for mask, block in list(upper.items())})
        marks = jnp.concatenate([marks, swap(marks, bit, 0)], axis=0)
    near_raw = swap(features, square, 0)
    low_rows, chosen = pl.pallas_call(
        choose_kernel,
        out_shape=[
            jax.ShapeDtypeStruct((part + extra, width), jnp.bfloat16),
            jax.ShapeDtypeStruct((part, width), jnp.float32),
        ],
        in_specs=[smem_spec, hbm_spec, hbm_spec],
        out_specs=[vmem_spec] * 2,
        scratch_shapes=[pltpu.SMEM((classes,), jnp.int32), pltpu.SemaphoreType.DMA((2,))],
        compiler_params=params(11264),
        name="choose",
    )(place, sampled, weights)
    def spread(block):
        near = [block]
        for _, bit in bits:
            near = near + [swap(value, 0, bit) for value in near]
        return near

    tie = lax.optimization_barrier
    low_rows, marks = tie((low_rows, marks))
    rows = [low_rows] + [swap(low_rows, side, 0) for side in range(1, square)]
    tied, near_raw = tie(({mask: block for mask, block in upper.items() if mask}, near_raw))
    upper.update(tied)
    packed = {
        mask: pl.pallas_call(
            pack_kernel,
            out_shape=jax.ShapeDtypeStruct((local_rows + extra, width), jnp.bfloat16),
            in_specs=[vmem_spec] * 2,
            out_specs=vmem_spec,
            compiler_params=params(56 * 1024),
            name="pack",
        )(block, marks)
        for mask, block in upper.items()
        if mask
    }
    pair = pl.pallas_call(
        normalize_kernel,
        out_shape=jax.ShapeDtypeStruct((2 * local_rows, width), jnp.bfloat16),
        in_specs=[vmem_spec] * 2,
        out_specs=vmem_spec,
        compiler_params=params(56 * 1024),
        name="normalize",
    )(features, near_raw)
    passed = {mask | square: swap(block, square, 0) for mask, block in packed.items()}
    rows = tie(rows[::-1])[::-1]
    passed, rows, pair = tie((passed, rows, pair))
    ups = list(packed)
    held = [pair, *packed.values(), *passed.values()]
    spread_out = [spread(array) for array in held]
    count = groups // square * replicas
    order = list(upper)

    def entry(index, first_replica):
        mask, replica_bit = index // replicas * square, index % replicas
        up, beside = mask & ~square, bool(mask & square)
        base = (replica_bit - first_replica) * len(held) + 1 + beside * len(ups)
        source = base + ups.index(groups // 2)
        if up:
            return (index, base + ups.index(up), 0, source, order.index(up))
        return (index, base - 1 - beside * len(ups), beside * local_rows, source, 0)

    spans, arrays = [], []
    for some in (range(1), range(1, replicas)):
        spans.append(
            tuple(entry(index, some[0]) for index in range(count) if index % replicas in some)
        )
        arrays.append([copies[bit] for bit in some for copies in spread_out])
    chunks, carried = [], rows
    for joined, span in enumerate(spans):
        shapes = [
            jax.ShapeDtypeStruct((square * part, len(span) * local_rows), jnp.float32),
            jax.ShapeDtypeStruct((2 * count, local_rows), jnp.float32),
            jax.ShapeDtypeStruct((len(span) * local_rows, width), jnp.bfloat16),
            jax.ShapeDtypeStruct((len(span), local_rows), jnp.int32),
            jax.ShapeDtypeStruct((square * part, width), jnp.bfloat16),
        ][: 5 - joined]
        exps, stats, every, marks, *together = pl.pallas_call(
            functools.partial(logits_kernel, count, span, len(arrays[joined]), joined),
            out_shape=shapes,
            in_specs=[smem_spec] + [vmem_spec] * (len(arrays[joined]) + len(carried)),
            out_specs=[vmem_spec] * len(shapes),
            compiler_params=params(16 * 1024),
            name="logits",
        )(place, *arrays[joined], *carried)
        chunks, carried = chunks + [exps, every, marks], together + [stats]
    near = [(0, 0)]
    for chip_bit, core_bit in bits[:1] + far_bits[:1]:
        near = near + [(chip_mask | chip_bit, core_mask | core_bit) for chip_mask, core_mask in near]
    stats = sum((swap(stats, *masks) for masks in near[1:]), stats)
    for chip_mask, core_mask in bits[1:] + far_bits[1:]:
        stats = stats + swap(stats, chip_mask, core_mask)

    def grads(sides):
        kinds = [jnp.bfloat16 if side else jnp.float32 for side in sides]
        shapes = [jax.ShapeDtypeStruct((part, width), kind) for kind in kinds]
        if 0 in sides:
            shapes.append(jax.ShapeDtypeStruct((1, local_rows), jnp.float32))
        return pl.pallas_call(
            functools.partial(grads_kernel, count, replicas, spans, sides),
            out_shape=shapes,
            in_specs=[smem_spec] + [vmem_spec] * (1 + len(chunks)),
            out_specs=[vmem_spec] * len(shapes),
            scratch_shapes=[
                pltpu.VMEM((len(sides) * part, len(span) * local_rows), jnp.bfloat16)
                for span in spans
            ],
            compiler_params=params(16 * 1024),
            name="grads",
        )(place, stats, *chunks)

    away = [swap(block, side, 0) for side, block in enumerate(grads((1, 2, 3)), 1)]
    mine, loss = grads((0,))
    weight_grad = pl.pallas_call(
        finish_kernel,
        out_shape=jax.ShapeDtypeStruct((part, width), jnp.float32),
        in_specs=[vmem_spec] * (2 + len(away)),
        out_specs=vmem_spec,
        compiler_params=params(56 * 1024),
        name="finish",
    )(chosen, mine, *away)
    return (loss.reshape(local_rows), weight_grad)


def solution(mesh):
    in_specs = (P(("cls", "dp"), None), P(("cls", "dp")), P("cls", None), P("cls"))
    out_specs = (P(("cls", "dp")), P(("cls", "dp"), None))
    return jax.shard_map(
        per_device, mesh=mesh, in_specs=in_specs, out_specs=out_specs, check_vma=False
    )
```

```python
import functools

import jax
import jax.numpy as jnp
from jax import lax
from jax.experimental import pallas as pl
from jax.experimental.pallas import tpu as pltpu
from jax.sharding import PartitionSpec as P

logit_scale = 64.0
margin = 0.35
epsilon = 1e-06
digit = 256
extra = 8
square = 4

vmem_spec = pl.BlockSpec(memory_space=pltpu.VMEM)
smem_spec = pl.BlockSpec(memory_space=pltpu.SMEM)
hbm_spec = pl.BlockSpec(memory_space=pltpu.HBM)


vmem_bytes = 64 * 1024 * 1024


def params(room):
    return pltpu.CompilerParams(vmem_limit_bytes=vmem_bytes - room * 1024)


def normalized(feat_ref):
    wide = feat_ref[...].astype(jnp.float32)
    squares = jnp.sum(wide * wide, axis=1, keepdims=True)
    return (wide * lax.rsqrt(squares + epsilon)).astype(jnp.bfloat16)


def normalize_kernel(*refs):
    rows = refs[0].shape[0]
    for index, feat_ref in enumerate(refs[:-1]):
        refs[-1][index * rows : (index + 1) * rows, :] = normalized(feat_ref)


def pack_kernel(feat_ref, label_ref, out_ref):
    rows, width = feat_ref.shape
    sets = label_ref.shape[0]
    out_ref[:rows, :] = normalized(feat_ref)
    labels = label_ref[...]
    digits = [labels // digit, labels % digit]
    line = lax.broadcasted_iota(jnp.int32, (extra, width), 0)
    packed = jnp.zeros((extra, width), jnp.float32)
    per_row = width // (2 * rows)
    for first in range(0, sets, per_row):
        pieces = [
            part[index : index + 1, :]
            for index in range(first, min(first + per_row, sets))
            for part in digits
        ]
        if len(pieces) * rows < width:
            pieces.append(jnp.zeros((1, width - len(pieces) * rows), jnp.int32))
        row = jnp.concatenate(pieces, axis=1).astype(jnp.float32)
        packed = jnp.where(line == first // per_row, row, packed)
    out_ref[rows:, :] = packed.astype(jnp.bfloat16)


def labels_of(packed_ref, index):
    rows = packed_ref.shape[0] - extra
    per_row = packed_ref.shape[1] // (2 * rows)
    line, start = index // per_row, index % per_row * 2 * rows
    digits = packed_ref[rows:, :].astype(jnp.float32)[line : line + 1, :].astype(jnp.int32)
    return digits[:, start : start + rows] * digit + digits[:, start + rows : start + 2 * rows]


def choose_kernel(place_ref, sampled_hbm, weight_hbm, low_ref, chosen_ref, sampled_ref, sems):
    part = chosen_ref.shape[0]
    first = place_ref[square] * part
    copy = pltpu.make_async_copy(sampled_hbm, sampled_ref, sems.at[0])
    copy.start()
    copy.wait()

    def start_row(row, carry):
        pltpu.make_async_copy(
            weight_hbm.at[pl.ds(sampled_ref[first + row], 1), :],
            chosen_ref.at[pl.ds(row, 1), :],
            sems.at[1],
        ).start()
        return carry

    lax.fori_loop(0, part, start_row, 0, unroll=32)
    pltpu.make_async_copy(weight_hbm.at[pl.ds(0, part), :], chosen_ref, sems.at[1]).wait()
    rows = chosen_ref[...]
    inverse = lax.rsqrt(jnp.sum(rows * rows, axis=1, keepdims=True) + epsilon)
    low_ref[:part, :] = (rows * inverse).astype(jnp.bfloat16) * logit_scale
    low_ref[part:, :] = jnp.zeros_like(low_ref[part:, :])


def logits_kernel(count, span, held, joined, place_ref, *refs):
    feats = refs[:held]
    if joined:
        rows, earlier_ref = refs[held : held + 2]
        exp_ref, stat_ref, every_ref, label_ref = refs[-4:]
        stat_ref[...] = earlier_ref[...]
    else:
        classes = refs[held : held + square]
        exp_ref, stat_ref, every_ref, label_ref, rows = refs[-5:]
        part = rows.shape[0] // square
        for side in range(square):
            rows[side * part : (side + 1) * part, :] = classes[side][:part, :]
    part = rows.shape[0] // square
    lanes = label_ref.shape[1]
    for index, (_, place, first, source, label_set) in enumerate(span):
        every_ref[index * lanes : (index + 1) * lanes, :] = feats[place][first : first + lanes, :]
        label_ref[index : index + 1, :] = labels_of(feats[source], label_set)
    line = lax.broadcasted_iota(jnp.int32, (part, lanes), 0)
    for pair in range(0, len(span), 2):
        scaled = lax.dot_general(
            rows[...],
            every_ref[pair * lanes : (pair + 2) * lanes, :],
            (((1,), (1,)), ((), ())),
            preferred_element_type=jnp.float32,
        )
        for index in (pair, pair + 1):
            start = (index - pair) * lanes
            labels = label_ref[index : index + 1, :]
            total = jnp.zeros((1, lanes), jnp.float32)
            target = jnp.zeros((1, lanes), jnp.float32)
            for side in range(square):
                lines = slice(side * part, (side + 1) * part)
                hit = labels - place_ref[side] == line
                tile = scaled[lines, start : start + lanes]
                exps = jnp.exp(
                    tile - jnp.where(hit, logit_scale + logit_scale * margin, logit_scale)
                )
                exp_ref[lines, index * lanes : (index + 1) * lanes] = exps
                total = total + jnp.sum(exps, axis=0, keepdims=True)
                target = target + jnp.sum(jnp.where(hit, tile, 0.0), axis=0, keepdims=True)
            group = place_ref[square + 1] ^ span[index][0]
            stat_ref[pl.ds(group, 1), :] = total
            stat_ref[pl.ds(count + group, 1), :] = target


def grads_kernel(count, replicas, spans, sides, place_ref, stat_ref, *refs):
    chunks = [refs[3 * index : 3 * index + 3] for index in range(len(spans))]
    refs = refs[3 * len(spans) :]
    outs, scratch = refs[: len(sides)], refs[-len(spans) :]
    part = chunks[0][0].shape[0] // square
    lanes = stat_ref.shape[1]
    scale = logit_scale / replicas
    group = place_ref[square + 1]
    if 0 in sides:
        refs[len(sides)][...] = (
            logit_scale
            + jnp.log(stat_ref[pl.ds(group, 1), :])
            - (stat_ref[pl.ds(count + group, 1), :] - logit_scale * margin)
        )
    line = lax.broadcasted_iota(jnp.int32, (part, lanes), 0)
    total = None
    for span, (exp_ref, every_ref, label_ref), grads in zip(spans, chunks, scratch):
        for index in range(len(span)):
            inverse = 1.0 / stat_ref[pl.ds(group ^ span[index][0], 1), :]
            columns = slice(index * lanes, (index + 1) * lanes)
            labels = label_ref[index : index + 1, :]
            for place, side in enumerate(sides):
                hit = labels - place_ref[side] == line
                exps = exp_ref[side * part : (side + 1) * part, columns]
                grads[place * part : (place + 1) * part, columns] = (
                    exps * inverse - jnp.where(hit, 1.0, 0.0)
                ).astype(jnp.bfloat16)
        product = jnp.dot(grads[...], every_ref[...], preferred_element_type=jnp.float32)
        total = product if total is None else total + product
    for index, out in enumerate(outs):
        out[...] = (total[index * part : (index + 1) * part, :] * scale).astype(out.dtype)


def finish_kernel(chosen_ref, own_ref, *refs):
    others, out_ref = refs[:-1], refs[-1]
    summed = own_ref[...]
    for other in others:
        summed = summed + other[...].astype(jnp.float32)
    rows = chosen_ref[...]
    inverse = lax.rsqrt(jnp.sum(rows * rows, axis=1, keepdims=True) + epsilon)
    unit = rows * inverse
    radial = jnp.sum(unit * summed, axis=1, keepdims=True)
    out_ref[...] = inverse * (summed - unit * radial)


def per_device(features, labels, weights, sampled):
    groups = lax.axis_size("cls")
    replicas = lax.axis_size("dp")
    local_rows, width = features.shape
    classes = sampled.shape[0]
    part = classes // replicas
    position = lax.axis_index("cls").astype(jnp.int32)
    replica = lax.axis_index("dp").astype(jnp.int32)
    place = jnp.stack(
        [(position ^ side) * classes + replica * part for side in range(square)]
        + [replica, position // square * replicas + replica]
    )

    def swap(value, chip_mask, core_mask):
        mask = chip_mask * replicas + core_mask
        return lax.ppermute(
            value, ("cls", "dp"), [(i, i ^ mask) for i in range(groups * replicas)]
        )

    bits = [(0, 1 << bit) for bit in range(replicas.bit_length() - 1)]
    far_bits = [(1 << bit, 0) for bit in range(2, groups.bit_length() - 1)]

    upper, marks = {0: features}, labels.reshape(1, local_rows)
    for bit, _ in far_bits[1:]:
        upper.update({mask | bit: swap(block, bit, 0) for mask, block in list(upper.items())})
        marks = jnp.concatenate([marks, swap(marks, bit, 0)], axis=0)
    near_raw = swap(features, square, 0)
    low_rows, chosen = pl.pallas_call(
        choose_kernel,
        out_shape=[
            jax.ShapeDtypeStruct((part + extra, width), jnp.bfloat16),
            jax.ShapeDtypeStruct((part, width), jnp.float32),
        ],
        in_specs=[smem_spec, hbm_spec, hbm_spec],
        out_specs=[vmem_spec] * 2,
        scratch_shapes=[pltpu.SMEM((classes,), jnp.int32), pltpu.SemaphoreType.DMA((2,))],
        compiler_params=params(11264),
        name="choose",
    )(place, sampled, weights)
    def spread(block):
        near = [block]
        for _, bit in bits:
            near = near + [swap(value, 0, bit) for value in near]
        return near

    tie = lax.optimization_barrier
    corner_rows, marks = tie((low_rows, marks))
    rows = [low_rows, swap(low_rows, 1, 0), swap(low_rows, 2, 0), swap(corner_rows, 3, 0)]
    tied, near_raw = tie(({mask: block for mask, block in upper.items() if mask}, near_raw))
    upper.update(tied)
    packed = {
        mask: pl.pallas_call(
            pack_kernel,
            out_shape=jax.ShapeDtypeStruct((local_rows + extra, width), jnp.bfloat16),
            in_specs=[vmem_spec] * 2,
            out_specs=vmem_spec,
            compiler_params=params(56 * 1024),
            name="pack",
        )(block, marks)
        for mask, block in upper.items()
        if mask
    }
    pair = pl.pallas_call(
        normalize_kernel,
        out_shape=jax.ShapeDtypeStruct((2 * local_rows, width), jnp.bfloat16),
        in_specs=[vmem_spec] * 2,
        out_specs=vmem_spec,
        compiler_params=params(56 * 1024),
        name="normalize",
    )(features, near_raw)
    passed = {mask | square: swap(block, square, 0) for mask, block in packed.items()}
    rows = tie(rows[::-1])[::-1]
    passed, rows, pair = tie((passed, rows, pair))
    ups = list(packed)
    held = [pair, *packed.values(), *passed.values()]
    spread_out = [spread(array) for array in held]
    count = groups // square * replicas
    order = list(upper)

    def entry(index, first_replica):
        mask, replica_bit = index // replicas * square, index % replicas
        up, beside = mask & ~square, bool(mask & square)
        base = (replica_bit - first_replica) * len(held) + 1 + beside * len(ups)
        source = base + ups.index(groups // 2)
        if up:
            return (index, base + ups.index(up), 0, source, order.index(up))
        return (index, base - 1 - beside * len(ups), beside * local_rows, source, 0)

    spans, arrays = [], []
    for some in (range(1), range(1, replicas)):
        spans.append(
            tuple(entry(index, some[0]) for index in range(count) if index % replicas in some)
        )
        arrays.append([copies[bit] for bit in some for copies in spread_out])
    chunks, carried = [], rows
    for joined, span in enumerate(spans):
        shapes = [
            jax.ShapeDtypeStruct((square * part, len(span) * local_rows), jnp.float32),
            jax.ShapeDtypeStruct((2 * count, local_rows), jnp.float32),
            jax.ShapeDtypeStruct((len(span) * local_rows, width), jnp.bfloat16),
            jax.ShapeDtypeStruct((len(span), local_rows), jnp.int32),
            jax.ShapeDtypeStruct((square * part, width), jnp.bfloat16),
        ][: 5 - joined]
        exps, stats, every, marks, *together = pl.pallas_call(
            functools.partial(logits_kernel, count, span, len(arrays[joined]), joined),
            out_shape=shapes,
            in_specs=[smem_spec] + [vmem_spec] * (len(arrays[joined]) + len(carried)),
            out_specs=[vmem_spec] * len(shapes),
            compiler_params=params(16 * 1024),
            name="logits",
        )(place, *arrays[joined], *carried)
        chunks, carried = chunks + [exps, every, marks], together + [stats]
    near = [(0, 0)]
    for chip_bit, core_bit in bits[:1] + far_bits[:1]:
        near = near + [(chip_mask | chip_bit, core_mask | core_bit) for chip_mask, core_mask in near]
    stats = sum((swap(stats, *masks) for masks in near[1:]), stats)
    for chip_mask, core_mask in bits[1:] + far_bits[1:]:
        stats = stats + swap(stats, chip_mask, core_mask)

    def grads(sides):
        kinds = [jnp.bfloat16 if side else jnp.float32 for side in sides]
        shapes = [jax.ShapeDtypeStruct((part, width), kind) for kind in kinds]
        if 0 in sides:
            shapes.append(jax.ShapeDtypeStruct((1, local_rows), jnp.float32))
        return pl.pallas_call(
            functools.partial(grads_kernel, count, replicas, spans, sides),
            out_shape=shapes,
            in_specs=[smem_spec] + [vmem_spec] * (1 + len(chunks)),
            out_specs=[vmem_spec] * len(shapes),
            scratch_shapes=[
                pltpu.VMEM((len(sides) * part, len(span) * local_rows), jnp.bfloat16)
                for span in spans
            ],
            compiler_params=params(16 * 1024),
            name="grads",
        )(place, stats, *chunks)

    away = [swap(block, side, 0) for side, block in enumerate(grads((1, 2, 3)), 1)]
    mine, loss = grads((0,))
    weight_grad = pl.pallas_call(
        finish_kernel,
        out_shape=jax.ShapeDtypeStruct((part, width), jnp.float32),
        in_specs=[vmem_spec] * (2 + len(away)),
        out_specs=vmem_spec,
        compiler_params=params(56 * 1024),
        name="finish",
    )(chosen, mine, *away)
    return (loss.reshape(local_rows), weight_grad)


def solution(mesh):
    in_specs = (P(("cls", "dp"), None), P(("cls", "dp")), P("cls", None), P("cls"))
    out_specs = (P(("cls", "dp")), P(("cls", "dp"), None))
    return jax.shard_map(
        per_device, mesh=mesh, in_specs=in_specs, out_specs=out_specs, check_vma=False
    )
```

```python
import functools

import jax
import jax.numpy as jnp
from jax import lax
from jax.experimental import pallas as pl
from jax.experimental.pallas import tpu as pltpu
from jax.sharding import PartitionSpec as P

logit_scale = 64.0
margin = 0.35
epsilon = 1e-06
digit = 256
extra = 8
square = 4

vmem_spec = pl.BlockSpec(memory_space=pltpu.VMEM)
smem_spec = pl.BlockSpec(memory_space=pltpu.SMEM)
hbm_spec = pl.BlockSpec(memory_space=pltpu.HBM)


vmem_bytes = 64 * 1024 * 1024


def params(room):
    return pltpu.CompilerParams(vmem_limit_bytes=vmem_bytes - room * 1024)


def normalized(feat_ref):
    wide = feat_ref[...].astype(jnp.float32)
    squares = jnp.sum(wide * wide, axis=1, keepdims=True)
    return (wide * lax.rsqrt(squares + epsilon)).astype(jnp.bfloat16)


def normalize_kernel(*refs):
    rows = refs[0].shape[0]
    for index, feat_ref in enumerate(refs[:-1]):
        refs[-1][index * rows : (index + 1) * rows, :] = normalized(feat_ref)


def pack_kernel(feat_ref, label_ref, out_ref):
    rows, width = feat_ref.shape
    sets = label_ref.shape[0]
    out_ref[:rows, :] = normalized(feat_ref)
    labels = label_ref[...]
    digits = [labels // digit, labels % digit]
    line = lax.broadcasted_iota(jnp.int32, (extra, width), 0)
    packed = jnp.zeros((extra, width), jnp.float32)
    per_row = width // (2 * rows)
    for first in range(0, sets, per_row):
        pieces = [
            part[index : index + 1, :]
            for index in range(first, min(first + per_row, sets))
            for part in digits
        ]
        if len(pieces) * rows < width:
            pieces.append(jnp.zeros((1, width - len(pieces) * rows), jnp.int32))
        row = jnp.concatenate(pieces, axis=1).astype(jnp.float32)
        packed = jnp.where(line == first // per_row, row, packed)
    out_ref[rows:, :] = packed.astype(jnp.bfloat16)


def labels_of(packed_ref, index):
    rows = packed_ref.shape[0] - extra
    per_row = packed_ref.shape[1] // (2 * rows)
    line, start = index // per_row, index % per_row * 2 * rows
    digits = packed_ref[rows:, :].astype(jnp.float32)[line : line + 1, :].astype(jnp.int32)
    return digits[:, start : start + rows] * digit + digits[:, start + rows : start + 2 * rows]


def choose_kernel(chosen_ref, low_ref):
    part = chosen_ref.shape[0]
    rows = chosen_ref[...]
    inverse = lax.rsqrt(jnp.sum(rows * rows, axis=1, keepdims=True) + epsilon)
    low_ref[:part, :] = (rows * inverse).astype(jnp.bfloat16) * logit_scale
    low_ref[part:, :] = jnp.zeros_like(low_ref[part:, :])


def logits_kernel(count, span, held, joined, place_ref, *refs):
    feats = refs[:held]
    if joined:
        rows, earlier_ref = refs[held : held + 2]
        exp_ref, stat_ref, every_ref, label_ref = refs[-4:]
        stat_ref[...] = earlier_ref[...]
    else:
        classes = refs[held : held + square]
        exp_ref, stat_ref, every_ref, label_ref, rows = refs[-5:]
        part = rows.shape[0] // square
        for side in range(square):
            rows[side * part : (side + 1) * part, :] = classes[side][:part, :]
    part = rows.shape[0] // square
    lanes = label_ref.shape[1]
    for index, (_, place, first, source, label_set) in enumerate(span):
        every_ref[index * lanes : (index + 1) * lanes, :] = feats[place][first : first + lanes, :]
        label_ref[index : index + 1, :] = labels_of(feats[source], label_set)
    line = lax.broadcasted_iota(jnp.int32, (part, lanes), 0)
    for pair in range(0, len(span), 2):
        scaled = lax.dot_general(
            rows[...],
            every_ref[pair * lanes : (pair + 2) * lanes, :],
            (((1,), (1,)), ((), ())),
            preferred_element_type=jnp.float32,
        )
        for index in (pair, pair + 1):
            start = (index - pair) * lanes
            labels = label_ref[index : index + 1, :]
            total = jnp.zeros((1, lanes), jnp.float32)
            target = jnp.zeros((1, lanes), jnp.float32)
            for side in range(square):
                lines = slice(side * part, (side + 1) * part)
                hit = labels - place_ref[side] == line
                tile = scaled[lines, start : start + lanes]
                exps = jnp.exp(
                    tile - jnp.where(hit, logit_scale + logit_scale * margin, logit_scale)
                )
                exp_ref[lines, index * lanes : (index + 1) * lanes] = exps
                total = total + jnp.sum(exps, axis=0, keepdims=True)
                target = target + jnp.sum(jnp.where(hit, tile, 0.0), axis=0, keepdims=True)
            group = place_ref[square + 1] ^ span[index][0]
            stat_ref[pl.ds(group, 1), :] = total
            stat_ref[pl.ds(count + group, 1), :] = target


def grads_kernel(count, replicas, spans, sides, place_ref, stat_ref, *refs):
    chunks = [refs[3 * index : 3 * index + 3] for index in range(len(spans))]
    refs = refs[3 * len(spans) :]
    outs, scratch = refs[: len(sides)], refs[-len(spans) :]
    part = chunks[0][0].shape[0] // square
    lanes = stat_ref.shape[1]
    scale = logit_scale / replicas
    group = place_ref[square + 1]
    if 0 in sides:
        refs[len(sides)][...] = (
            logit_scale
            + jnp.log(stat_ref[pl.ds(group, 1), :])
            - (stat_ref[pl.ds(count + group, 1), :] - logit_scale * margin)
        )
    line = lax.broadcasted_iota(jnp.int32, (part, lanes), 0)
    total = None
    for span, (exp_ref, every_ref, label_ref), grads in zip(spans, chunks, scratch):
        for index in range(len(span)):
            inverse = 1.0 / stat_ref[pl.ds(group ^ span[index][0], 1), :]
            columns = slice(index * lanes, (index + 1) * lanes)
            labels = label_ref[index : index + 1, :]
            for place, side in enumerate(sides):
                hit = labels - place_ref[side] == line
                exps = exp_ref[side * part : (side + 1) * part, columns]
                grads[place * part : (place + 1) * part, columns] = (
                    exps * inverse - jnp.where(hit, 1.0, 0.0)
                ).astype(jnp.bfloat16)
        product = jnp.dot(grads[...], every_ref[...], preferred_element_type=jnp.float32)
        total = product if total is None else total + product
    for index, out in enumerate(outs):
        out[...] = (total[index * part : (index + 1) * part, :] * scale).astype(out.dtype)


def finish_kernel(chosen_ref, own_ref, *refs):
    others, out_ref = refs[:-1], refs[-1]
    summed = own_ref[...]
    for other in others:
        summed = summed + other[...].astype(jnp.float32)
    rows = chosen_ref[...]
    inverse = lax.rsqrt(jnp.sum(rows * rows, axis=1, keepdims=True) + epsilon)
    unit = rows * inverse
    radial = jnp.sum(unit * summed, axis=1, keepdims=True)
    out_ref[...] = inverse * (summed - unit * radial)


def per_device(features, labels, weights, sampled):
    groups = lax.axis_size("cls")
    replicas = lax.axis_size("dp")
    local_rows, width = features.shape
    classes = sampled.shape[0]
    part = classes // replicas
    position = lax.axis_index("cls").astype(jnp.int32)
    replica = lax.axis_index("dp").astype(jnp.int32)
    place = jnp.stack(
        [(position ^ side) * classes + replica * part for side in range(square)]
        + [replica, position // square * replicas + replica]
    )

    def swap(value, chip_mask, core_mask):
        mask = chip_mask * replicas + core_mask
        return lax.ppermute(
            value, ("cls", "dp"), [(i, i ^ mask) for i in range(groups * replicas)]
        )

    bits = [(0, 1 << bit) for bit in range(replicas.bit_length() - 1)]
    far_bits = [(1 << bit, 0) for bit in range(2, groups.bit_length() - 1)]

    upper, marks = {0: features}, labels.reshape(1, local_rows)
    for bit, _ in far_bits[1:]:
        upper.update({mask | bit: swap(block, bit, 0) for mask, block in list(upper.items())})
        marks = jnp.concatenate([marks, swap(marks, bit, 0)], axis=0)
    near_raw = swap(features, square, 0)
    mine = lax.dynamic_slice_in_dim(sampled, replica * part, part)
    chosen = weights.at[mine].get(mode="promise_in_bounds", unique_indices=True)
    low_rows = pl.pallas_call(
        choose_kernel,
        out_shape=jax.ShapeDtypeStruct((part + extra, width), jnp.bfloat16),
        in_specs=[vmem_spec],
        out_specs=vmem_spec,
        compiler_params=params(16 * 1024),
        name="choose",
    )(chosen)
    def spread(block):
        near = [block]
        for _, bit in bits:
            near = near + [swap(value, 0, bit) for value in near]
        return near

    tie = lax.optimization_barrier
    corner_rows, marks = tie((low_rows, marks))
    rows = [low_rows, swap(low_rows, 1, 0), swap(low_rows, 2, 0), swap(corner_rows, 3, 0)]
    tied, near_raw = tie(({mask: block for mask, block in upper.items() if mask}, near_raw))
    upper.update(tied)
    packed = {
        mask: pl.pallas_call(
            pack_kernel,
            out_shape=jax.ShapeDtypeStruct((local_rows + extra, width), jnp.bfloat16),
            in_specs=[vmem_spec] * 2,
            out_specs=vmem_spec,
            compiler_params=params(56 * 1024),
            name="pack",
        )(block, marks)
        for mask, block in upper.items()
        if mask
    }
    pair = pl.pallas_call(
        normalize_kernel,
        out_shape=jax.ShapeDtypeStruct((2 * local_rows, width), jnp.bfloat16),
        in_specs=[vmem_spec] * 2,
        out_specs=vmem_spec,
        compiler_params=params(56 * 1024),
        name="normalize",
    )(features, near_raw)
    passed = {mask | square: swap(block, square, 0) for mask, block in packed.items()}
    rows = tie(rows[::-1])[::-1]
    passed, rows, pair = tie((passed, rows, pair))
    ups = list(packed)
    held = [pair, *packed.values(), *passed.values()]
    spread_out = [spread(array) for array in held]
    count = groups // square * replicas
    order = list(upper)

    def entry(index, first_replica):
        mask, replica_bit = index // replicas * square, index % replicas
        up, beside = mask & ~square, bool(mask & square)
        base = (replica_bit - first_replica) * len(held) + 1 + beside * len(ups)
        source = base + ups.index(groups // 2)
        if up:
            return (index, base + ups.index(up), 0, source, order.index(up))
        return (index, base - 1 - beside * len(ups), beside * local_rows, source, 0)

    spans, arrays = [], []
    for some in (range(1), range(1, replicas)):
        spans.append(
            tuple(entry(index, some[0]) for index in range(count) if index % replicas in some)
        )
        arrays.append([copies[bit] for bit in some for copies in spread_out])
    chunks, carried = [], rows
    for joined, span in enumerate(spans):
        shapes = [
            jax.ShapeDtypeStruct((square * part, len(span) * local_rows), jnp.float32),
            jax.ShapeDtypeStruct((2 * count, local_rows), jnp.float32),
            jax.ShapeDtypeStruct((len(span) * local_rows, width), jnp.bfloat16),
            jax.ShapeDtypeStruct((len(span), local_rows), jnp.int32),
            jax.ShapeDtypeStruct((square * part, width), jnp.bfloat16),
        ][: 5 - joined]
        exps, stats, every, marks, *together = pl.pallas_call(
            functools.partial(logits_kernel, count, span, len(arrays[joined]), joined),
            out_shape=shapes,
            in_specs=[smem_spec] + [vmem_spec] * (len(arrays[joined]) + len(carried)),
            out_specs=[vmem_spec] * len(shapes),
            compiler_params=params(16 * 1024),
            name="logits",
        )(place, *arrays[joined], *carried)
        chunks, carried = chunks + [exps, every, marks], together + [stats]
    near = [(0, 0)]
    for chip_bit, core_bit in bits[:1] + far_bits[:1]:
        near = near + [(chip_mask | chip_bit, core_mask | core_bit) for chip_mask, core_mask in near]
    stats = sum((swap(stats, *masks) for masks in near[1:]), stats)
    for chip_mask, core_mask in bits[1:] + far_bits[1:]:
        stats = stats + swap(stats, chip_mask, core_mask)

    def grads(sides):
        kinds = [jnp.bfloat16 if side else jnp.float32 for side in sides]
        shapes = [jax.ShapeDtypeStruct((part, width), kind) for kind in kinds]
        if 0 in sides:
            shapes.append(jax.ShapeDtypeStruct((1, local_rows), jnp.float32))
        return pl.pallas_call(
            functools.partial(grads_kernel, count, replicas, spans, sides),
            out_shape=shapes,
            in_specs=[smem_spec] + [vmem_spec] * (1 + len(chunks)),
            out_specs=[vmem_spec] * len(shapes),
            scratch_shapes=[
                pltpu.VMEM((len(sides) * part, len(span) * local_rows), jnp.bfloat16)
                for span in spans
            ],
            compiler_params=params(16 * 1024),
            name="grads",
        )(place, stats, *chunks)

    away = [swap(block, side, 0) for side, block in enumerate(grads((1, 2, 3)), 1)]
    own_part, loss = grads((0,))
    weight_grad = pl.pallas_call(
        finish_kernel,
        out_shape=jax.ShapeDtypeStruct((part, width), jnp.float32),
        in_specs=[vmem_spec] * (2 + len(away)),
        out_specs=vmem_spec,
        compiler_params=params(56 * 1024),
        name="finish",
    )(chosen, own_part, *away)
    return (loss.reshape(local_rows), weight_grad)


def solution(mesh):
    in_specs = (P(("cls", "dp"), None), P(("cls", "dp")), P("cls", None), P("cls"))
    out_specs = (P(("cls", "dp")), P(("cls", "dp"), None))
    return jax.shard_map(
        per_device, mesh=mesh, in_specs=in_specs, out_specs=out_specs, check_vma=False
    )
```

```python
import functools

import jax
import jax.numpy as jnp
from jax import lax
from jax.experimental import pallas as pl
from jax.experimental.pallas import tpu as pltpu
from jax.sharding import PartitionSpec as P

logit_scale = 64.0
margin = 0.35
epsilon = 1e-06
digit = 256
extra = 8
square = 4

vmem_spec = pl.BlockSpec(memory_space=pltpu.VMEM)
smem_spec = pl.BlockSpec(memory_space=pltpu.SMEM)
hbm_spec = pl.BlockSpec(memory_space=pltpu.HBM)


def params(operand_bytes=0):
    limit = min(48 * 1024 * 1024, 8 * 1024 * 1024 + 5 * operand_bytes // 4)
    return pltpu.CompilerParams(vmem_limit_bytes=limit)


def bytes_of(arrays):
    return sum(array.size * array.dtype.itemsize for array in arrays)


def normalized(feat_ref):
    wide = feat_ref[...].astype(jnp.float32)
    squares = jnp.sum(wide * wide, axis=1, keepdims=True)
    return (wide * lax.rsqrt(squares + epsilon)).astype(jnp.bfloat16)


def normalize_kernel(*refs):
    rows = refs[0].shape[0]
    for index, feat_ref in enumerate(refs[:-1]):
        refs[-1][index * rows : (index + 1) * rows, :] = normalized(feat_ref)


def pack_kernel(feat_ref, label_ref, out_ref):
    rows, width = feat_ref.shape
    sets = label_ref.shape[0]
    out_ref[:rows, :] = normalized(feat_ref)
    labels = label_ref[...]
    digits = [labels // digit, labels % digit]
    line = lax.broadcasted_iota(jnp.int32, (extra, width), 0)
    packed = jnp.zeros((extra, width), jnp.float32)
    per_row = width // (2 * rows)
    for first in range(0, sets, per_row):
        pieces = [
            part[index : index + 1, :]
            for index in range(first, min(first + per_row, sets))
            for part in digits
        ]
        if len(pieces) * rows < width:
            pieces.append(jnp.zeros((1, width - len(pieces) * rows), jnp.int32))
        row = jnp.concatenate(pieces, axis=1).astype(jnp.float32)
        packed = jnp.where(line == first // per_row, row, packed)
    out_ref[rows:, :] = packed.astype(jnp.bfloat16)


def labels_of(packed_ref, index):
    rows = packed_ref.shape[0] - extra
    per_row = packed_ref.shape[1] // (2 * rows)
    line, start = index // per_row, index % per_row * 2 * rows
    digits = packed_ref[rows:, :].astype(jnp.float32)[line : line + 1, :].astype(jnp.int32)
    return digits[:, start : start + rows] * digit + digits[:, start + rows : start + 2 * rows]


def choose_kernel(chosen_ref, low_ref):
    part = chosen_ref.shape[0]
    rows = chosen_ref[...]
    inverse = lax.rsqrt(jnp.sum(rows * rows, axis=1, keepdims=True) + epsilon)
    low_ref[:part, :] = (rows * inverse).astype(jnp.bfloat16) * logit_scale
    low_ref[part:, :] = jnp.zeros_like(low_ref[part:, :])


def logits_kernel(count, span, held, joined, place_ref, *refs):
    feats = refs[:held]
    if joined:
        rows, earlier_ref = refs[held : held + 2]
        exp_ref, stat_ref, every_ref, label_ref = refs[-4:]
        stat_ref[...] = earlier_ref[...]
    else:
        classes = refs[held : held + square]
        exp_ref, stat_ref, every_ref, label_ref, rows = refs[-5:]
        part = rows.shape[0] // square
        for side in range(square):
            rows[side * part : (side + 1) * part, :] = classes[side][:part, :]
    part = rows.shape[0] // square
    lanes = label_ref.shape[1]
    for index, (_, place, first, source, label_set) in enumerate(span):
        every_ref[index * lanes : (index + 1) * lanes, :] = feats[place][first : first + lanes, :]
        label_ref[index : index + 1, :] = labels_of(feats[source], label_set)
    line = lax.broadcasted_iota(jnp.int32, (part, lanes), 0)
    for pair in range(0, len(span), 2):
        scaled = lax.dot_general(
            rows[...],
            every_ref[pair * lanes : (pair + 2) * lanes, :],
            (((1,), (1,)), ((), ())),
            preferred_element_type=jnp.float32,
        )
        for index in (pair, pair + 1):
            start = (index - pair) * lanes
            labels = label_ref[index : index + 1, :]
            total = jnp.zeros((1, lanes), jnp.float32)
            target = jnp.zeros((1, lanes), jnp.float32)
            for side in range(square):
                lines = slice(side * part, (side + 1) * part)
                hit = labels - place_ref[side] == line
                tile = scaled[lines, start : start + lanes]
                exps = jnp.exp(
                    tile - jnp.where(hit, logit_scale + logit_scale * margin, logit_scale)
                )
                exp_ref[lines, index * lanes : (index + 1) * lanes] = exps
                total = total + jnp.sum(exps, axis=0, keepdims=True)
                target = target + jnp.sum(jnp.where(hit, tile, 0.0), axis=0, keepdims=True)
            group = place_ref[square + 1] ^ span[index][0]
            stat_ref[pl.ds(group, 1), :] = total
            stat_ref[pl.ds(count + group, 1), :] = target


def grads_kernel(count, replicas, spans, sides, place_ref, stat_ref, *refs):
    chunks = [refs[3 * index : 3 * index + 3] for index in range(len(spans))]
    refs = refs[3 * len(spans) :]
    outs, scratch = refs[: len(sides)], refs[-len(spans) :]
    part = chunks[0][0].shape[0] // square
    lanes = stat_ref.shape[1]
    scale = logit_scale / replicas
    group = place_ref[square + 1]
    if 0 in sides:
        refs[len(sides)][...] = (
            logit_scale
            + jnp.log(stat_ref[pl.ds(group, 1), :])
            - (stat_ref[pl.ds(count + group, 1), :] - logit_scale * margin)
        )
    line = lax.broadcasted_iota(jnp.int32, (part, lanes), 0)
    total = None
    for span, (exp_ref, every_ref, label_ref), grads in zip(spans, chunks, scratch):
        for index in range(len(span)):
            inverse = 1.0 / stat_ref[pl.ds(group ^ span[index][0], 1), :]
            columns = slice(index * lanes, (index + 1) * lanes)
            labels = label_ref[index : index + 1, :]
            for place, side in enumerate(sides):
                hit = labels - place_ref[side] == line
                exps = exp_ref[side * part : (side + 1) * part, columns]
                grads[place * part : (place + 1) * part, columns] = (
                    exps * inverse - jnp.where(hit, 1.0, 0.0)
                ).astype(jnp.bfloat16)
        product = jnp.dot(grads[...], every_ref[...], preferred_element_type=jnp.float32)
        total = product if total is None else total + product
    for index, out in enumerate(outs):
        out[...] = (total[index * part : (index + 1) * part, :] * scale).astype(out.dtype)


def finish_kernel(chosen_ref, own_ref, *refs):
    others, out_ref = refs[:-1], refs[-1]
    summed = own_ref[...]
    for other in others:
        summed = summed + other[...].astype(jnp.float32)
    rows = chosen_ref[...]
    inverse = lax.rsqrt(jnp.sum(rows * rows, axis=1, keepdims=True) + epsilon)
    unit = rows * inverse
    radial = jnp.sum(unit * summed, axis=1, keepdims=True)
    out_ref[...] = inverse * (summed - unit * radial)


def per_device(features, labels, weights, sampled):
    groups = lax.axis_size("cls")
    replicas = lax.axis_size("dp")
    local_rows, width = features.shape
    classes = sampled.shape[0]
    part = classes // replicas
    position = lax.axis_index("cls").astype(jnp.int32)
    replica = lax.axis_index("dp").astype(jnp.int32)
    place = jnp.stack(
        [(position ^ side) * classes + replica * part for side in range(square)]
        + [replica, position // square * replicas + replica]
    )

    def swap(value, chip_mask, core_mask):
        mask = chip_mask * replicas + core_mask
        return lax.ppermute(
            value, ("cls", "dp"), [(i, i ^ mask) for i in range(groups * replicas)]
        )

    bits = [(0, 1 << bit) for bit in range(replicas.bit_length() - 1)]
    far_bits = [(1 << bit, 0) for bit in range(2, groups.bit_length() - 1)]

    upper, marks = {0: features}, labels.reshape(1, local_rows)
    for bit, _ in far_bits[1:]:
        upper.update({mask | bit: swap(block, bit, 0) for mask, block in list(upper.items())})
        marks = jnp.concatenate([marks, swap(marks, bit, 0)], axis=0)
    near_raw = swap(features, square, 0)
    mine = lax.dynamic_slice_in_dim(sampled, replica * part, part)
    chosen = weights.at[mine].get(mode="promise_in_bounds", unique_indices=True)
    low_rows = pl.pallas_call(
        choose_kernel,
        out_shape=jax.ShapeDtypeStruct((part + extra, width), jnp.bfloat16),
        in_specs=[vmem_spec],
        out_specs=vmem_spec,
        compiler_params=params(),
        name="choose",
    )(chosen)
    def spread(block):
        near = [block]
        for _, bit in bits:
            near = near + [swap(value, 0, bit) for value in near]
        return near

    tie = lax.optimization_barrier
    corner_rows, marks = tie((low_rows, marks))
    rows = [low_rows, swap(low_rows, 1, 0), swap(low_rows, 2, 0), swap(corner_rows, 3, 0)]
    tied, near_raw = tie(({mask: block for mask, block in upper.items() if mask}, near_raw))
    upper.update(tied)
    packed = {
        mask: pl.pallas_call(
            pack_kernel,
            out_shape=jax.ShapeDtypeStruct((local_rows + extra, width), jnp.bfloat16),
            in_specs=[vmem_spec] * 2,
            out_specs=vmem_spec,
            compiler_params=params(),
            name="pack",
        )(block, marks)
        for mask, block in upper.items()
        if mask
    }
    pair = pl.pallas_call(
        normalize_kernel,
        out_shape=jax.ShapeDtypeStruct((2 * local_rows, width), jnp.bfloat16),
        in_specs=[vmem_spec] * 2,
        out_specs=vmem_spec,
        compiler_params=params(),
        name="normalize",
    )(features, near_raw)
    passed = {mask | square: swap(block, square, 0) for mask, block in packed.items()}
    rows = tie(rows[::-1])[::-1]
    passed, rows, pair = tie((passed, rows, pair))
    ups = list(packed)
    held = [pair, *packed.values(), *passed.values()]
    spread_out = [spread(array) for array in held]
    count = groups // square * replicas
    order = list(upper)

    def entry(index, first_replica):
        mask, replica_bit = index // replicas * square, index % replicas
        up, beside = mask & ~square, bool(mask & square)
        base = (replica_bit - first_replica) * len(held) + 1 + beside * len(ups)
        source = base + ups.index(groups // 2)
        if up:
            return (index, base + ups.index(up), 0, source, order.index(up))
        return (index, base - 1 - beside * len(ups), beside * local_rows, source, 0)

    spans, arrays = [], []
    for some in (range(1), range(1, replicas)):
        spans.append(
            tuple(entry(index, some[0]) for index in range(count) if index % replicas in some)
        )
        arrays.append([copies[bit] for bit in some for copies in spread_out])
    chunks, carried = [], rows
    for joined, span in enumerate(spans):
        shapes = [
            jax.ShapeDtypeStruct((square * part, len(span) * local_rows), jnp.float32),
            jax.ShapeDtypeStruct((2 * count, local_rows), jnp.float32),
            jax.ShapeDtypeStruct((len(span) * local_rows, width), jnp.bfloat16),
            jax.ShapeDtypeStruct((len(span), local_rows), jnp.int32),
            jax.ShapeDtypeStruct((square * part, width), jnp.bfloat16),
        ][: 5 - joined]
        exps, stats, every, marks, *together = pl.pallas_call(
            functools.partial(logits_kernel, count, span, len(arrays[joined]), joined),
            out_shape=shapes,
            in_specs=[smem_spec] + [vmem_spec] * (len(arrays[joined]) + len(carried)),
            out_specs=[vmem_spec] * len(shapes),
            compiler_params=params(bytes_of([*arrays[joined], *carried, *shapes])),
            name="logits",
        )(place, *arrays[joined], *carried)
        chunks, carried = chunks + [exps, every, marks], together + [stats]
    near = [(0, 0)]
    for chip_bit, core_bit in bits[:1] + far_bits[:1]:
        near = near + [(chip_mask | chip_bit, core_mask | core_bit) for chip_mask, core_mask in near]
    stats = sum((swap(stats, *masks) for masks in near[1:]), stats)
    for chip_mask, core_mask in bits[1:] + far_bits[1:]:
        stats = stats + swap(stats, chip_mask, core_mask)

    def grads(sides):
        kinds = [jnp.bfloat16 if side else jnp.float32 for side in sides]
        shapes = [jax.ShapeDtypeStruct((part, width), kind) for kind in kinds]
        if 0 in sides:
            shapes.append(jax.ShapeDtypeStruct((1, local_rows), jnp.float32))
        return pl.pallas_call(
            functools.partial(grads_kernel, count, replicas, spans, sides),
            out_shape=shapes,
            in_specs=[smem_spec] + [vmem_spec] * (1 + len(chunks)),
            out_specs=[vmem_spec] * len(shapes),
            scratch_shapes=[
                pltpu.VMEM((len(sides) * part, len(span) * local_rows), jnp.bfloat16)
                for span in spans
            ],
            compiler_params=params(bytes_of([stats, *chunks, *shapes]) + bytes_of(chunks) // 2),
            name="grads",
        )(place, stats, *chunks)

    away = [swap(block, side, 0) for side, block in enumerate(grads((1, 2, 3)), 1)]
    own_part, loss = grads((0,))
    weight_grad = pl.pallas_call(
        finish_kernel,
        out_shape=jax.ShapeDtypeStruct((part, width), jnp.float32),
        in_specs=[vmem_spec] * (2 + len(away)),
        out_specs=vmem_spec,
        compiler_params=params(),
        name="finish",
    )(chosen, own_part, *away)
    return (loss.reshape(local_rows), weight_grad)


def solution(mesh):
    in_specs = (P(("cls", "dp"), None), P(("cls", "dp")), P("cls", None), P("cls"))
    out_specs = (P(("cls", "dp")), P(("cls", "dp"), None))
    return jax.shard_map(
        per_device, mesh=mesh, in_specs=in_specs, out_specs=out_specs, check_vma=False
    )
```

```python
import functools

import jax
import jax.numpy as jnp
from jax import lax
from jax.experimental import pallas as pl
from jax.experimental.pallas import tpu as pltpu
from jax.sharding import PartitionSpec as P

logit_scale = 64.0
margin = 0.35
epsilon = 1e-06
digit = 256
extra = 8
square = 4

vmem_spec = pl.BlockSpec(memory_space=pltpu.VMEM)
smem_spec = pl.BlockSpec(memory_space=pltpu.SMEM)
hbm_spec = pl.BlockSpec(memory_space=pltpu.HBM)


def params(operand_bytes=0):
    limit = min(48 * 1024 * 1024, 8 * 1024 * 1024 + 5 * operand_bytes // 4)
    return pltpu.CompilerParams(vmem_limit_bytes=limit)


def bytes_of(arrays):
    return sum(array.size * array.dtype.itemsize for array in arrays)


def normalized(feat_ref):
    wide = feat_ref[...].astype(jnp.float32)
    squares = jnp.sum(wide * wide, axis=1, keepdims=True)
    return (wide * lax.rsqrt(squares + epsilon)).astype(jnp.bfloat16)


def pack_kernel(feat_ref, label_ref, *refs):
    out_ref = refs[-1]
    rows, width = feat_ref.shape
    sets = label_ref.shape[0]
    out_ref[:rows, :] = normalized(feat_ref)
    labels = label_ref[...]
    digits = [labels // digit, labels % digit]
    line = lax.broadcasted_iota(jnp.int32, (extra, width), 0)
    packed = jnp.zeros((extra, width), jnp.float32)
    per_row = width // (2 * rows)
    for first in range(0, sets, per_row):
        pieces = [
            part[index : index + 1, :]
            for index in range(first, min(first + per_row, sets))
            for part in digits
        ]
        if len(pieces) * rows < width:
            pieces.append(jnp.zeros((1, width - len(pieces) * rows), jnp.int32))
        row = jnp.concatenate(pieces, axis=1).astype(jnp.float32)
        packed = jnp.where(line == first // per_row, row, packed)
    out_ref[rows:, :] = packed.astype(jnp.bfloat16)
    for index, raw_ref in enumerate(refs[:-2]):
        refs[-2][index * rows : (index + 1) * rows, :] = normalized(raw_ref)


def labels_of(packed_ref, index):
    rows = packed_ref.shape[0] - extra
    per_row = packed_ref.shape[1] // (2 * rows)
    line, start = index // per_row, index % per_row * 2 * rows
    digits = packed_ref[rows:, :].astype(jnp.float32)[line : line + 1, :].astype(jnp.int32)
    return digits[:, start : start + rows] * digit + digits[:, start + rows : start + 2 * rows]


def choose_kernel(chosen_ref, low_ref):
    part = chosen_ref.shape[0]
    rows = chosen_ref[...]
    inverse = lax.rsqrt(jnp.sum(rows * rows, axis=1, keepdims=True) + epsilon)
    low_ref[:part, :] = (rows * inverse).astype(jnp.bfloat16) * logit_scale
    low_ref[part:, :] = jnp.zeros_like(low_ref[part:, :])


def logits_kernel(count, span, held, joined, place_ref, *refs):
    feats = refs[:held]
    if joined:
        rows, earlier_ref = refs[held : held + 2]
        exp_ref, stat_ref, every_ref, label_ref = refs[-4:]
        stat_ref[...] = earlier_ref[...]
    else:
        classes = refs[held : held + square]
        exp_ref, stat_ref, every_ref, label_ref, rows = refs[-5:]
        part = rows.shape[0] // square
        for side in range(square):
            rows[side * part : (side + 1) * part, :] = classes[side][:part, :]
    part = rows.shape[0] // square
    lanes = label_ref.shape[1]
    for index, (_, place, first, source, label_set) in enumerate(span):
        every_ref[index * lanes : (index + 1) * lanes, :] = feats[place][first : first + lanes, :]
        label_ref[index : index + 1, :] = labels_of(feats[source], label_set)
    line = lax.broadcasted_iota(jnp.int32, (part, lanes), 0)
    for pair in range(0, len(span), 2):
        scaled = lax.dot_general(
            rows[...],
            every_ref[pair * lanes : (pair + 2) * lanes, :],
            (((1,), (1,)), ((), ())),
            preferred_element_type=jnp.float32,
        )
        for index in (pair, pair + 1):
            start = (index - pair) * lanes
            labels = label_ref[index : index + 1, :]
            total = jnp.zeros((1, lanes), jnp.float32)
            target = jnp.zeros((1, lanes), jnp.float32)
            for side in range(square):
                lines = slice(side * part, (side + 1) * part)
                hit = labels - place_ref[side] == line
                tile = scaled[lines, start : start + lanes]
                exps = jnp.exp(
                    tile - jnp.where(hit, logit_scale + logit_scale * margin, logit_scale)
                )
                exp_ref[lines, index * lanes : (index + 1) * lanes] = exps.astype(jnp.bfloat16)
                total = total + jnp.sum(exps, axis=0, keepdims=True)
                target = target + jnp.sum(jnp.where(hit, tile, 0.0), axis=0, keepdims=True)
            group = place_ref[square + 1] ^ span[index][0]
            stat_ref[pl.ds(group, 1), :] = total
            stat_ref[pl.ds(count + group, 1), :] = target


def grads_kernel(count, replicas, spans, sides, place_ref, stat_ref, *refs):
    chunks = [refs[3 * index : 3 * index + 3] for index in range(len(spans))]
    refs = refs[3 * len(spans) :]
    outs, scratch = refs[: len(sides)], refs[-len(spans) :]
    part = chunks[0][0].shape[0] // square
    lanes = stat_ref.shape[1]
    scale = logit_scale / replicas
    group = place_ref[square + 1]
    if 0 in sides:
        refs[len(sides)][...] = (
            logit_scale
            + jnp.log(stat_ref[pl.ds(group, 1), :])
            - (stat_ref[pl.ds(count + group, 1), :] - logit_scale * margin)
        )
    line = lax.broadcasted_iota(jnp.int32, (part, lanes), 0)
    total = None
    for span, (exp_ref, every_ref, label_ref), grads in zip(spans, chunks, scratch):
        for index in range(len(span)):
            inverse = 1.0 / stat_ref[pl.ds(group ^ span[index][0], 1), :]
            columns = slice(index * lanes, (index + 1) * lanes)
            labels = label_ref[index : index + 1, :]
            for place, side in enumerate(sides):
                hit = labels - place_ref[side] == line
                exps = exp_ref[side * part : (side + 1) * part, columns].astype(jnp.float32)
                grads[place * part : (place + 1) * part, columns] = (
                    exps * inverse - jnp.where(hit, 1.0, 0.0)
                ).astype(jnp.bfloat16)
        product = jnp.dot(grads[...], every_ref[...], preferred_element_type=jnp.float32)
        total = product if total is None else total + product
    for index, out in enumerate(outs):
        out[...] = (total[index * part : (index + 1) * part, :] * scale).astype(out.dtype)


def finish_kernel(chosen_ref, own_ref, *refs):
    others, out_ref = refs[:-1], refs[-1]
    summed = own_ref[...]
    for other in others:
        summed = summed + other[...].astype(jnp.float32)
    rows = chosen_ref[...]
    inverse = lax.rsqrt(jnp.sum(rows * rows, axis=1, keepdims=True) + epsilon)
    unit = rows * inverse
    radial = jnp.sum(unit * summed, axis=1, keepdims=True)
    out_ref[...] = inverse * (summed - unit * radial)


def per_device(features, labels, weights, sampled):
    groups = lax.axis_size("cls")
    replicas = lax.axis_size("dp")
    local_rows, width = features.shape
    classes = sampled.shape[0]
    part = classes // replicas
    position = lax.axis_index("cls").astype(jnp.int32)
    replica = lax.axis_index("dp").astype(jnp.int32)
    place = jnp.stack(
        [(position ^ side) * classes + replica * part for side in range(square)]
        + [replica, position // square * replicas + replica]
    )

    def swap(value, chip_mask, core_mask):
        mask = chip_mask * replicas + core_mask
        return lax.ppermute(
            value, ("cls", "dp"), [(i, i ^ mask) for i in range(groups * replicas)]
        )

    bits = [(0, 1 << bit) for bit in range(replicas.bit_length() - 1)]
    far_bits = [(1 << bit, 0) for bit in range(2, groups.bit_length() - 1)]

    upper, marks = {0: features}, labels.reshape(1, local_rows)
    for bit, _ in far_bits[1:]:
        upper.update({mask | bit: swap(block, bit, 0) for mask, block in list(upper.items())})
        marks = jnp.concatenate([marks, swap(marks, bit, 0)], axis=0)
    near_raw = swap(features, square, 0)
    mine = lax.dynamic_slice_in_dim(sampled, replica * part, part)
    chosen = weights.at[mine].get(mode="promise_in_bounds", unique_indices=True)
    low_rows = pl.pallas_call(
        choose_kernel,
        out_shape=jax.ShapeDtypeStruct((part + extra, width), jnp.bfloat16),
        in_specs=[vmem_spec],
        out_specs=vmem_spec,
        compiler_params=params(),
        name="choose",
    )(chosen)
    def spread(block):
        near = [block]
        for _, bit in bits:
            near = near + [swap(value, 0, bit) for value in near]
        return near

    tie = lax.optimization_barrier
    corner_rows, marks = tie((low_rows, marks))
    rows = [low_rows, swap(low_rows, 1, 0), swap(low_rows, 2, 0), swap(corner_rows, 3, 0)]
    tied, near_raw = tie(({mask: block for mask, block in upper.items() if mask}, near_raw))
    upper.update(tied)
    packed, pair = {}, None
    for mask, block in upper.items():
        if mask == 0:
            continue
        raw = [features, near_raw] if pair is None else []
        shapes = [jax.ShapeDtypeStruct((2 * local_rows, width), jnp.bfloat16)] * (pair is None)
        shapes.append(jax.ShapeDtypeStruct((local_rows + extra, width), jnp.bfloat16))
        *made, packed[mask] = pl.pallas_call(
            pack_kernel,
            out_shape=shapes,
            in_specs=[vmem_spec] * (2 + len(raw)),
            out_specs=[vmem_spec] * len(shapes),
            compiler_params=params(),
            name="pack",
        )(block, marks, *raw)
        pair = made[0] if made else pair
    passed = {mask | square: swap(block, square, 0) for mask, block in packed.items()}
    rows = tie(rows[::-1])[::-1]
    passed, rows = tie((passed, rows))
    ups = list(packed)
    held = [pair, *packed.values(), *passed.values()]
    spread_out = [spread(array) for array in held]
    count = groups // square * replicas
    order = list(upper)

    def entry(index, first_replica):
        mask, replica_bit = index // replicas * square, index % replicas
        up, beside = mask & ~square, bool(mask & square)
        base = (replica_bit - first_replica) * len(held) + 1 + beside * len(ups)
        source = base + ups.index(groups // 2)
        if up:
            return (index, base + ups.index(up), 0, source, order.index(up))
        return (index, base - 1 - beside * len(ups), beside * local_rows, source, 0)

    spans, arrays = [], []
    for some in (range(1), range(1, replicas)):
        spans.append(
            tuple(entry(index, some[0]) for index in range(count) if index % replicas in some)
        )
        arrays.append([copies[bit] for bit in some for copies in spread_out])
    chunks, carried = [], rows
    for joined, span in enumerate(spans):
        shapes = [
            jax.ShapeDtypeStruct((square * part, len(span) * local_rows), jnp.bfloat16),
            jax.ShapeDtypeStruct((2 * count, local_rows), jnp.float32),
            jax.ShapeDtypeStruct((len(span) * local_rows, width), jnp.bfloat16),
            jax.ShapeDtypeStruct((len(span), local_rows), jnp.int32),
            jax.ShapeDtypeStruct((square * part, width), jnp.bfloat16),
        ][: 5 - joined]
        exps, stats, every, marks, *together = pl.pallas_call(
            functools.partial(logits_kernel, count, span, len(arrays[joined]), joined),
            out_shape=shapes,
            in_specs=[smem_spec] + [vmem_spec] * (len(arrays[joined]) + len(carried)),
            out_specs=[vmem_spec] * len(shapes),
            compiler_params=params(bytes_of([*arrays[joined], *carried, *shapes])),
            name="logits",
        )(place, *arrays[joined], *carried)
        chunks, carried = chunks + [exps, every, marks], together + [stats]
    near = [(0, 0)]
    for chip_bit, core_bit in bits[:1] + far_bits[:1]:
        near = near + [(chip_mask | chip_bit, core_mask | core_bit) for chip_mask, core_mask in near]
    stats = sum((swap(stats, *masks) for masks in near[1:]), stats)
    for chip_mask, core_mask in bits[1:] + far_bits[1:]:
        stats = stats + swap(stats, chip_mask, core_mask)

    def grads(sides):
        kinds = [jnp.bfloat16 if side else jnp.float32 for side in sides]
        shapes = [jax.ShapeDtypeStruct((part, width), kind) for kind in kinds]
        if 0 in sides:
            shapes.append(jax.ShapeDtypeStruct((1, local_rows), jnp.float32))
        return pl.pallas_call(
            functools.partial(grads_kernel, count, replicas, spans, sides),
            out_shape=shapes,
            in_specs=[smem_spec] + [vmem_spec] * (1 + len(chunks)),
            out_specs=[vmem_spec] * len(shapes),
            scratch_shapes=[
                pltpu.VMEM((len(sides) * part, len(span) * local_rows), jnp.bfloat16)
                for span in spans
            ],
            compiler_params=params(bytes_of([stats, *chunks, *shapes]) + bytes_of(chunks) // 2),
            name="grads",
        )(place, stats, *chunks)

    away = [swap(block, side, 0) for side, block in enumerate(grads((1, 2, 3)), 1)]
    own_part, loss = grads((0,))
    weight_grad = pl.pallas_call(
        finish_kernel,
        out_shape=jax.ShapeDtypeStruct((part, width), jnp.float32),
        in_specs=[vmem_spec] * (2 + len(away)),
        out_specs=vmem_spec,
        compiler_params=params(),
        name="finish",
    )(chosen, own_part, *away)
    return (loss.reshape(local_rows), weight_grad)


def solution(mesh):
    in_specs = (P(("cls", "dp"), None), P(("cls", "dp")), P("cls", None), P("cls"))
    out_specs = (P(("cls", "dp")), P(("cls", "dp"), None))
    return jax.shard_map(
        per_device, mesh=mesh, in_specs=in_specs, out_specs=out_specs, check_vma=False
    )
```

```python
import functools

import jax
import jax.numpy as jnp
from jax import lax
from jax.experimental import pallas as pl
from jax.experimental.pallas import tpu as pltpu
from jax.sharding import PartitionSpec as P

logit_scale = 64.0
margin = 0.35
epsilon = 1e-06
digit = 256
extra = 8
square = 4

vmem_spec = pl.BlockSpec(memory_space=pltpu.VMEM)
smem_spec = pl.BlockSpec(memory_space=pltpu.SMEM)
hbm_spec = pl.BlockSpec(memory_space=pltpu.HBM)


vmem_bytes = 64 * 1024 * 1024


def params(room):
    return pltpu.CompilerParams(vmem_limit_bytes=vmem_bytes - room * 1024)


def normalized(feat_ref):
    wide = feat_ref[...].astype(jnp.float32)
    squares = jnp.sum(wide * wide, axis=1, keepdims=True)
    return (wide * lax.rsqrt(squares + epsilon)).astype(jnp.bfloat16)


def normalize_kernel(*refs):
    rows = refs[0].shape[0]
    for index, feat_ref in enumerate(refs[:-1]):
        refs[-1][index * rows : (index + 1) * rows, :] = normalized(feat_ref)


def pack_kernel(feat_ref, label_ref, out_ref):
    rows, width = feat_ref.shape
    sets = label_ref.shape[0]
    out_ref[:rows, :] = normalized(feat_ref)
    labels = label_ref[...]
    digits = [labels // digit, labels % digit]
    line = lax.broadcasted_iota(jnp.int32, (extra, width), 0)
    packed = jnp.zeros((extra, width), jnp.float32)
    per_row = width // (2 * rows)
    for first in range(0, sets, per_row):
        pieces = [
            part[index : index + 1, :]
            for index in range(first, min(first + per_row, sets))
            for part in digits
        ]
        if len(pieces) * rows < width:
            pieces.append(jnp.zeros((1, width - len(pieces) * rows), jnp.int32))
        row = jnp.concatenate(pieces, axis=1).astype(jnp.float32)
        packed = jnp.where(line == first // per_row, row, packed)
    out_ref[rows:, :] = packed.astype(jnp.bfloat16)


def labels_of(packed_ref, index):
    rows = packed_ref.shape[0] - extra
    per_row = packed_ref.shape[1] // (2 * rows)
    line, start = index // per_row, index % per_row * 2 * rows
    digits = packed_ref[rows:, :].astype(jnp.float32)[line : line + 1, :].astype(jnp.int32)
    return digits[:, start : start + rows] * digit + digits[:, start + rows : start + 2 * rows]


def choose_kernel(place_ref, sampled_hbm, weight_hbm, low_ref, chosen_ref, sampled_ref, sems):
    part = chosen_ref.shape[0]
    first = place_ref[square] * part
    copy = pltpu.make_async_copy(sampled_hbm, sampled_ref, sems.at[0])
    copy.start()
    copy.wait()

    def start_row(row, carry):
        pltpu.make_async_copy(
            weight_hbm.at[pl.ds(sampled_ref[first + row], 1), :],
            chosen_ref.at[pl.ds(row, 1), :],
            sems.at[1],
        ).start()
        return carry

    lax.fori_loop(0, part, start_row, 0, unroll=32)
    pltpu.make_async_copy(weight_hbm.at[pl.ds(0, part), :], chosen_ref, sems.at[1]).wait()
    rows = chosen_ref[...]
    inverse = lax.rsqrt(jnp.sum(rows * rows, axis=1, keepdims=True) + epsilon)
    low_ref[:part, :] = (rows * inverse).astype(jnp.bfloat16) * logit_scale
    low_ref[part:, :] = jnp.zeros_like(low_ref[part:, :])


def logits_kernel(count, span, held, joined, place_ref, *refs):
    feats = refs[:held]
    if joined:
        rows, earlier_ref = refs[held : held + 2]
        exp_ref, stat_ref, every_ref, label_ref = refs[-4:]
        stat_ref[...] = earlier_ref[...]
    else:
        classes = refs[held : held + square]
        exp_ref, stat_ref, every_ref, label_ref, rows = refs[-5:]
        part = rows.shape[0] // square
        for side in range(square):
            rows[side * part : (side + 1) * part, :] = classes[side][:part, :]
    part = rows.shape[0] // square
    lanes = label_ref.shape[1]
    for index, (_, place, first, source, label_set) in enumerate(span):
        every_ref[index * lanes : (index + 1) * lanes, :] = feats[place][first : first + lanes, :]
        label_ref[index : index + 1, :] = labels_of(feats[source], label_set)
    line = lax.broadcasted_iota(jnp.int32, (part, lanes), 0)
    for pair in range(0, len(span), 2):
        scaled = lax.dot_general(
            rows[...],
            every_ref[pair * lanes : (pair + 2) * lanes, :],
            (((1,), (1,)), ((), ())),
            preferred_element_type=jnp.float32,
        )
        for index in (pair, pair + 1):
            start = (index - pair) * lanes
            labels = label_ref[index : index + 1, :]
            total = jnp.zeros((1, lanes), jnp.float32)
            target = jnp.zeros((1, lanes), jnp.float32)
            for side in range(square):
                lines = slice(side * part, (side + 1) * part)
                hit = labels - place_ref[side] == line
                tile = scaled[lines, start : start + lanes]
                exps = jnp.exp(
                    tile - jnp.where(hit, logit_scale + logit_scale * margin, logit_scale)
                )
                exp_ref[lines, index * lanes : (index + 1) * lanes] = exps
                total = total + jnp.sum(exps, axis=0, keepdims=True)
                target = target + jnp.sum(jnp.where(hit, tile, 0.0), axis=0, keepdims=True)
            group = place_ref[square + 1] ^ span[index][0]
            stat_ref[pl.ds(group, 1), :] = total
            stat_ref[pl.ds(count + group, 1), :] = target


def grads_kernel(count, replicas, spans, sides, place_ref, stat_ref, *refs):
    chunks = [refs[3 * index : 3 * index + 3] for index in range(len(spans))]
    refs = refs[3 * len(spans) :]
    outs, scratch = refs[: len(sides)], refs[-len(spans) :]
    part = chunks[0][0].shape[0] // square
    lanes = stat_ref.shape[1]
    scale = logit_scale / replicas
    group = place_ref[square + 1]
    if 0 in sides:
        refs[len(sides)][...] = (
            logit_scale
            + jnp.log(stat_ref[pl.ds(group, 1), :])
            - (stat_ref[pl.ds(count + group, 1), :] - logit_scale * margin)
        )
    line = lax.broadcasted_iota(jnp.int32, (part, lanes), 0)
    total = None
    for span, (exp_ref, every_ref, label_ref), grads in zip(spans, chunks, scratch):
        for index in range(len(span)):
            inverse = 1.0 / stat_ref[pl.ds(group ^ span[index][0], 1), :]
            columns = slice(index * lanes, (index + 1) * lanes)
            labels = label_ref[index : index + 1, :]
            for place, side in enumerate(sides):
                hit = labels - place_ref[side] == line
                exps = exp_ref[side * part : (side + 1) * part, columns]
                grads[place * part : (place + 1) * part, columns] = (
                    exps * inverse - jnp.where(hit, 1.0, 0.0)
                ).astype(jnp.bfloat16)
        product = jnp.dot(grads[...], every_ref[...], preferred_element_type=jnp.float32)
        total = product if total is None else total + product
    for index, out in enumerate(outs):
        out[...] = (total[index * part : (index + 1) * part, :] * scale).astype(out.dtype)


def finish_kernel(chosen_ref, own_ref, *refs):
    others, out_ref = refs[:-1], refs[-1]
    summed = own_ref[...]
    for other in others:
        summed = summed + other[...].astype(jnp.float32)
    rows = chosen_ref[...]
    inverse = lax.rsqrt(jnp.sum(rows * rows, axis=1, keepdims=True) + epsilon)
    unit = rows * inverse
    radial = jnp.sum(unit * summed, axis=1, keepdims=True)
    out_ref[...] = inverse * (summed - unit * radial)


def per_device(features, labels, weights, sampled):
    groups = lax.axis_size("cls")
    replicas = lax.axis_size("dp")
    local_rows, width = features.shape
    classes = sampled.shape[0]
    part = classes // replicas
    position = lax.axis_index("cls").astype(jnp.int32)
    replica = lax.axis_index("dp").astype(jnp.int32)
    place = jnp.stack(
        [(position ^ side) * classes + replica * part for side in range(square)]
        + [replica, position // square * replicas + replica]
    )

    def swap(value, chip_mask, core_mask):
        mask = chip_mask * replicas + core_mask
        return lax.ppermute(
            value, ("cls", "dp"), [(i, i ^ mask) for i in range(groups * replicas)]
        )

    bits = [(0, 1 << bit) for bit in range(replicas.bit_length() - 1)]
    far_bits = [(1 << bit, 0) for bit in range(2, groups.bit_length() - 1)]

    upper, marks = {0: features}, labels.reshape(1, local_rows)
    for bit, _ in far_bits[1:]:
        upper.update({mask | bit: swap(block, bit, 0) for mask, block in list(upper.items())})
        marks = jnp.concatenate([marks, swap(marks, bit, 0)], axis=0)
    near_raw = swap(features, square, 0)
    low_rows, chosen = pl.pallas_call(
        choose_kernel,
        out_shape=[
            jax.ShapeDtypeStruct((part + extra, width), jnp.bfloat16),
            jax.ShapeDtypeStruct((part, width), jnp.float32),
        ],
        in_specs=[smem_spec, hbm_spec, hbm_spec],
        out_specs=[vmem_spec] * 2,
        scratch_shapes=[pltpu.SMEM((classes,), jnp.int32), pltpu.SemaphoreType.DMA((2,))],
        compiler_params=params(11264),
        name="choose",
    )(place, sampled, weights)
    def spread(block):
        near = [block]
        for _, bit in bits:
            near = near + [swap(value, 0, bit) for value in near]
        return near

    tie = lax.optimization_barrier
    corner_rows, marks = tie((low_rows, marks))
    rows = [low_rows, swap(low_rows, 1, 0), swap(low_rows, 2, 0), swap(corner_rows, 3, 0)]
    tied, near_raw = tie(({mask: block for mask, block in upper.items() if mask}, near_raw))
    upper.update(tied)
    packed = {
        mask: pl.pallas_call(
            pack_kernel,
            out_shape=jax.ShapeDtypeStruct((local_rows + extra, width), jnp.bfloat16),
            in_specs=[vmem_spec] * 2,
            out_specs=vmem_spec,
            compiler_params=params(56 * 1024),
            name="pack",
        )(block, marks)
        for mask, block in upper.items()
        if mask
    }
    pair = pl.pallas_call(
        normalize_kernel,
        out_shape=jax.ShapeDtypeStruct((2 * local_rows, width), jnp.bfloat16),
        in_specs=[vmem_spec] * 2,
        out_specs=vmem_spec,
        compiler_params=params(56 * 1024),
        name="normalize",
    )(features, near_raw)
    passed = {mask | square: swap(block, square, 0) for mask, block in packed.items()}
    rows = tie(rows[::-1])[::-1]
    passed, rows = tie((passed, rows))
    ups = list(packed)
    held = [pair, *packed.values(), *passed.values()]
    spread_out = [spread(array) for array in held]
    count = groups // square * replicas
    order = list(upper)

    def entry(index, first_replica):
        mask, replica_bit = index // replicas * square, index % replicas
        up, beside = mask & ~square, bool(mask & square)
        base = (replica_bit - first_replica) * len(held) + 1 + beside * len(ups)
        source = base + ups.index(groups // 2)
        if up:
            return (index, base + ups.index(up), 0, source, order.index(up))
        return (index, base - 1 - beside * len(ups), beside * local_rows, source, 0)

    spans, arrays = [], []
    for some in (range(1), range(1, replicas)):
        spans.append(
            tuple(entry(index, some[0]) for index in range(count) if index % replicas in some)
        )
        arrays.append([copies[bit] for bit in some for copies in spread_out])
    chunks, carried = [], rows
    for joined, span in enumerate(spans):
        shapes = [
            jax.ShapeDtypeStruct((square * part, len(span) * local_rows), jnp.float32),
            jax.ShapeDtypeStruct((2 * count, local_rows), jnp.float32),
            jax.ShapeDtypeStruct((len(span) * local_rows, width), jnp.bfloat16),
            jax.ShapeDtypeStruct((len(span), local_rows), jnp.int32),
            jax.ShapeDtypeStruct((square * part, width), jnp.bfloat16),
        ][: 5 - joined]
        exps, stats, every, marks, *together = pl.pallas_call(
            functools.partial(logits_kernel, count, span, len(arrays[joined]), joined),
            out_shape=shapes,
            in_specs=[smem_spec] + [vmem_spec] * (len(arrays[joined]) + len(carried)),
            out_specs=[vmem_spec] * len(shapes),
            compiler_params=params(16 * 1024),
            name="logits",
        )(place, *arrays[joined], *carried)
        chunks, carried = chunks + [exps, every, marks], together + [stats]
    near = [(0, 0)]
    for chip_bit, core_bit in bits[:1] + far_bits[:1]:
        near = near + [(chip_mask | chip_bit, core_mask | core_bit) for chip_mask, core_mask in near]
    stats = sum((swap(stats, *masks) for masks in near[1:]), stats)
    for chip_mask, core_mask in bits[1:] + far_bits[1:]:
        stats = stats + swap(stats, chip_mask, core_mask)

    def grads(sides):
        kinds = [jnp.bfloat16 if side else jnp.float32 for side in sides]
        shapes = [jax.ShapeDtypeStruct((part, width), kind) for kind in kinds]
        if 0 in sides:
            shapes.append(jax.ShapeDtypeStruct((1, local_rows), jnp.float32))
        return pl.pallas_call(
            functools.partial(grads_kernel, count, replicas, spans, sides),
            out_shape=shapes,
            in_specs=[smem_spec] + [vmem_spec] * (1 + len(chunks)),
            out_specs=[vmem_spec] * len(shapes),
            scratch_shapes=[
                pltpu.VMEM((len(sides) * part, len(span) * local_rows), jnp.bfloat16)
                for span in spans
            ],
            compiler_params=params(16 * 1024),
            name="grads",
        )(place, stats, *chunks)

    away = [swap(block, side, 0) for side, block in enumerate(grads((1, 2, 3)), 1)]
    mine, loss = grads((0,))
    weight_grad = pl.pallas_call(
        finish_kernel,
        out_shape=jax.ShapeDtypeStruct((part, width), jnp.float32),
        in_specs=[vmem_spec] * (2 + len(away)),
        out_specs=vmem_spec,
        compiler_params=params(56 * 1024),
        name="finish",
    )(chosen, mine, *away)
    return (loss.reshape(local_rows), weight_grad)


def solution(mesh):
    in_specs = (P(("cls", "dp"), None), P(("cls", "dp")), P("cls", None), P("cls"))
    out_specs = (P(("cls", "dp")), P(("cls", "dp"), None))
    return jax.shard_map(
        per_device, mesh=mesh, in_specs=in_specs, out_specs=out_specs, check_vma=False
    )
```

```python
import functools

import jax
import jax.numpy as jnp
from jax import lax
from jax.experimental import pallas as pl
from jax.experimental.pallas import tpu as pltpu
from jax.sharding import PartitionSpec as P

logit_scale = 64.0
margin = 0.35
epsilon = 1e-06
digit = 256
extra = 8
square = 4

vmem_spec = pl.BlockSpec(memory_space=pltpu.VMEM)
smem_spec = pl.BlockSpec(memory_space=pltpu.SMEM)
hbm_spec = pl.BlockSpec(memory_space=pltpu.HBM)


vmem_bytes = 64 * 1024 * 1024


def params(room):
    return pltpu.CompilerParams(vmem_limit_bytes=vmem_bytes - room * 1024)


def normalized(feat_ref):
    wide = feat_ref[...].astype(jnp.float32)
    squares = jnp.sum(wide * wide, axis=1, keepdims=True)
    return (wide * lax.rsqrt(squares + epsilon)).astype(jnp.bfloat16)


def normalize_kernel(*refs):
    rows = refs[0].shape[0]
    for index, feat_ref in enumerate(refs[:-1]):
        refs[-1][index * rows : (index + 1) * rows, :] = normalized(feat_ref)


def pack_kernel(feat_ref, label_ref, out_ref):
    rows, width = feat_ref.shape
    sets = label_ref.shape[0]
    out_ref[:rows, :] = normalized(feat_ref)
    labels = label_ref[...]
    digits = [labels // digit, labels % digit]
    line = lax.broadcasted_iota(jnp.int32, (extra, width), 0)
    packed = jnp.zeros((extra, width), jnp.float32)
    per_row = width // (2 * rows)
    for first in range(0, sets, per_row):
        pieces = [
            part[index : index + 1, :]
            for index in range(first, min(first + per_row, sets))
            for part in digits
        ]
        if len(pieces) * rows < width:
            pieces.append(jnp.zeros((1, width - len(pieces) * rows), jnp.int32))
        row = jnp.concatenate(pieces, axis=1).astype(jnp.float32)
        packed = jnp.where(line == first // per_row, row, packed)
    out_ref[rows:, :] = packed.astype(jnp.bfloat16)


def labels_of(packed_ref, index):
    rows = packed_ref.shape[0] - extra
    per_row = packed_ref.shape[1] // (2 * rows)
    line, start = index // per_row, index % per_row * 2 * rows
    digits = packed_ref[rows:, :].astype(jnp.float32)[line : line + 1, :].astype(jnp.int32)
    return digits[:, start : start + rows] * digit + digits[:, start + rows : start + 2 * rows]


def choose_kernel(place_ref, sampled_hbm, weight_hbm, low_ref, chosen_ref, sampled_ref, sems):
    part = chosen_ref.shape[0]
    first = place_ref[square] * part
    copy = pltpu.make_async_copy(sampled_hbm, sampled_ref, sems.at[0])
    copy.start()
    copy.wait()

    def start_rows(step, carry):
        for lane in range(8):
            row = step * 8 + lane
            pltpu.make_async_copy(
                weight_hbm.at[pl.ds(sampled_ref[first + row], 1), :],
                chosen_ref.at[pl.ds(row, 1), :],
                sems.at[1],
            ).start(priority=lane % 2)
        return carry

    lax.fori_loop(0, part // 8, start_rows, 0, unroll=4)
    pltpu.make_async_copy(weight_hbm.at[pl.ds(0, part), :], chosen_ref, sems.at[1]).wait()
    rows = chosen_ref[...]
    inverse = lax.rsqrt(jnp.sum(rows * rows, axis=1, keepdims=True) + epsilon)
    low_ref[:part, :] = (rows * inverse).astype(jnp.bfloat16) * logit_scale
    low_ref[part:, :] = jnp.zeros_like(low_ref[part:, :])


def logits_kernel(count, span, held, joined, place_ref, *refs):
    feats = refs[:held]
    if joined:
        rows, earlier_ref = refs[held : held + 2]
        exp_ref, stat_ref, every_ref, label_ref = refs[-4:]
        stat_ref[...] = earlier_ref[...]
    else:
        classes = refs[held : held + square]
        exp_ref, stat_ref, every_ref, label_ref, rows = refs[-5:]
        part = rows.shape[0] // square
        for side in range(square):
            rows[side * part : (side + 1) * part, :] = classes[side][:part, :]
    part = rows.shape[0] // square
    lanes = label_ref.shape[1]
    for index, (_, place, first, source, label_set) in enumerate(span):
        every_ref[index * lanes : (index + 1) * lanes, :] = feats[place][first : first + lanes, :]
        label_ref[index : index + 1, :] = labels_of(feats[source], label_set)
    line = lax.broadcasted_iota(jnp.int32, (part, lanes), 0)
    for pair in range(0, len(span), 2):
        scaled = lax.dot_general(
            rows[...],
            every_ref[pair * lanes : (pair + 2) * lanes, :],
            (((1,), (1,)), ((), ())),
            preferred_element_type=jnp.float32,
        )
        for index in (pair, pair + 1):
            start = (index - pair) * lanes
            labels = label_ref[index : index + 1, :]
            total = jnp.zeros((1, lanes), jnp.float32)
            target = jnp.zeros((1, lanes), jnp.float32)
            for side in range(square):
                lines = slice(side * part, (side + 1) * part)
                hit = labels - place_ref[side] == line
                tile = scaled[lines, start : start + lanes]
                exps = jnp.exp(
                    tile - jnp.where(hit, logit_scale + logit_scale * margin, logit_scale)
                )
                exp_ref[lines, index * lanes : (index + 1) * lanes] = exps
                total = total + jnp.sum(exps, axis=0, keepdims=True)
                target = target + jnp.sum(jnp.where(hit, tile, 0.0), axis=0, keepdims=True)
            group = place_ref[square + 1] ^ span[index][0]
            stat_ref[pl.ds(group, 1), :] = total
            stat_ref[pl.ds(count + group, 1), :] = target


def grads_kernel(count, replicas, spans, sides, place_ref, stat_ref, *refs):
    chunks = [refs[3 * index : 3 * index + 3] for index in range(len(spans))]
    refs = refs[3 * len(spans) :]
    outs, scratch = refs[: len(sides)], refs[-len(spans) :]
    part = chunks[0][0].shape[0] // square
    lanes = stat_ref.shape[1]
    scale = logit_scale / replicas
    group = place_ref[square + 1]
    if 0 in sides:
        refs[len(sides)][...] = (
            logit_scale
            + jnp.log(stat_ref[pl.ds(group, 1), :])
            - (stat_ref[pl.ds(count + group, 1), :] - logit_scale * margin)
        )
    line = lax.broadcasted_iota(jnp.int32, (part, lanes), 0)
    total = None
    for span, (exp_ref, every_ref, label_ref), grads in zip(spans, chunks, scratch):
        for index in range(len(span)):
            inverse = 1.0 / stat_ref[pl.ds(group ^ span[index][0], 1), :]
            columns = slice(index * lanes, (index + 1) * lanes)
            labels = label_ref[index : index + 1, :]
            for place, side in enumerate(sides):
                hit = labels - place_ref[side] == line
                exps = exp_ref[side * part : (side + 1) * part, columns]
                grads[place * part : (place + 1) * part, columns] = (
                    exps * inverse - jnp.where(hit, 1.0, 0.0)
                ).astype(jnp.bfloat16)
        product = jnp.dot(grads[...], every_ref[...], preferred_element_type=jnp.float32)
        total = product if total is None else total + product
    for index, out in enumerate(outs):
        out[...] = (total[index * part : (index + 1) * part, :] * scale).astype(out.dtype)


def finish_kernel(chosen_ref, own_ref, *refs):
    others, out_ref = refs[:-1], refs[-1]
    summed = own_ref[...]
    for other in others:
        summed = summed + other[...].astype(jnp.float32)
    rows = chosen_ref[...]
    inverse = lax.rsqrt(jnp.sum(rows * rows, axis=1, keepdims=True) + epsilon)
    unit = rows * inverse
    radial = jnp.sum(unit * summed, axis=1, keepdims=True)
    out_ref[...] = inverse * (summed - unit * radial)


def per_device(features, labels, weights, sampled):
    groups = lax.axis_size("cls")
    replicas = lax.axis_size("dp")
    local_rows, width = features.shape
    classes = sampled.shape[0]
    part = classes // replicas
    position = lax.axis_index("cls").astype(jnp.int32)
    replica = lax.axis_index("dp").astype(jnp.int32)
    place = jnp.stack(
        [(position ^ side) * classes + replica * part for side in range(square)]
        + [replica, position // square * replicas + replica]
    )

    def swap(value, chip_mask, core_mask):
        mask = chip_mask * replicas + core_mask
        return lax.ppermute(
            value, ("cls", "dp"), [(i, i ^ mask) for i in range(groups * replicas)]
        )

    bits = [(0, 1 << bit) for bit in range(replicas.bit_length() - 1)]
    far_bits = [(1 << bit, 0) for bit in range(2, groups.bit_length() - 1)]

    upper, marks = {0: features}, labels.reshape(1, local_rows)
    for bit, _ in far_bits[1:]:
        upper.update({mask | bit: swap(block, bit, 0) for mask, block in list(upper.items())})
        marks = jnp.concatenate([marks, swap(marks, bit, 0)], axis=0)
    near_raw = swap(features, square, 0)
    low_rows, chosen = pl.pallas_call(
        choose_kernel,
        out_shape=[
            jax.ShapeDtypeStruct((part + extra, width), jnp.bfloat16),
            jax.ShapeDtypeStruct((part, width), jnp.float32),
        ],
        in_specs=[smem_spec, hbm_spec, hbm_spec],
        out_specs=[vmem_spec] * 2,
        scratch_shapes=[pltpu.SMEM((classes,), jnp.int32), pltpu.SemaphoreType.DMA((2,))],
        compiler_params=params(11264),
        name="choose",
    )(place, sampled, weights)
    def spread(block):
        near = [block]
        for _, bit in bits:
            near = near + [swap(value, 0, bit) for value in near]
        return near

    tie = lax.optimization_barrier
    corner_rows, marks = tie((low_rows, marks))
    rows = [low_rows, swap(low_rows, 1, 0), swap(low_rows, 2, 0), swap(corner_rows, 3, 0)]
    tied, near_raw = tie(({mask: block for mask, block in upper.items() if mask}, near_raw))
    upper.update(tied)
    packed = {
        mask: pl.pallas_call(
            pack_kernel,
            out_shape=jax.ShapeDtypeStruct((local_rows + extra, width), jnp.bfloat16),
            in_specs=[vmem_spec] * 2,
            out_specs=vmem_spec,
            compiler_params=params(56 * 1024),
            name="pack",
        )(block, marks)
        for mask, block in upper.items()
        if mask
    }
    pair = pl.pallas_call(
        normalize_kernel,
        out_shape=jax.ShapeDtypeStruct((2 * local_rows, width), jnp.bfloat16),
        in_specs=[vmem_spec] * 2,
        out_specs=vmem_spec,
        compiler_params=params(56 * 1024),
        name="normalize",
    )(features, near_raw)
    passed = {mask | square: swap(block, square, 0) for mask, block in packed.items()}
    rows = tie(rows[::-1])[::-1]
    passed, rows = tie((passed, rows))
    ups = list(packed)
    held = [pair, *packed.values(), *passed.values()]
    spread_out = [spread(array) for array in held]
    count = groups // square * replicas
    order = list(upper)

    def entry(index, first_replica):
        mask, replica_bit = index // replicas * square, index % replicas
        up, beside = mask & ~square, bool(mask & square)
        base = (replica_bit - first_replica) * len(held) + 1 + beside * len(ups)
        source = base + ups.index(groups // 2)
        if up:
            return (index, base + ups.index(up), 0, source, order.index(up))
        return (index, base - 1 - beside * len(ups), beside * local_rows, source, 0)

    spans, arrays = [], []
    for some in (range(1), range(1, replicas)):
        spans.append(
            tuple(entry(index, some[0]) for index in range(count) if index % replicas in some)
        )
        arrays.append([copies[bit] for bit in some for copies in spread_out])
    chunks, carried = [], rows
    for joined, span in enumerate(spans):
        shapes = [
            jax.ShapeDtypeStruct((square * part, len(span) * local_rows), jnp.float32),
            jax.ShapeDtypeStruct((2 * count, local_rows), jnp.float32),
            jax.ShapeDtypeStruct((len(span) * local_rows, width), jnp.bfloat16),
            jax.ShapeDtypeStruct((len(span), local_rows), jnp.int32),
            jax.ShapeDtypeStruct((square * part, width), jnp.bfloat16),
        ][: 5 - joined]
        exps, stats, every, marks, *together = pl.pallas_call(
            functools.partial(logits_kernel, count, span, len(arrays[joined]), joined),
            out_shape=shapes,
            in_specs=[smem_spec] + [vmem_spec] * (len(arrays[joined]) + len(carried)),
            out_specs=[vmem_spec] * len(shapes),
            compiler_params=params(16 * 1024),
            name="logits",
        )(place, *arrays[joined], *carried)
        chunks, carried = chunks + [exps, every, marks], together + [stats]
    near = [(0, 0)]
    for chip_bit, core_bit in bits[:1] + far_bits[:1]:
        near = near + [(chip_mask | chip_bit, core_mask | core_bit) for chip_mask, core_mask in near]
    stats = sum((swap(stats, *masks) for masks in near[1:]), stats)
    for chip_mask, core_mask in bits[1:] + far_bits[1:]:
        stats = stats + swap(stats, chip_mask, core_mask)

    def grads(sides):
        kinds = [jnp.bfloat16 if side else jnp.float32 for side in sides]
        shapes = [jax.ShapeDtypeStruct((part, width), kind) for kind in kinds]
        if 0 in sides:
            shapes.append(jax.ShapeDtypeStruct((1, local_rows), jnp.float32))
        return pl.pallas_call(
            functools.partial(grads_kernel, count, replicas, spans, sides),
            out_shape=shapes,
            in_specs=[smem_spec] + [vmem_spec] * (1 + len(chunks)),
            out_specs=[vmem_spec] * len(shapes),
            scratch_shapes=[
                pltpu.VMEM((len(sides) * part, len(span) * local_rows), jnp.bfloat16)
                for span in spans
            ],
            compiler_params=params(16 * 1024),
            name="grads",
        )(place, stats, *chunks)

    away = [swap(block, side, 0) for side, block in enumerate(grads((1, 2, 3)), 1)]
    mine, loss = grads((0,))
    weight_grad = pl.pallas_call(
        finish_kernel,
        out_shape=jax.ShapeDtypeStruct((part, width), jnp.float32),
        in_specs=[vmem_spec] * (2 + len(away)),
        out_specs=vmem_spec,
        compiler_params=params(56 * 1024),
        name="finish",
    )(chosen, mine, *away)
    return (loss.reshape(local_rows), weight_grad)


def solution(mesh):
    in_specs = (P(("cls", "dp"), None), P(("cls", "dp")), P("cls", None), P("cls"))
    out_specs = (P(("cls", "dp")), P(("cls", "dp"), None))
    return jax.shard_map(
        per_device, mesh=mesh, in_specs=in_specs, out_specs=out_specs, check_vma=False
    )
```

```python
import functools

import jax
import jax.numpy as jnp
from jax import lax
from jax.experimental import pallas as pl
from jax.experimental.pallas import tpu as pltpu
from jax.sharding import PartitionSpec as P

logit_scale = 64.0
margin = 0.35
epsilon = 1e-06
digit = 256
extra = 8
square = 4

vmem_spec = pl.BlockSpec(memory_space=pltpu.VMEM)
smem_spec = pl.BlockSpec(memory_space=pltpu.SMEM)
hbm_spec = pl.BlockSpec(memory_space=pltpu.HBM)


vmem_bytes = 64 * 1024 * 1024


def params(room):
    return pltpu.CompilerParams(vmem_limit_bytes=vmem_bytes - room * 1024)


def normalized(feat_ref):
    wide = feat_ref[...].astype(jnp.float32)
    squares = jnp.sum(wide * wide, axis=1, keepdims=True)
    return (wide * lax.rsqrt(squares + epsilon)).astype(jnp.bfloat16)


def normalize_kernel(*refs):
    rows = refs[0].shape[0]
    for index, feat_ref in enumerate(refs[:-1]):
        refs[-1][index * rows : (index + 1) * rows, :] = normalized(feat_ref)


def pack_kernel(feat_ref, label_ref, out_ref):
    rows, width = feat_ref.shape
    sets = label_ref.shape[0]
    out_ref[:rows, :] = normalized(feat_ref)
    labels = label_ref[...]
    digits = [labels // digit, labels % digit]
    line = lax.broadcasted_iota(jnp.int32, (extra, width), 0)
    packed = jnp.zeros((extra, width), jnp.float32)
    per_row = width // (2 * rows)
    for first in range(0, sets, per_row):
        pieces = [
            part[index : index + 1, :]
            for index in range(first, min(first + per_row, sets))
            for part in digits
        ]
        if len(pieces) * rows < width:
            pieces.append(jnp.zeros((1, width - len(pieces) * rows), jnp.int32))
        row = jnp.concatenate(pieces, axis=1).astype(jnp.float32)
        packed = jnp.where(line == first // per_row, row, packed)
    out_ref[rows:, :] = packed.astype(jnp.bfloat16)


def labels_of(packed_ref, index):
    rows = packed_ref.shape[0] - extra
    per_row = packed_ref.shape[1] // (2 * rows)
    line, start = index // per_row, index % per_row * 2 * rows
    digits = packed_ref[rows:, :].astype(jnp.float32)[line : line + 1, :].astype(jnp.int32)
    return digits[:, start : start + rows] * digit + digits[:, start + rows : start + 2 * rows]


def choose_kernel(sampled_ref, weight_hbm, low_ref, chosen_ref, sem):
    part = chosen_ref.shape[0]

    def start_row(row, carry):
        pltpu.make_async_copy(
            weight_hbm.at[pl.ds(sampled_ref[row], 1), :],
            chosen_ref.at[pl.ds(row, 1), :],
            sem,
        ).start()
        return carry

    lax.fori_loop(0, part, start_row, 0, unroll=32)
    pltpu.make_async_copy(weight_hbm.at[pl.ds(0, part), :], chosen_ref, sem).wait()
    rows = chosen_ref[...]
    inverse = lax.rsqrt(jnp.sum(rows * rows, axis=1, keepdims=True) + epsilon)
    low_ref[:part, :] = (rows * inverse).astype(jnp.bfloat16) * logit_scale
    low_ref[part:, :] = jnp.zeros_like(low_ref[part:, :])


def logits_kernel(count, span, held, joined, place_ref, *refs):
    feats = refs[:held]
    if joined:
        rows, earlier_ref = refs[held : held + 2]
        exp_ref, stat_ref, every_ref, label_ref = refs[-4:]
        stat_ref[...] = earlier_ref[...]
    else:
        classes = refs[held : held + square]
        exp_ref, stat_ref, every_ref, label_ref, rows = refs[-5:]
        part = rows.shape[0] // square
        for side in range(square):
            rows[side * part : (side + 1) * part, :] = classes[side][:part, :]
    part = rows.shape[0] // square
    lanes = label_ref.shape[1]
    for index, (_, place, first, source, label_set) in enumerate(span):
        every_ref[index * lanes : (index + 1) * lanes, :] = feats[place][first : first + lanes, :]
        label_ref[index : index + 1, :] = labels_of(feats[source], label_set)
    line = lax.broadcasted_iota(jnp.int32, (part, lanes), 0)
    for pair in range(0, len(span), 2):
        scaled = lax.dot_general(
            rows[...],
            every_ref[pair * lanes : (pair + 2) * lanes, :],
            (((1,), (1,)), ((), ())),
            preferred_element_type=jnp.float32,
        )
        for index in (pair, pair + 1):
            start = (index - pair) * lanes
            labels = label_ref[index : index + 1, :]
            total = jnp.zeros((1, lanes), jnp.float32)
            target = jnp.zeros((1, lanes), jnp.float32)
            for side in range(square):
                lines = slice(side * part, (side + 1) * part)
                hit = labels - place_ref[side] == line
                tile = scaled[lines, start : start + lanes]
                exps = jnp.exp(
                    tile - jnp.where(hit, logit_scale + logit_scale * margin, logit_scale)
                )
                exp_ref[lines, index * lanes : (index + 1) * lanes] = exps
                total = total + jnp.sum(exps, axis=0, keepdims=True)
                target = target + jnp.sum(jnp.where(hit, tile, 0.0), axis=0, keepdims=True)
            group = place_ref[square + 1] ^ span[index][0]
            stat_ref[pl.ds(group, 1), :] = total
            stat_ref[pl.ds(count + group, 1), :] = target


def grads_kernel(count, replicas, spans, sides, place_ref, stat_ref, *refs):
    chunks = [refs[3 * index : 3 * index + 3] for index in range(len(spans))]
    refs = refs[3 * len(spans) :]
    outs, scratch = refs[: len(sides)], refs[-len(spans) :]
    part = chunks[0][0].shape[0] // square
    lanes = stat_ref.shape[1]
    scale = logit_scale / replicas
    group = place_ref[square + 1]
    if 0 in sides:
        refs[len(sides)][...] = (
            logit_scale
            + jnp.log(stat_ref[pl.ds(group, 1), :])
            - (stat_ref[pl.ds(count + group, 1), :] - logit_scale * margin)
        )
    line = lax.broadcasted_iota(jnp.int32, (part, lanes), 0)
    total = None
    for span, (exp_ref, every_ref, label_ref), grads in zip(spans, chunks, scratch):
        for index in range(len(span)):
            inverse = 1.0 / stat_ref[pl.ds(group ^ span[index][0], 1), :]
            columns = slice(index * lanes, (index + 1) * lanes)
            labels = label_ref[index : index + 1, :]
            for place, side in enumerate(sides):
                hit = labels - place_ref[side] == line
                exps = exp_ref[side * part : (side + 1) * part, columns]
                grads[place * part : (place + 1) * part, columns] = (
                    exps * inverse - jnp.where(hit, 1.0, 0.0)
                ).astype(jnp.bfloat16)
        product = jnp.dot(grads[...], every_ref[...], preferred_element_type=jnp.float32)
        total = product if total is None else total + product
    for index, out in enumerate(outs):
        out[...] = (total[index * part : (index + 1) * part, :] * scale).astype(out.dtype)


def finish_kernel(chosen_ref, own_ref, *refs):
    others, out_ref = refs[:-1], refs[-1]
    summed = own_ref[...]
    for other in others:
        summed = summed + other[...].astype(jnp.float32)
    rows = chosen_ref[...]
    inverse = lax.rsqrt(jnp.sum(rows * rows, axis=1, keepdims=True) + epsilon)
    unit = rows * inverse
    radial = jnp.sum(unit * summed, axis=1, keepdims=True)
    out_ref[...] = inverse * (summed - unit * radial)


def per_device(features, labels, weights, sampled):
    groups = lax.axis_size("cls")
    replicas = lax.axis_size("dp")
    local_rows, width = features.shape
    classes = sampled.shape[0]
    part = classes // replicas
    position = lax.axis_index("cls").astype(jnp.int32)
    replica = lax.axis_index("dp").astype(jnp.int32)
    place = jnp.stack(
        [(position ^ side) * classes + replica * part for side in range(square)]
        + [replica, position // square * replicas + replica]
    )

    def swap(value, chip_mask, core_mask):
        mask = chip_mask * replicas + core_mask
        return lax.ppermute(
            value, ("cls", "dp"), [(i, i ^ mask) for i in range(groups * replicas)]
        )

    bits = [(0, 1 << bit) for bit in range(replicas.bit_length() - 1)]
    far_bits = [(1 << bit, 0) for bit in range(2, groups.bit_length() - 1)]

    upper, marks = {0: features}, labels.reshape(1, local_rows)
    for bit, _ in far_bits[1:]:
        upper.update({mask | bit: swap(block, bit, 0) for mask, block in list(upper.items())})
        marks = jnp.concatenate([marks, swap(marks, bit, 0)], axis=0)
    near_raw = swap(features, square, 0)
    low_rows, chosen = pl.pallas_call(
        choose_kernel,
        out_shape=[
            jax.ShapeDtypeStruct((part + extra, width), jnp.bfloat16),
            jax.ShapeDtypeStruct((part, width), jnp.float32),
        ],
        in_specs=[smem_spec, hbm_spec],
        out_specs=[vmem_spec] * 2,
        scratch_shapes=[pltpu.SemaphoreType.DMA],
        compiler_params=params(11 * 1024),
        name="choose",
    )(lax.dynamic_slice_in_dim(sampled, replica * part, part), weights)
    def spread(block):
        near = [block]
        for _, bit in bits:
            near = near + [swap(value, 0, bit) for value in near]
        return near

    tie = lax.optimization_barrier
    corner_rows, marks = tie((low_rows, marks))
    rows = [low_rows, swap(low_rows, 1, 0), swap(low_rows, 2, 0), swap(corner_rows, 3, 0)]
    tied, near_raw = tie(({mask: block for mask, block in upper.items() if mask}, near_raw))
    upper.update(tied)
    packed = {
        mask: pl.pallas_call(
            pack_kernel,
            out_shape=jax.ShapeDtypeStruct((local_rows + extra, width), jnp.bfloat16),
            in_specs=[vmem_spec] * 2,
            out_specs=vmem_spec,
            compiler_params=params(56 * 1024),
            name="pack",
        )(block, marks)
        for mask, block in upper.items()
        if mask
    }
    pair = pl.pallas_call(
        normalize_kernel,
        out_shape=jax.ShapeDtypeStruct((2 * local_rows, width), jnp.bfloat16),
        in_specs=[vmem_spec] * 2,
        out_specs=vmem_spec,
        compiler_params=params(56 * 1024),
        name="normalize",
    )(features, near_raw)
    passed = {mask | square: swap(block, square, 0) for mask, block in packed.items()}
    rows = tie(rows[::-1])[::-1]
    passed, rows = tie((passed, rows))
    ups = list(packed)
    held = [pair, *packed.values(), *passed.values()]
    spread_out = [spread(array) for array in held]
    count = groups // square * replicas
    order = list(upper)

    def entry(index, first_replica):
        mask, replica_bit = index // replicas * square, index % replicas
        up, beside = mask & ~square, bool(mask & square)
        base = (replica_bit - first_replica) * len(held) + 1 + beside * len(ups)
        source = base + ups.index(groups // 2)
        if up:
            return (index, base + ups.index(up), 0, source, order.index(up))
        return (index, base - 1 - beside * len(ups), beside * local_rows, source, 0)

    spans, arrays = [], []
    for some in (range(1), range(1, replicas)):
        spans.append(
            tuple(entry(index, some[0]) for index in range(count) if index % replicas in some)
        )
        arrays.append([copies[bit] for bit in some for copies in spread_out])
    chunks, carried = [], rows
    for joined, span in enumerate(spans):
        shapes = [
            jax.ShapeDtypeStruct((square * part, len(span) * local_rows), jnp.float32),
            jax.ShapeDtypeStruct((2 * count, local_rows), jnp.float32),
            jax.ShapeDtypeStruct((len(span) * local_rows, width), jnp.bfloat16),
            jax.ShapeDtypeStruct((len(span), local_rows), jnp.int32),
            jax.ShapeDtypeStruct((square * part, width), jnp.bfloat16),
        ][: 5 - joined]
        exps, stats, every, marks, *together = pl.pallas_call(
            functools.partial(logits_kernel, count, span, len(arrays[joined]), joined),
            out_shape=shapes,
            in_specs=[smem_spec] + [vmem_spec] * (len(arrays[joined]) + len(carried)),
            out_specs=[vmem_spec] * len(shapes),
            compiler_params=params(16 * 1024),
            name="logits",
        )(place, *arrays[joined], *carried)
        chunks, carried = chunks + [exps, every, marks], together + [stats]
    near = [(0, 0)]
    for chip_bit, core_bit in bits[:1] + far_bits[:1]:
        near = near + [(chip_mask | chip_bit, core_mask | core_bit) for chip_mask, core_mask in near]
    stats = sum((swap(stats, *masks) for masks in near[1:]), stats)
    for chip_mask, core_mask in bits[1:] + far_bits[1:]:
        stats = stats + swap(stats, chip_mask, core_mask)

    def grads(sides):
        kinds = [jnp.bfloat16 if side else jnp.float32 for side in sides]
        shapes = [jax.ShapeDtypeStruct((part, width), kind) for kind in kinds]
        if 0 in sides:
            shapes.append(jax.ShapeDtypeStruct((1, local_rows), jnp.float32))
        return pl.pallas_call(
            functools.partial(grads_kernel, count, replicas, spans, sides),
            out_shape=shapes,
            in_specs=[smem_spec] + [vmem_spec] * (1 + len(chunks)),
            out_specs=[vmem_spec] * len(shapes),
            scratch_shapes=[
                pltpu.VMEM((len(sides) * part, len(span) * local_rows), jnp.bfloat16)
                for span in spans
            ],
            compiler_params=params(16 * 1024),
            name="grads",
        )(place, stats, *chunks)

    away = [swap(block, side, 0) for side, block in enumerate(grads((1, 2, 3)), 1)]
    mine, loss = grads((0,))
    weight_grad = pl.pallas_call(
        finish_kernel,
        out_shape=jax.ShapeDtypeStruct((part, width), jnp.float32),
        in_specs=[vmem_spec] * (2 + len(away)),
        out_specs=vmem_spec,
        compiler_params=params(56 * 1024),
        name="finish",
    )(chosen, mine, *away)
    return (loss.reshape(local_rows), weight_grad)


def solution(mesh):
    in_specs = (P(("cls", "dp"), None), P(("cls", "dp")), P("cls", None), P("cls"))
    out_specs = (P(("cls", "dp")), P(("cls", "dp"), None))
    return jax.shard_map(
        per_device, mesh=mesh, in_specs=in_specs, out_specs=out_specs, check_vma=False
    )
```

```python
import functools

import jax
import jax.numpy as jnp
from jax import lax
from jax.experimental import pallas as pl
from jax.experimental.pallas import tpu as pltpu
from jax.sharding import PartitionSpec as P

logit_scale = 64.0
margin = 0.35
epsilon = 1e-06
digit = 256
extra = 8
square = 4

vmem_spec = pl.BlockSpec(memory_space=pltpu.VMEM)
smem_spec = pl.BlockSpec(memory_space=pltpu.SMEM)
hbm_spec = pl.BlockSpec(memory_space=pltpu.HBM)


vmem_bytes = 64 * 1024 * 1024


def params(room):
    return pltpu.CompilerParams(vmem_limit_bytes=vmem_bytes - room * 1024)


def normalized(feat_ref):
    wide = feat_ref[...].astype(jnp.float32)
    squares = jnp.sum(wide * wide, axis=1, keepdims=True)
    return (wide * lax.rsqrt(squares + epsilon)).astype(jnp.bfloat16)


def normalize_kernel(*refs):
    rows = refs[0].shape[0]
    for index, feat_ref in enumerate(refs[:-1]):
        refs[-1][index * rows : (index + 1) * rows, :] = normalized(feat_ref)


def pack_kernel(feat_ref, label_ref, out_ref):
    rows, width = feat_ref.shape
    sets = label_ref.shape[0]
    out_ref[:rows, :] = normalized(feat_ref)
    labels = label_ref[...]
    digits = [labels // digit, labels % digit]
    line = lax.broadcasted_iota(jnp.int32, (extra, width), 0)
    packed = jnp.zeros((extra, width), jnp.float32)
    per_row = width // (2 * rows)
    for first in range(0, sets, per_row):
        pieces = [
            part[index : index + 1, :]
            for index in range(first, min(first + per_row, sets))
            for part in digits
        ]
        if len(pieces) * rows < width:
            pieces.append(jnp.zeros((1, width - len(pieces) * rows), jnp.int32))
        row = jnp.concatenate(pieces, axis=1).astype(jnp.float32)
        packed = jnp.where(line == first // per_row, row, packed)
    out_ref[rows:, :] = packed.astype(jnp.bfloat16)


def labels_of(packed_ref, index):
    rows = packed_ref.shape[0] - extra
    per_row = packed_ref.shape[1] // (2 * rows)
    line, start = index // per_row, index % per_row * 2 * rows
    digits = packed_ref[rows:, :].astype(jnp.float32)[line : line + 1, :].astype(jnp.int32)
    return digits[:, start : start + rows] * digit + digits[:, start + rows : start + 2 * rows]


def choose_kernel(sampled_ref, weight_hbm, low_ref, chosen_ref, sem):
    part = chosen_ref.shape[0]

    def start_row(row, carry):
        pltpu.make_async_copy(
            weight_hbm.at[pl.ds(sampled_ref[row], 1), :],
            chosen_ref.at[pl.ds(row, 1), :],
            sem,
        ).start()
        return carry

    lax.fori_loop(0, part, start_row, 0, unroll=32)
    pltpu.make_async_copy(weight_hbm.at[pl.ds(0, part), :], chosen_ref, sem).wait()
    rows = chosen_ref[...]
    inverse = lax.rsqrt(jnp.sum(rows * rows, axis=1, keepdims=True) + epsilon)
    low_ref[:part, :] = (rows * inverse).astype(jnp.bfloat16) * logit_scale
    low_ref[part:, :] = jnp.zeros_like(low_ref[part:, :])


def logits_kernel(count, span, held, joined, place_ref, *refs):
    feats = refs[:held]
    if joined:
        rows, earlier_ref = refs[held : held + 2]
        exp_ref, stat_ref, every_ref, label_ref = refs[-4:]
        stat_ref[...] = earlier_ref[...]
    else:
        classes = refs[held : held + square]
        exp_ref, stat_ref, every_ref, label_ref, rows = refs[-5:]
        part = rows.shape[0] // square
        for side in range(square):
            rows[side * part : (side + 1) * part, :] = classes[side][:part, :]
    part = rows.shape[0] // square
    lanes = label_ref.shape[1]
    for index, (_, place, first, source, label_set) in enumerate(span):
        every_ref[index * lanes : (index + 1) * lanes, :] = feats[place][first : first + lanes, :]
        label_ref[index : index + 1, :] = labels_of(feats[source], label_set)
    line = lax.broadcasted_iota(jnp.int32, (part, lanes), 0)
    for pair in range(0, len(span), 2):
        scaled = lax.dot_general(
            rows[...],
            every_ref[pair * lanes : (pair + 2) * lanes, :],
            (((1,), (1,)), ((), ())),
            preferred_element_type=jnp.float32,
        )
        for index in (pair, pair + 1):
            start = (index - pair) * lanes
            labels = label_ref[index : index + 1, :]
            total = jnp.zeros((8, lanes), jnp.float32)
            target = jnp.zeros((8, lanes), jnp.float32)
            for side in range(square):
                lines = slice(side * part, (side + 1) * part)
                hit = labels - place_ref[side] == line
                tile = scaled[lines, start : start + lanes]
                exps = jnp.exp(
                    tile - jnp.where(hit, logit_scale + logit_scale * margin, logit_scale)
                )
                exp_ref[lines, index * lanes : (index + 1) * lanes] = exps
                total = total + jnp.sum(exps.reshape(-1, 8, lanes), axis=0)
                target = target + jnp.sum(jnp.where(hit, tile, 0.0).reshape(-1, 8, lanes), axis=0)
            group = place_ref[square + 1] ^ span[index][0]
            stat_ref[pl.ds(group, 1), :] = jnp.sum(total, axis=0, keepdims=True)
            stat_ref[pl.ds(count + group, 1), :] = jnp.sum(target, axis=0, keepdims=True)


def grads_kernel(count, replicas, spans, sides, place_ref, stat_ref, *refs):
    chunks = [refs[3 * index : 3 * index + 3] for index in range(len(spans))]
    refs = refs[3 * len(spans) :]
    outs, scratch = refs[: len(sides)], refs[-len(spans) :]
    part = chunks[0][0].shape[0] // square
    lanes = stat_ref.shape[1]
    scale = logit_scale / replicas
    group = place_ref[square + 1]
    if 0 in sides:
        refs[len(sides)][...] = (
            logit_scale
            + jnp.log(stat_ref[pl.ds(group, 1), :])
            - (stat_ref[pl.ds(count + group, 1), :] - logit_scale * margin)
        )
    line = lax.broadcasted_iota(jnp.int32, (part, lanes), 0)
    total = None
    for span, (exp_ref, every_ref, label_ref), grads in zip(spans, chunks, scratch):
        for index in range(len(span)):
            inverse = 1.0 / stat_ref[pl.ds(group ^ span[index][0], 1), :]
            columns = slice(index * lanes, (index + 1) * lanes)
            labels = label_ref[index : index + 1, :]
            for place, side in enumerate(sides):
                hit = labels - place_ref[side] == line
                exps = exp_ref[side * part : (side + 1) * part, columns]
                grads[place * part : (place + 1) * part, columns] = (
                    exps * inverse - jnp.where(hit, 1.0, 0.0)
                ).astype(jnp.bfloat16)
        product = jnp.dot(grads[...], every_ref[...], preferred_element_type=jnp.float32)
        total = product if total is None else total + product
    for index, out in enumerate(outs):
        out[...] = (total[index * part : (index + 1) * part, :] * scale).astype(out.dtype)


def finish_kernel(chosen_ref, own_ref, *refs):
    others, out_ref = refs[:-1], refs[-1]
    summed = own_ref[...]
    for other in others:
        summed = summed + other[...].astype(jnp.float32)
    rows = chosen_ref[...]
    inverse = lax.rsqrt(jnp.sum(rows * rows, axis=1, keepdims=True) + epsilon)
    unit = rows * inverse
    radial = jnp.sum(unit * summed, axis=1, keepdims=True)
    out_ref[...] = inverse * (summed - unit * radial)


def per_device(features, labels, weights, sampled):
    groups = lax.axis_size("cls")
    replicas = lax.axis_size("dp")
    local_rows, width = features.shape
    classes = sampled.shape[0]
    part = classes // replicas
    position = lax.axis_index("cls").astype(jnp.int32)
    replica = lax.axis_index("dp").astype(jnp.int32)
    place = jnp.stack(
        [(position ^ side) * classes + replica * part for side in range(square)]
        + [replica, position // square * replicas + replica]
    )

    def swap(value, chip_mask, core_mask):
        mask = chip_mask * replicas + core_mask
        return lax.ppermute(
            value, ("cls", "dp"), [(i, i ^ mask) for i in range(groups * replicas)]
        )

    bits = [(0, 1 << bit) for bit in range(replicas.bit_length() - 1)]
    far_bits = [(1 << bit, 0) for bit in range(2, groups.bit_length() - 1)]

    upper, marks = {0: features}, labels.reshape(1, local_rows)
    for bit, _ in far_bits[1:]:
        upper.update({mask | bit: swap(block, bit, 0) for mask, block in list(upper.items())})
        marks = jnp.concatenate([marks, swap(marks, bit, 0)], axis=0)
    near_raw = swap(features, square, 0)
    low_rows, chosen = pl.pallas_call(
        choose_kernel,
        out_shape=[
            jax.ShapeDtypeStruct((part + extra, width), jnp.bfloat16),
            jax.ShapeDtypeStruct((part, width), jnp.float32),
        ],
        in_specs=[smem_spec, hbm_spec],
        out_specs=[vmem_spec] * 2,
        scratch_shapes=[pltpu.SemaphoreType.DMA],
        compiler_params=params(11 * 1024),
        name="choose",
    )(lax.dynamic_slice_in_dim(sampled, replica * part, part), weights)
    def spread(block):
        near = [block]
        for _, bit in bits:
            near = near + [swap(value, 0, bit) for value in near]
        return near

    tie = lax.optimization_barrier
    corner_rows, marks = tie((low_rows, marks))
    rows = [low_rows, swap(low_rows, 1, 0), swap(low_rows, 2, 0), swap(corner_rows, 3, 0)]
    tied, near_raw = tie(({mask: block for mask, block in upper.items() if mask}, near_raw))
    upper.update(tied)
    packed = {
        mask: pl.pallas_call(
            pack_kernel,
            out_shape=jax.ShapeDtypeStruct((local_rows + extra, width), jnp.bfloat16),
            in_specs=[vmem_spec] * 2,
            out_specs=vmem_spec,
            compiler_params=params(56 * 1024),
            name="pack",
        )(block, marks)
        for mask, block in upper.items()
        if mask
    }
    pair = pl.pallas_call(
        normalize_kernel,
        out_shape=jax.ShapeDtypeStruct((2 * local_rows, width), jnp.bfloat16),
        in_specs=[vmem_spec] * 2,
        out_specs=vmem_spec,
        compiler_params=params(56 * 1024),
        name="normalize",
    )(features, near_raw)
    passed = {mask | square: swap(block, square, 0) for mask, block in packed.items()}
    rows = tie(rows[::-1])[::-1]
    passed, rows = tie((passed, rows))
    ups = list(packed)
    held = [pair, *packed.values(), *passed.values()]
    spread_out = [spread(array) for array in held]
    count = groups // square * replicas
    order = list(upper)

    def entry(index, first_replica):
        mask, replica_bit = index // replicas * square, index % replicas
        up, beside = mask & ~square, bool(mask & square)
        base = (replica_bit - first_replica) * len(held) + 1 + beside * len(ups)
        source = base + ups.index(groups // 2)
        if up:
            return (index, base + ups.index(up), 0, source, order.index(up))
        return (index, base - 1 - beside * len(ups), beside * local_rows, source, 0)

    spans, arrays = [], []
    for some in (range(1), range(1, replicas)):
        spans.append(
            tuple(entry(index, some[0]) for index in range(count) if index % replicas in some)
        )
        arrays.append([copies[bit] for bit in some for copies in spread_out])
    chunks, carried = [], rows
    for joined, span in enumerate(spans):
        shapes = [
            jax.ShapeDtypeStruct((square * part, len(span) * local_rows), jnp.float32),
            jax.ShapeDtypeStruct((2 * count, local_rows), jnp.float32),
            jax.ShapeDtypeStruct((len(span) * local_rows, width), jnp.bfloat16),
            jax.ShapeDtypeStruct((len(span), local_rows), jnp.int32),
            jax.ShapeDtypeStruct((square * part, width), jnp.bfloat16),
        ][: 5 - joined]
        exps, stats, every, marks, *together = pl.pallas_call(
            functools.partial(logits_kernel, count, span, len(arrays[joined]), joined),
            out_shape=shapes,
            in_specs=[smem_spec] + [vmem_spec] * (len(arrays[joined]) + len(carried)),
            out_specs=[vmem_spec] * len(shapes),
            compiler_params=params(16 * 1024),
            name="logits",
        )(place, *arrays[joined], *carried)
        chunks, carried = chunks + [exps, every, marks], together + [stats]
    near = [(0, 0)]
    for chip_bit, core_bit in bits[:1] + far_bits[:1]:
        near = near + [(chip_mask | chip_bit, core_mask | core_bit) for chip_mask, core_mask in near]
    stats = sum((swap(stats, *masks) for masks in near[1:]), stats)
    for chip_mask, core_mask in bits[1:] + far_bits[1:]:
        stats = stats + swap(stats, chip_mask, core_mask)

    def grads(sides):
        kinds = [jnp.bfloat16 if side else jnp.float32 for side in sides]
        shapes = [jax.ShapeDtypeStruct((part, width), kind) for kind in kinds]
        if 0 in sides:
            shapes.append(jax.ShapeDtypeStruct((1, local_rows), jnp.float32))
        return pl.pallas_call(
            functools.partial(grads_kernel, count, replicas, spans, sides),
            out_shape=shapes,
            in_specs=[smem_spec] + [vmem_spec] * (1 + len(chunks)),
            out_specs=[vmem_spec] * len(shapes),
            scratch_shapes=[
                pltpu.VMEM((len(sides) * part, len(span) * local_rows), jnp.bfloat16)
                for span in spans
            ],
            compiler_params=params(16 * 1024),
            name="grads",
        )(place, stats, *chunks)

    away = [swap(block, side, 0) for side, block in enumerate(grads((1, 2, 3)), 1)]
    mine, loss = grads((0,))
    weight_grad = pl.pallas_call(
        finish_kernel,
        out_shape=jax.ShapeDtypeStruct((part, width), jnp.float32),
        in_specs=[vmem_spec] * (2 + len(away)),
        out_specs=vmem_spec,
        compiler_params=params(56 * 1024),
        name="finish",
    )(chosen, mine, *away)
    return (loss.reshape(local_rows), weight_grad)


def solution(mesh):
    in_specs = (P(("cls", "dp"), None), P(("cls", "dp")), P("cls", None), P("cls"))
    out_specs = (P(("cls", "dp")), P(("cls", "dp"), None))
    return jax.shard_map(
        per_device, mesh=mesh, in_specs=in_specs, out_specs=out_specs, check_vma=False
    )
```

```python
import functools

import jax
import jax.numpy as jnp
from jax import lax
from jax.experimental import pallas as pl
from jax.experimental.pallas import tpu as pltpu
from jax.sharding import PartitionSpec as P

logit_scale = 64.0
margin = 0.35
epsilon = 1e-06
digit = 256
extra = 8
square = 4

vmem_spec = pl.BlockSpec(memory_space=pltpu.VMEM)
smem_spec = pl.BlockSpec(memory_space=pltpu.SMEM)
hbm_spec = pl.BlockSpec(memory_space=pltpu.HBM)


vmem_bytes = 64 * 1024 * 1024


def params(room):
    return pltpu.CompilerParams(vmem_limit_bytes=vmem_bytes - room * 1024)


def normalized(feat_ref):
    wide = feat_ref[...].astype(jnp.float32)
    squares = jnp.sum(wide * wide, axis=1, keepdims=True)
    return (wide * lax.rsqrt(squares + epsilon)).astype(jnp.bfloat16)


def normalize_kernel(*refs):
    rows = refs[0].shape[0]
    for index, feat_ref in enumerate(refs[:-1]):
        refs[-1][index * rows : (index + 1) * rows, :] = normalized(feat_ref)


def pack_kernel(feat_ref, label_ref, out_ref):
    rows, width = feat_ref.shape
    sets = label_ref.shape[0]
    out_ref[:rows, :] = normalized(feat_ref)
    labels = label_ref[...]
    digits = [labels // digit, labels % digit]
    line = lax.broadcasted_iota(jnp.int32, (extra, width), 0)
    packed = jnp.zeros((extra, width), jnp.float32)
    per_row = width // (2 * rows)
    for first in range(0, sets, per_row):
        pieces = [
            part[index : index + 1, :]
            for index in range(first, min(first + per_row, sets))
            for part in digits
        ]
        if len(pieces) * rows < width:
            pieces.append(jnp.zeros((1, width - len(pieces) * rows), jnp.int32))
        row = jnp.concatenate(pieces, axis=1).astype(jnp.float32)
        packed = jnp.where(line == first // per_row, row, packed)
    out_ref[rows:, :] = packed.astype(jnp.bfloat16)


def labels_of(packed_ref, index):
    rows = packed_ref.shape[0] - extra
    per_row = packed_ref.shape[1] // (2 * rows)
    line, start = index // per_row, index % per_row * 2 * rows
    digits = packed_ref[rows:, :].astype(jnp.float32)[line : line + 1, :].astype(jnp.int32)
    return digits[:, start : start + rows] * digit + digits[:, start + rows : start + 2 * rows]


def choose_kernel(sampled_ref, weight_hbm, low_ref, chosen_ref, sem):
    part = chosen_ref.shape[0]

    def start_row(row, carry):
        pltpu.make_async_copy(
            weight_hbm.at[pl.ds(sampled_ref[row], 1), :],
            chosen_ref.at[pl.ds(row, 1), :],
            sem,
        ).start()
        return carry

    lax.fori_loop(0, part, start_row, 0, unroll=32)
    pltpu.make_async_copy(weight_hbm.at[pl.ds(0, part), :], chosen_ref, sem).wait()
    rows = chosen_ref[...]
    inverse = lax.rsqrt(jnp.sum(rows * rows, axis=1, keepdims=True) + epsilon)
    low_ref[:part, :] = (rows * inverse).astype(jnp.bfloat16) * logit_scale
    low_ref[part:, :] = jnp.zeros_like(low_ref[part:, :])


def logits_kernel(count, span, held, joined, place_ref, *refs):
    feats = refs[:held]
    if joined:
        rows, earlier_ref = refs[held : held + 2]
        exp_ref, stat_ref, every_ref, label_ref = refs[-4:]
        stat_ref[...] = earlier_ref[...]
    else:
        classes = refs[held : held + square]
        exp_ref, stat_ref, every_ref, label_ref, rows = refs[-5:]
        part = rows.shape[0] // square
        for side in range(square):
            rows[side * part : (side + 1) * part, :] = classes[side][:part, :]
    part = rows.shape[0] // square
    lanes = label_ref.shape[1]
    for index, (_, place, first, source, label_set) in enumerate(span):
        every_ref[index * lanes : (index + 1) * lanes, :] = feats[place][first : first + lanes, :]
        label_ref[index : index + 1, :] = labels_of(feats[source], label_set)
    line = lax.broadcasted_iota(jnp.int32, (part, lanes), 0)
    for pair in range(0, len(span), 2):
        scaled = lax.dot_general(
            rows[...],
            every_ref[pair * lanes : (pair + 2) * lanes, :],
            (((1,), (1,)), ((), ())),
            preferred_element_type=jnp.float32,
        )
        for index in (pair, pair + 1):
            start = (index - pair) * lanes
            labels = label_ref[index : index + 1, :]
            total = jnp.zeros((1, lanes), jnp.float32)
            target = jnp.zeros((1, lanes), jnp.float32)
            for side in range(square):
                lines = slice(side * part, (side + 1) * part)
                hit = labels - place_ref[side] == line
                tile = scaled[lines, start : start + lanes]
                exps = jnp.exp(
                    tile - jnp.where(hit, logit_scale + logit_scale * margin, logit_scale)
                )
                exp_ref[lines, index * lanes : (index + 1) * lanes] = exps
                total = total + jnp.sum(exps, axis=0, keepdims=True)
                target = target + jnp.sum(jnp.where(hit, tile, 0.0), axis=0, keepdims=True)
            group = place_ref[square + 1] ^ span[index][0]
            stat_ref[pl.ds(group, 1), :] = total
            stat_ref[pl.ds(count + group, 1), :] = target


def grads_kernel(count, replicas, spans, sides, place_ref, stat_ref, *refs):
    chunks = [refs[3 * index : 3 * index + 3] for index in range(len(spans))]
    refs = refs[3 * len(spans) :]
    outs, scratch = refs[: len(sides)], refs[-len(spans) :]
    part = chunks[0][0].shape[0] // square
    lanes = stat_ref.shape[1]
    scale = logit_scale / replicas
    group = place_ref[square + 1]
    if 0 in sides:
        refs[len(sides)][...] = (
            logit_scale
            + jnp.log(stat_ref[pl.ds(group, 1), :])
            - (stat_ref[pl.ds(count + group, 1), :] - logit_scale * margin)
        )
    line = lax.broadcasted_iota(jnp.int32, (part, lanes), 0)
    total = None
    for span, (exp_ref, every_ref, label_ref), grads in zip(spans, chunks, scratch):
        for index in range(len(span)):
            inverse = 1.0 / stat_ref[pl.ds(group ^ span[index][0], 1), :]
            columns = slice(index * lanes, (index + 1) * lanes)
            labels = label_ref[index : index + 1, :]
            for place, side in enumerate(sides):
                hit = labels - place_ref[side] == line
                exps = exp_ref[side * part : (side + 1) * part, columns]
                grads[place * part : (place + 1) * part, columns] = (
                    exps * inverse - jnp.where(hit, 1.0, 0.0)
                ).astype(jnp.bfloat16)
        product = jnp.dot(grads[...], every_ref[...], preferred_element_type=jnp.float32)
        total = product if total is None else total + product
    for index, out in enumerate(outs):
        out[...] = (total[index * part : (index + 1) * part, :] * scale).astype(out.dtype)


def finish_kernel(chosen_ref, own_ref, *refs):
    others, out_ref = refs[:-1], refs[-1]
    summed = own_ref[...]
    for other in others:
        summed = summed + other[...].astype(jnp.float32)
    rows = chosen_ref[...]
    inverse = lax.rsqrt(jnp.sum(rows * rows, axis=1, keepdims=True) + epsilon)
    unit = rows * inverse
    radial = jnp.sum(unit * summed, axis=1, keepdims=True)
    out_ref[...] = inverse * (summed - unit * radial)


def per_device(features, labels, weights, sampled):
    groups = lax.axis_size("cls")
    replicas = lax.axis_size("dp")
    local_rows, width = features.shape
    classes = sampled.shape[0]
    part = classes // replicas
    position = lax.axis_index("cls").astype(jnp.int32)
    replica = lax.axis_index("dp").astype(jnp.int32)
    place = jnp.stack(
        [(position ^ side) * classes + replica * part for side in range(square)]
        + [replica, position // square * replicas + replica]
    )

    def swap(value, chip_mask, core_mask):
        mask = chip_mask * replicas + core_mask
        return lax.ppermute(
            value, ("cls", "dp"), [(i, i ^ mask) for i in range(groups * replicas)]
        )

    bits = [(0, 1 << bit) for bit in range(replicas.bit_length() - 1)]
    far_bits = [(1 << bit, 0) for bit in range(2, groups.bit_length() - 1)]

    upper, marks = {0: features}, labels.reshape(1, local_rows)
    for bit, _ in far_bits[1:]:
        upper.update({mask | bit: swap(block, bit, 0) for mask, block in list(upper.items())})
        marks = jnp.concatenate([marks, swap(marks, bit, 0)], axis=0)
    near_raw = swap(features, square, 0)
    low_rows, chosen = pl.pallas_call(
        choose_kernel,
        out_shape=[
            jax.ShapeDtypeStruct((part + extra, width), jnp.bfloat16),
            jax.ShapeDtypeStruct((part, width), jnp.float32),
        ],
        in_specs=[smem_spec, hbm_spec],
        out_specs=[vmem_spec] * 2,
        scratch_shapes=[pltpu.SemaphoreType.DMA],
        compiler_params=params(11 * 1024),
        name="choose",
    )(lax.dynamic_slice_in_dim(sampled, replica * part, part), weights)
    def spread(block):
        near = [block]
        for _, bit in bits:
            near = near + [swap(value, 0, bit) for value in near]
        return near

    tie = lax.optimization_barrier
    corner_rows, marks = tie((low_rows, marks))
    rows = [low_rows, swap(low_rows, 1, 0), swap(low_rows, 2, 0), swap(corner_rows, 3, 0)]
    tied, near_raw = tie(({mask: block for mask, block in upper.items() if mask}, near_raw))
    upper.update(tied)
    packed = {
        mask: pl.pallas_call(
            pack_kernel,
            out_shape=jax.ShapeDtypeStruct((local_rows + extra, width), jnp.bfloat16),
            in_specs=[vmem_spec] * 2,
            out_specs=vmem_spec,
            compiler_params=params(56 * 1024),
            name="pack",
        )(block, marks)
        for mask, block in upper.items()
        if mask
    }
    pair = pl.pallas_call(
        normalize_kernel,
        out_shape=jax.ShapeDtypeStruct((2 * local_rows, width), jnp.bfloat16),
        in_specs=[vmem_spec] * 2,
        out_specs=vmem_spec,
        compiler_params=params(56 * 1024),
        name="normalize",
    )(features, near_raw)
    passed = {mask | square: swap(block, square, 0) for mask, block in packed.items()}
    rows = tie(rows[::-1])[::-1]
    passed, rows = tie((passed, rows))
    ups = list(packed)
    held = [pair, *packed.values(), *passed.values()]
    spread_out = [spread(array) for array in held]
    count = groups // square * replicas
    order = list(upper)

    def entry(index, first_replica):
        mask, replica_bit = index // replicas * square, index % replicas
        up, beside = mask & ~square, bool(mask & square)
        base = (replica_bit - first_replica) * len(held) + 1 + beside * len(ups)
        source = base + ups.index(groups // 2)
        if up:
            return (index, base + ups.index(up), 0, source, order.index(up))
        return (index, base - 1 - beside * len(ups), beside * local_rows, source, 0)

    spans, arrays = [], []
    for some in (range(1), range(1, replicas)):
        spans.append(
            tuple(entry(index, some[0]) for index in range(count) if index % replicas in some)
        )
        arrays.append([copies[bit] for bit in some for copies in spread_out])
    chunks, carried = [], rows
    for joined, span in enumerate(spans):
        shapes = [
            jax.ShapeDtypeStruct((square * part, len(span) * local_rows), jnp.float32),
            jax.ShapeDtypeStruct((2 * count, local_rows), jnp.float32),
            jax.ShapeDtypeStruct((len(span) * local_rows, width), jnp.bfloat16),
            jax.ShapeDtypeStruct((len(span), local_rows), jnp.int32),
            jax.ShapeDtypeStruct((square * part, width), jnp.bfloat16),
        ][: 5 - joined]
        exps, stats, every, marks, *together = pl.pallas_call(
            functools.partial(logits_kernel, count, span, len(arrays[joined]), joined),
            out_shape=shapes,
            in_specs=[smem_spec] + [vmem_spec] * (len(arrays[joined]) + len(carried)),
            out_specs=[vmem_spec] * len(shapes),
            compiler_params=params(16 * 1024),
            name="logits",
        )(place, *arrays[joined], *carried)
        chunks, carried = chunks + [exps, every, marks], together + [stats]
    for chip_mask, core_mask in bits:
        stats = stats + swap(stats, chip_mask, core_mask)
    stats = sum((swap(stats, mask, 0) for mask in range(square, groups, square)), stats)

    def grads(sides):
        kinds = [jnp.bfloat16 if side else jnp.float32 for side in sides]
        shapes = [jax.ShapeDtypeStruct((part, width), kind) for kind in kinds]
        if 0 in sides:
            shapes.append(jax.ShapeDtypeStruct((1, local_rows), jnp.float32))
        return pl.pallas_call(
            functools.partial(grads_kernel, count, replicas, spans, sides),
            out_shape=shapes,
            in_specs=[smem_spec] + [vmem_spec] * (1 + len(chunks)),
            out_specs=[vmem_spec] * len(shapes),
            scratch_shapes=[
                pltpu.VMEM((len(sides) * part, len(span) * local_rows), jnp.bfloat16)
                for span in spans
            ],
            compiler_params=params(16 * 1024),
            name="grads",
        )(place, stats, *chunks)

    away = [swap(block, side, 0) for side, block in enumerate(grads((1, 2, 3)), 1)]
    mine, loss = grads((0,))
    weight_grad = pl.pallas_call(
        finish_kernel,
        out_shape=jax.ShapeDtypeStruct((part, width), jnp.float32),
        in_specs=[vmem_spec] * (2 + len(away)),
        out_specs=vmem_spec,
        compiler_params=params(56 * 1024),
        name="finish",
    )(chosen, mine, *away)
    return (loss.reshape(local_rows), weight_grad)


def solution(mesh):
    in_specs = (P(("cls", "dp"), None), P(("cls", "dp")), P("cls", None), P("cls"))
    out_specs = (P(("cls", "dp")), P(("cls", "dp"), None))
    return jax.shard_map(
        per_device, mesh=mesh, in_specs=in_specs, out_specs=out_specs, check_vma=False
    )
```

```python
import functools

import jax
import jax.numpy as jnp
from jax import lax
from jax.experimental import pallas as pl
from jax.experimental.pallas import tpu as pltpu
from jax.sharding import PartitionSpec as P

logit_scale = 64.0
margin = 0.35
epsilon = 1e-06
digit = 256
extra = 8
square = 4

vmem_spec = pl.BlockSpec(memory_space=pltpu.VMEM)
smem_spec = pl.BlockSpec(memory_space=pltpu.SMEM)
hbm_spec = pl.BlockSpec(memory_space=pltpu.HBM)


vmem_bytes = 64 * 1024 * 1024


def params(room):
    return pltpu.CompilerParams(vmem_limit_bytes=vmem_bytes - room * 1024)


def normalized(feat_ref):
    wide = feat_ref[...].astype(jnp.float32)
    squares = jnp.sum(wide * wide, axis=1, keepdims=True)
    return (wide * lax.rsqrt(squares + epsilon)).astype(jnp.bfloat16)


def normalize_kernel(*refs):
    rows = refs[0].shape[0]
    for index, feat_ref in enumerate(refs[:-1]):
        refs[-1][index * rows : (index + 1) * rows, :] = normalized(feat_ref)


def pack_kernel(feat_ref, label_ref, out_ref):
    rows, width = feat_ref.shape
    sets = label_ref.shape[0]
    out_ref[:rows, :] = normalized(feat_ref)
    labels = label_ref[...]
    digits = [labels // digit, labels % digit]
    line = lax.broadcasted_iota(jnp.int32, (extra, width), 0)
    packed = jnp.zeros((extra, width), jnp.float32)
    per_row = width // (2 * rows)
    for first in range(0, sets, per_row):
        pieces = [
            part[index : index + 1, :]
            for index in range(first, min(first + per_row, sets))
            for part in digits
        ]
        if len(pieces) * rows < width:
            pieces.append(jnp.zeros((1, width - len(pieces) * rows), jnp.int32))
        row = jnp.concatenate(pieces, axis=1).astype(jnp.float32)
        packed = jnp.where(line == first // per_row, row, packed)
    out_ref[rows:, :] = packed.astype(jnp.bfloat16)


def labels_of(packed_ref, index):
    rows = packed_ref.shape[0] - extra
    per_row = packed_ref.shape[1] // (2 * rows)
    line, start = index // per_row, index % per_row * 2 * rows
    digits = packed_ref[rows:, :].astype(jnp.float32)[line : line + 1, :].astype(jnp.int32)
    return digits[:, start : start + rows] * digit + digits[:, start + rows : start + 2 * rows]


def choose_kernel(sampled_ref, weight_hbm, low_ref, chosen_ref, sem):
    part = chosen_ref.shape[0]

    def start_row(row, carry):
        pltpu.make_async_copy(
            weight_hbm.at[pl.ds(sampled_ref[row], 1), :],
            chosen_ref.at[pl.ds(row, 1), :],
            sem,
        ).start()
        return carry

    lax.fori_loop(0, part, start_row, 0, unroll=32)
    pltpu.make_async_copy(weight_hbm.at[pl.ds(0, part), :], chosen_ref, sem).wait()
    rows = chosen_ref[...]
    inverse = lax.rsqrt(jnp.sum(rows * rows, axis=1, keepdims=True) + epsilon)
    low_ref[:part, :] = (rows * inverse).astype(jnp.bfloat16) * logit_scale
    low_ref[part:, :] = jnp.zeros_like(low_ref[part:, :])


def logits_kernel(count, span, held, joined, place_ref, *refs):
    feats = refs[:held]
    if joined:
        rows, earlier_ref = refs[held : held + 2]
        exp_ref, stat_ref, every_ref, label_ref = refs[-4:]
        stat_ref[...] = earlier_ref[...]
    else:
        classes = refs[held : held + square]
        exp_ref, stat_ref, every_ref, label_ref, rows = refs[-5:]
        part = rows.shape[0] // square
        for side in range(square):
            rows[side * part : (side + 1) * part, :] = classes[side][:part, :]
    part = rows.shape[0] // square
    lanes = label_ref.shape[1]
    for index, (_, place, first, source, label_set) in enumerate(span):
        every_ref[index * lanes : (index + 1) * lanes, :] = feats[place][first : first + lanes, :]
        label_ref[index : index + 1, :] = labels_of(feats[source], label_set)
    line = lax.broadcasted_iota(jnp.int32, (part, lanes), 0)
    for pair in range(0, len(span), 2):
        scaled = lax.dot_general(
            rows[...],
            every_ref[pair * lanes : (pair + 2) * lanes, :],
            (((1,), (1,)), ((), ())),
            preferred_element_type=jnp.float32,
        )
        for index in (pair, pair + 1):
            start = (index - pair) * lanes
            labels = label_ref[index : index + 1, :]
            total = jnp.zeros((8, lanes), jnp.float32)
            target = jnp.zeros((8, lanes), jnp.float32)
            for side in range(square):
                lines = slice(side * part, (side + 1) * part)
                hit = labels - place_ref[side] == line
                tile = scaled[lines, start : start + lanes]
                exps = jnp.exp(
                    tile - jnp.where(hit, logit_scale + logit_scale * margin, logit_scale)
                )
                exp_ref[lines, index * lanes : (index + 1) * lanes] = exps
                total = total + jnp.sum(exps.reshape(-1, 8, lanes), axis=0)
                target = target + jnp.sum(jnp.where(hit, tile, 0.0).reshape(-1, 8, lanes), axis=0)
            group = place_ref[square + 1] ^ span[index][0]
            stat_ref[pl.ds(group, 1), :] = jnp.sum(total, axis=0, keepdims=True)
            stat_ref[pl.ds(count + group, 1), :] = jnp.sum(target, axis=0, keepdims=True)


def grads_kernel(count, replicas, spans, sides, place_ref, stat_ref, *refs):
    chunks = [refs[3 * index : 3 * index + 3] for index in range(len(spans))]
    refs = refs[3 * len(spans) :]
    outs, scratch = refs[: len(sides)], refs[-len(spans) :]
    part = chunks[0][0].shape[0] // square
    lanes = stat_ref.shape[1]
    scale = logit_scale / replicas
    group = place_ref[square + 1]
    if 0 in sides:
        refs[len(sides)][...] = (
            logit_scale
            + jnp.log(stat_ref[pl.ds(group, 1), :])
            - (stat_ref[pl.ds(count + group, 1), :] - logit_scale * margin)
        )
    line = lax.broadcasted_iota(jnp.int32, (part, lanes), 0)
    total = None
    for span, (exp_ref, every_ref, label_ref), grads in zip(spans, chunks, scratch):
        for index in range(len(span)):
            inverse = 1.0 / stat_ref[pl.ds(group ^ span[index][0], 1), :]
            columns = slice(index * lanes, (index + 1) * lanes)
            labels = label_ref[index : index + 1, :]
            for place, side in enumerate(sides):
                hit = labels - place_ref[side] == line
                exps = exp_ref[side * part : (side + 1) * part, columns]
                grads[place * part : (place + 1) * part, columns] = (
                    exps * inverse - jnp.where(hit, 1.0, 0.0)
                ).astype(jnp.bfloat16)
        product = jnp.dot(grads[...], every_ref[...], preferred_element_type=jnp.float32)
        total = product if total is None else total + product
    for index, out in enumerate(outs):
        out[...] = (total[index * part : (index + 1) * part, :] * scale).astype(out.dtype)


def finish_kernel(chosen_ref, own_ref, *refs):
    others, out_ref = refs[:-1], refs[-1]
    summed = own_ref[...]
    for other in others:
        summed = summed + other[...].astype(jnp.float32)
    rows = chosen_ref[...]
    inverse = lax.rsqrt(jnp.sum(rows * rows, axis=1, keepdims=True) + epsilon)
    unit = rows * inverse
    radial = jnp.sum(unit * summed, axis=1, keepdims=True)
    out_ref[...] = inverse * (summed - unit * radial)


def per_device(features, labels, weights, sampled):
    groups = lax.axis_size("cls")
    replicas = lax.axis_size("dp")
    local_rows, width = features.shape
    classes = sampled.shape[0]
    part = classes // replicas
    position = lax.axis_index("cls").astype(jnp.int32)
    replica = lax.axis_index("dp").astype(jnp.int32)
    place = jnp.stack(
        [(position ^ side) * classes + replica * part for side in range(square)]
        + [replica, position // square * replicas + replica]
    )

    def swap(value, chip_mask, core_mask):
        mask = chip_mask * replicas + core_mask
        return lax.ppermute(
            value, ("cls", "dp"), [(i, i ^ mask) for i in range(groups * replicas)]
        )

    bits = [(0, 1 << bit) for bit in range(replicas.bit_length() - 1)]
    far_bits = [(1 << bit, 0) for bit in range(2, groups.bit_length() - 1)]

    upper, marks = {0: features}, labels.reshape(1, local_rows)
    for bit, _ in far_bits[1:]:
        upper.update({mask | bit: swap(block, bit, 0) for mask, block in list(upper.items())})
        marks = jnp.concatenate([marks, swap(marks, bit, 0)], axis=0)
    near_raw = swap(features, square, 0)
    low_rows, chosen = pl.pallas_call(
        choose_kernel,
        out_shape=[
            jax.ShapeDtypeStruct((part + extra, width), jnp.bfloat16),
            jax.ShapeDtypeStruct((part, width), jnp.float32),
        ],
        in_specs=[smem_spec, hbm_spec],
        out_specs=[vmem_spec] * 2,
        scratch_shapes=[pltpu.SemaphoreType.DMA],
        compiler_params=params(11 * 1024),
        name="choose",
    )(lax.dynamic_slice_in_dim(sampled, replica * part, part), weights)
    def spread(block):
        near = [block]
        for _, bit in bits:
            near = near + [swap(value, 0, bit) for value in near]
        return near

    tie = lax.optimization_barrier
    corner_rows, marks = tie((low_rows, marks))
    rows = [low_rows, swap(low_rows, 1, 0), swap(low_rows, 2, 0), swap(corner_rows, 3, 0)]
    tied, near_raw = tie(({mask: block for mask, block in upper.items() if mask}, near_raw))
    upper.update(tied)
    packed = {
        mask: pl.pallas_call(
            pack_kernel,
            out_shape=jax.ShapeDtypeStruct((local_rows + extra, width), jnp.bfloat16),
            in_specs=[vmem_spec] * 2,
            out_specs=vmem_spec,
            compiler_params=params(56 * 1024),
            name="pack",
        )(block, marks)
        for mask, block in upper.items()
        if mask
    }
    pair = pl.pallas_call(
        normalize_kernel,
        out_shape=jax.ShapeDtypeStruct((2 * local_rows, width), jnp.bfloat16),
        in_specs=[vmem_spec] * 2,
        out_specs=vmem_spec,
        compiler_params=params(56 * 1024),
        name="normalize",
    )(features, near_raw)
    passed = {mask | square: swap(block, square, 0) for mask, block in packed.items()}
    rows = tie(rows[::-1])[::-1]
    passed, rows = tie((passed, rows))
    ups = list(packed)
    pair, place = tie((pair, place))
    held = [pair, *packed.values(), *passed.values()]
    spread_out = [spread(array) for array in held]
    count = groups // square * replicas
    order = list(upper)

    def entry(index, first_replica):
        mask, replica_bit = index // replicas * square, index % replicas
        up, beside = mask & ~square, bool(mask & square)
        base = (replica_bit - first_replica) * len(held) + 1 + beside * len(ups)
        source = base + ups.index(groups // 2)
        if up:
            return (index, base + ups.index(up), 0, source, order.index(up))
        return (index, base - 1 - beside * len(ups), beside * local_rows, source, 0)

    spans, arrays = [], []
    for some in (range(1), range(1, replicas)):
        spans.append(
            tuple(entry(index, some[0]) for index in range(count) if index % replicas in some)
        )
        arrays.append([copies[bit] for bit in some for copies in spread_out])
    chunks, carried = [], rows
    for joined, span in enumerate(spans):
        shapes = [
            jax.ShapeDtypeStruct((square * part, len(span) * local_rows), jnp.float32),
            jax.ShapeDtypeStruct((2 * count, local_rows), jnp.float32),
            jax.ShapeDtypeStruct((len(span) * local_rows, width), jnp.bfloat16),
            jax.ShapeDtypeStruct((len(span), local_rows), jnp.int32),
            jax.ShapeDtypeStruct((square * part, width), jnp.bfloat16),
        ][: 5 - joined]
        exps, stats, every, marks, *together = pl.pallas_call(
            functools.partial(logits_kernel, count, span, len(arrays[joined]), joined),
            out_shape=shapes,
            in_specs=[smem_spec] + [vmem_spec] * (len(arrays[joined]) + len(carried)),
            out_specs=[vmem_spec] * len(shapes),
            compiler_params=params(16 * 1024),
            name="logits",
        )(place, *arrays[joined], *carried)
        chunks, carried = chunks + [exps, every, marks], together + [stats]
    near = [(0, 0)]
    for chip_bit, core_bit in bits[:1] + far_bits[:1]:
        near = near + [(chip_mask | chip_bit, core_mask | core_bit) for chip_mask, core_mask in near]
    stats = sum((swap(stats, *masks) for masks in near[1:]), stats)
    for chip_mask, core_mask in bits[1:] + far_bits[1:]:
        stats = stats + swap(stats, chip_mask, core_mask)

    def grads(sides):
        kinds = [jnp.bfloat16 if side else jnp.float32 for side in sides]
        shapes = [jax.ShapeDtypeStruct((part, width), kind) for kind in kinds]
        if 0 in sides:
            shapes.append(jax.ShapeDtypeStruct((1, local_rows), jnp.float32))
        return pl.pallas_call(
            functools.partial(grads_kernel, count, replicas, spans, sides),
            out_shape=shapes,
            in_specs=[smem_spec] + [vmem_spec] * (1 + len(chunks)),
            out_specs=[vmem_spec] * len(shapes),
            scratch_shapes=[
                pltpu.VMEM((len(sides) * part, len(span) * local_rows), jnp.bfloat16)
                for span in spans
            ],
            compiler_params=params(16 * 1024),
            name="grads",
        )(place, stats, *chunks)

    away = [swap(block, side, 0) for side, block in enumerate(grads((1, 2, 3)), 1)]
    mine, loss = grads((0,))
    weight_grad = pl.pallas_call(
        finish_kernel,
        out_shape=jax.ShapeDtypeStruct((part, width), jnp.float32),
        in_specs=[vmem_spec] * (2 + len(away)),
        out_specs=vmem_spec,
        compiler_params=params(56 * 1024),
        name="finish",
    )(chosen, mine, *away)
    return (loss.reshape(local_rows), weight_grad)


def solution(mesh):
    in_specs = (P(("cls", "dp"), None), P(("cls", "dp")), P("cls", None), P("cls"))
    out_specs = (P(("cls", "dp")), P(("cls", "dp"), None))
    return jax.shard_map(
        per_device, mesh=mesh, in_specs=in_specs, out_specs=out_specs, check_vma=False
    )
```

```python
import functools

import jax
import jax.numpy as jnp
from jax import lax
from jax.experimental import pallas as pl
from jax.experimental.pallas import tpu as pltpu
from jax.sharding import PartitionSpec as P

logit_scale = 64.0
margin = 0.35
epsilon = 1e-06
digit = 256
extra = 8
square = 4

vmem_spec = pl.BlockSpec(memory_space=pltpu.VMEM)
smem_spec = pl.BlockSpec(memory_space=pltpu.SMEM)
hbm_spec = pl.BlockSpec(memory_space=pltpu.HBM)


vmem_bytes = 64 * 1024 * 1024


def params(room):
    return pltpu.CompilerParams(vmem_limit_bytes=vmem_bytes - room * 1024)


def normalized(feat_ref):
    wide = feat_ref[...].astype(jnp.float32)
    squares = jnp.sum(wide * wide, axis=1, keepdims=True)
    return (wide * lax.rsqrt(squares + epsilon)).astype(jnp.bfloat16)


def normalize_kernel(*refs):
    rows = refs[0].shape[0]
    for index, feat_ref in enumerate(refs[:-1]):
        refs[-1][index * rows : (index + 1) * rows, :] = normalized(feat_ref)


def pack_kernel(feat_ref, label_ref, out_ref):
    rows, width = feat_ref.shape
    sets = label_ref.shape[0]
    out_ref[:rows, :] = normalized(feat_ref)
    labels = label_ref[...]
    digits = [labels // digit, labels % digit]
    line = lax.broadcasted_iota(jnp.int32, (extra, width), 0)
    packed = jnp.zeros((extra, width), jnp.float32)
    per_row = width // (2 * rows)
    for first in range(0, sets, per_row):
        pieces = [
            part[index : index + 1, :]
            for index in range(first, min(first + per_row, sets))
            for part in digits
        ]
        if len(pieces) * rows < width:
            pieces.append(jnp.zeros((1, width - len(pieces) * rows), jnp.int32))
        row = jnp.concatenate(pieces, axis=1).astype(jnp.float32)
        packed = jnp.where(line == first // per_row, row, packed)
    out_ref[rows:, :] = packed.astype(jnp.bfloat16)


def labels_of(packed_ref, index):
    rows = packed_ref.shape[0] - extra
    per_row = packed_ref.shape[1] // (2 * rows)
    line, start = index // per_row, index % per_row * 2 * rows
    digits = packed_ref[rows:, :].astype(jnp.float32)[line : line + 1, :].astype(jnp.int32)
    return digits[:, start : start + rows] * digit + digits[:, start + rows : start + 2 * rows]


def choose_kernel(sampled_ref, weight_hbm, low_ref, chosen_ref, sem):
    part = chosen_ref.shape[0]

    def start_row(row, carry):
        pltpu.make_async_copy(
            weight_hbm.at[pl.ds(sampled_ref[row], 1), :],
            chosen_ref.at[pl.ds(row, 1), :],
            sem,
        ).start()
        return carry

    lax.fori_loop(0, part, start_row, 0, unroll=32)
    pltpu.make_async_copy(weight_hbm.at[pl.ds(0, part), :], chosen_ref, sem).wait()
    rows = chosen_ref[...]
    inverse = lax.rsqrt(jnp.sum(rows * rows, axis=1, keepdims=True) + epsilon)
    low_ref[:part, :] = (rows * inverse).astype(jnp.bfloat16) * logit_scale
    low_ref[part:, :] = jnp.zeros_like(low_ref[part:, :])


def logits_kernel(count, span, held, joined, place_ref, *refs):
    feats = refs[:held]
    if joined:
        rows, earlier_ref = refs[held : held + 2]
        exp_ref, stat_ref, every_ref, label_ref = refs[-4:]
        stat_ref[...] = earlier_ref[...]
    else:
        classes = refs[held : held + square]
        exp_ref, stat_ref, every_ref, label_ref, rows = refs[-5:]
        part = rows.shape[0] // square
        for side in range(square):
            rows[side * part : (side + 1) * part, :] = classes[side][:part, :]
    part = rows.shape[0] // square
    lanes = label_ref.shape[1]
    for index, (_, place, first, source, label_set) in enumerate(span):
        every_ref[index * lanes : (index + 1) * lanes, :] = feats[place][first : first + lanes, :]
        label_ref[index : index + 1, :] = labels_of(feats[source], label_set)
    line = lax.broadcasted_iota(jnp.int32, (part, lanes), 0)
    for pair in range(0, len(span), 2):
        scaled = lax.dot_general(
            rows[...],
            every_ref[pair * lanes : (pair + 2) * lanes, :],
            (((1,), (1,)), ((), ())),
            preferred_element_type=jnp.float32,
        )
        for index in (pair, pair + 1):
            start = (index - pair) * lanes
            labels = label_ref[index : index + 1, :]
            total = jnp.zeros((8, lanes), jnp.float32)
            target = jnp.zeros((8, lanes), jnp.float32)
            for side in range(square):
                lines = slice(side * part, (side + 1) * part)
                hit = labels - place_ref[side] == line
                tile = scaled[lines, start : start + lanes]
                exps = jnp.exp(
                    tile - jnp.where(hit, logit_scale + logit_scale * margin, logit_scale)
                )
                exp_ref[lines, index * lanes : (index + 1) * lanes] = exps
                total = total + jnp.sum(exps.reshape(-1, 8, lanes), axis=0)
                target = target + jnp.sum(jnp.where(hit, tile, 0.0).reshape(-1, 8, lanes), axis=0)
            group = place_ref[square + 1] ^ span[index][0]
            stat_ref[pl.ds(group, 1), :] = jnp.sum(total, axis=0, keepdims=True)
            stat_ref[pl.ds(count + group, 1), :] = jnp.sum(target, axis=0, keepdims=True)


def grads_kernel(count, replicas, spans, sides, place_ref, stat_ref, *refs):
    chunks = [refs[3 * index : 3 * index + 3] for index in range(len(spans))]
    refs = refs[3 * len(spans) :]
    outs, scratch = refs[: len(sides)], refs[-len(spans) :]
    part = chunks[0][0].shape[0] // square
    lanes = stat_ref.shape[1]
    scale = logit_scale / replicas
    group = place_ref[square + 1]
    if 0 in sides:
        refs[len(sides)][...] = (
            logit_scale
            + jnp.log(stat_ref[pl.ds(group, 1), :])
            - (stat_ref[pl.ds(count + group, 1), :] - logit_scale * margin)
        )
    line = lax.broadcasted_iota(jnp.int32, (part, lanes), 0)
    total = None
    for span, (exp_ref, every_ref, label_ref), grads in zip(spans, chunks, scratch):
        for index in range(len(span)):
            inverse = 1.0 / stat_ref[pl.ds(group ^ span[index][0], 1), :]
            columns = slice(index * lanes, (index + 1) * lanes)
            labels = label_ref[index : index + 1, :]
            for place, side in enumerate(sides):
                hit = labels - place_ref[side] == line
                exps = exp_ref[side * part : (side + 1) * part, columns]
                grads[place * part : (place + 1) * part, columns] = (
                    exps * inverse - jnp.where(hit, 1.0, 0.0)
                ).astype(jnp.bfloat16)
        product = jnp.dot(grads[...], every_ref[...], preferred_element_type=jnp.float32)
        total = product if total is None else total + product
    for index, out in enumerate(outs):
        out[...] = (total[index * part : (index + 1) * part, :] * scale).astype(out.dtype)


def finish_kernel(chosen_ref, own_ref, *refs):
    others, out_ref = refs[:-1], refs[-1]
    summed = own_ref[...]
    for other in others:
        summed = summed + other[...].astype(jnp.float32)
    rows = chosen_ref[...]
    inverse = lax.rsqrt(jnp.sum(rows * rows, axis=1, keepdims=True) + epsilon)
    unit = rows * inverse
    radial = jnp.sum(unit * summed, axis=1, keepdims=True)
    out_ref[...] = inverse * (summed - unit * radial)


def per_device(features, labels, weights, sampled):
    groups = lax.axis_size("cls")
    replicas = lax.axis_size("dp")
    local_rows, width = features.shape
    classes = sampled.shape[0]
    part = classes // replicas
    position = lax.axis_index("cls").astype(jnp.int32)
    replica = lax.axis_index("dp").astype(jnp.int32)
    place = jnp.stack(
        [(position ^ side) * classes + replica * part for side in range(square)]
        + [replica, position // square * replicas + replica]
    )

    def swap(value, chip_mask, core_mask):
        mask = chip_mask * replicas + core_mask
        return lax.ppermute(
            value, ("cls", "dp"), [(i, i ^ mask) for i in range(groups * replicas)]
        )

    bits = [(0, 1 << bit) for bit in range(replicas.bit_length() - 1)]
    far_bits = [(1 << bit, 0) for bit in range(2, groups.bit_length() - 1)]

    upper, marks = {0: features}, labels.reshape(1, local_rows)
    for bit, _ in far_bits[1:]:
        upper.update({mask | bit: swap(block, bit, 0) for mask, block in list(upper.items())})
        marks = jnp.concatenate([marks, swap(marks, bit, 0)], axis=0)
    near_raw = swap(features, square, 0)
    low_rows, chosen = pl.pallas_call(
        choose_kernel,
        out_shape=[
            jax.ShapeDtypeStruct((part + extra, width), jnp.bfloat16),
            jax.ShapeDtypeStruct((part, width), jnp.float32),
        ],
        in_specs=[smem_spec, hbm_spec],
        out_specs=[vmem_spec] * 2,
        scratch_shapes=[pltpu.SemaphoreType.DMA],
        compiler_params=params(11 * 1024),
        name="choose",
    )(lax.dynamic_slice_in_dim(sampled, replica * part, part), weights)
    def spread(block):
        near = [block]
        for _, bit in bits:
            near = near + [swap(value, 0, bit) for value in near]
        return near

    tie = lax.optimization_barrier
    corner_rows, marks = tie((low_rows, marks))
    rows = [low_rows, swap(low_rows, 1, 0), swap(low_rows, 2, 0), swap(corner_rows, 3, 0)]
    tied, near_raw = tie(({mask: block for mask, block in upper.items() if mask}, near_raw))
    upper.update(tied)
    packed = {
        mask: pl.pallas_call(
            pack_kernel,
            out_shape=jax.ShapeDtypeStruct((local_rows + extra, width), jnp.bfloat16),
            in_specs=[vmem_spec] * 2,
            out_specs=vmem_spec,
            compiler_params=params(56 * 1024),
            name="pack",
        )(block, marks)
        for mask, block in upper.items()
        if mask
    }
    pair = pl.pallas_call(
        normalize_kernel,
        out_shape=jax.ShapeDtypeStruct((2 * local_rows, width), jnp.bfloat16),
        in_specs=[vmem_spec] * 2,
        out_specs=vmem_spec,
        compiler_params=params(56 * 1024),
        name="normalize",
    )(features, near_raw)
    passed = {mask | square: swap(block, square, 0) for mask, block in packed.items()}
    rows = tie(rows[::-1])[::-1]
    passed, rows = tie((passed, rows))
    ups = list(packed)
    pair, place = tie((pair, place))
    held = [pair, *packed.values(), *passed.values()]
    spread_out = [spread(array) for array in held]
    count = groups // square * replicas
    order = list(upper)

    def entry(index, first_replica):
        mask, replica_bit = index // replicas * square, index % replicas
        up, beside = mask & ~square, bool(mask & square)
        base = (replica_bit - first_replica) * len(held) + 1 + beside * len(ups)
        source = base + ups.index(groups // 2)
        if up:
            return (index, base + ups.index(up), 0, source, order.index(up))
        return (index, base - 1 - beside * len(ups), beside * local_rows, source, 0)

    spans, arrays = [], []
    for some in (range(1), range(1, replicas)):
        spans.append(
            tuple(entry(index, some[0]) for index in range(count) if index % replicas in some)
        )
        arrays.append([copies[bit] for bit in some for copies in spread_out])
    chunks, carried = [], rows
    for joined, span in enumerate(spans):
        shapes = [
            jax.ShapeDtypeStruct((square * part, len(span) * local_rows), jnp.float32),
            jax.ShapeDtypeStruct((2 * count, local_rows), jnp.float32),
            jax.ShapeDtypeStruct((len(span) * local_rows, width), jnp.bfloat16),
            jax.ShapeDtypeStruct((len(span), local_rows), jnp.int32),
            jax.ShapeDtypeStruct((square * part, width), jnp.bfloat16),
        ][: 5 - joined]
        exps, stats, every, marks, *together = pl.pallas_call(
            functools.partial(logits_kernel, count, span, len(arrays[joined]), joined),
            out_shape=shapes,
            in_specs=[smem_spec] + [vmem_spec] * (len(arrays[joined]) + len(carried)),
            out_specs=[vmem_spec] * len(shapes),
            compiler_params=params(16 * 1024),
            name="logits",
        )(place, *arrays[joined], *carried)
        chunks, carried = chunks + [exps, every, marks], together + [stats]
    for chip_mask, core_mask in bits:
        stats = stats + swap(stats, chip_mask, core_mask)
    stats = sum((swap(stats, mask, 0) for mask in range(square, groups, square)), stats)

    def grads(sides):
        kinds = [jnp.bfloat16 if side else jnp.float32 for side in sides]
        shapes = [jax.ShapeDtypeStruct((part, width), kind) for kind in kinds]
        if 0 in sides:
            shapes.append(jax.ShapeDtypeStruct((1, local_rows), jnp.float32))
        return pl.pallas_call(
            functools.partial(grads_kernel, count, replicas, spans, sides),
            out_shape=shapes,
            in_specs=[smem_spec] + [vmem_spec] * (1 + len(chunks)),
            out_specs=[vmem_spec] * len(shapes),
            scratch_shapes=[
                pltpu.VMEM((len(sides) * part, len(span) * local_rows), jnp.bfloat16)
                for span in spans
            ],
            compiler_params=params(16 * 1024),
            name="grads",
        )(place, stats, *chunks)

    away = [swap(block, side, 0) for side, block in enumerate(grads((1, 2, 3)), 1)]
    mine, loss = grads((0,))
    weight_grad = pl.pallas_call(
        finish_kernel,
        out_shape=jax.ShapeDtypeStruct((part, width), jnp.float32),
        in_specs=[vmem_spec] * (2 + len(away)),
        out_specs=vmem_spec,
        compiler_params=params(56 * 1024),
        name="finish",
    )(chosen, mine, *away)
    return (loss.reshape(local_rows), weight_grad)


def solution(mesh):
    in_specs = (P(("cls", "dp"), None), P(("cls", "dp")), P("cls", None), P("cls"))
    out_specs = (P(("cls", "dp")), P(("cls", "dp"), None))
    return jax.shard_map(
        per_device, mesh=mesh, in_specs=in_specs, out_specs=out_specs, check_vma=False
    )
```
